32 devices in a mesh: rep: 4 (over z), tok: 4 (over y, core), head: 2 (over x).
Axes of the slice: x: 2, y: 2, z: 4, core: 2. Of those that a mesh axis runs over, the one named last changes fastest.
Arguments:
- image_tokens: bfloat16 [8, 1024, 1536], P('rep', 'tok'), may hold values from -6 to 6
- text_tokens: bfloat16 [8, 152, 1536], P('rep'), may hold values from -6 to 6
- text_owner: int32 [8, 152], P('rep'), may hold values from 0 to 3, as said below
- conditioning: float32 [8, 1536], replicated, may hold values from -6 to 6
- slot_sequence: int32 [8], replicated, may hold values from 0 to 7, each once
- image_w_mod: bfloat16 [1536, 6, 1536], P('tok'), may hold values from -0.15625 to 0.15625
- image_b_mod: bfloat16 [6, 1536], replicated, may hold values from -3 to 3
- image_w_qkv: bfloat16 [1536, 3, 1536], P('tok', None, 'head'), may hold values from -0.15625 to 0.15625
- image_w_proj: bfloat16 [1536, 1536], P('tok', 'head'), may hold values from -2.5 to 2.5
- image_w_up: bfloat16 [1536, 6144], P('tok', 'head'), may hold values from -0.15625 to 0.15625
- image_w_down: bfloat16 [1536, 6144], P('tok', 'head'), may hold values from -0.078125 to 0.078125
- text_w_mod: bfloat16 [1536, 6, 1536], P('tok'), may hold values from -0.15625 to 0.15625
- text_b_mod: bfloat16 [6, 1536], replicated, may hold values from -3 to 3
- text_w_qkv: bfloat16 [1536, 3, 1536], P('tok', None, 'head'), may hold values from -0.15625 to 0.15625
- text_w_proj: bfloat16 [1536, 1536], P('tok', 'head'), may hold values from -2.5 to 2.5
- text_w_up: bfloat16 [1536, 6144], P('tok', 'head'), may hold values from -0.15625 to 0.15625
- text_w_down: bfloat16 [1536, 6144], P('tok', 'head'), may hold values from -0.078125 to 0.078125
- image_cotangent: bfloat16 [8, 1024, 1536], P('rep', 'tok'), may hold values from -6 to 6
- text_cotangent: bfloat16 [8, 152, 1536], P('rep', 'tok'), may hold values from -6 to 6
Outputs:
- image_out: bfloat16 [8, 1024, 1536], P('rep', 'tok')
- text_out: bfloat16 [8, 152, 1536], P('rep', 'tok')
- image_grad: bfloat16 [8, 1024, 1536], P('rep', 'tok')
- text_grad: bfloat16 [8, 152, 1536], P('rep', 'tok')
- cond_grad: float32 [8, 1536], P(None, 'tok')
- image_g_mod: float32 [1536, 6, 1536], P('tok')
- image_g_bmod: float32 [6, 1536], replicated
- image_g_qkv: float32 [1536, 3, 1536], P('tok', None, 'head')
- image_g_proj: float32 [1536, 1536], P('tok', 'head')
- image_g_up: float32 [1536, 6144], P('tok', 'head')
- image_g_down: float32 [1536, 6144], P('tok', 'head')
- text_g_mod: float32 [1536, 6, 1536], P('tok')
- text_g_bmod: float32 [6, 1536], replicated
- text_g_qkv: float32 [1536, 3, 1536], P('tok', None, 'head')
- text_g_proj: float32 [1536, 1536], P('tok', 'head')
- text_g_up: float32 [1536, 6144], P('tok', 'head')
- text_g_down: float32 [1536, 6144], P('tok', 'head')
- stream_rms: float32 [10], replicated
The draws below stay inside these ranges and needn't reach their ends.
Inputs may be any that keep to these rules, and one draw needn't show every extreme that they name: `text_owner`: in every row each value occurs exactly 38 times. `slot_sequence`: each sequence number occurs once.
All inputs are finite; a program needn't handle non-finite values.
Results may differ from the reference program's by a relative error of at most 0.02.
Values may be sent and summed in bfloat16 or wider, within the bound.
No kernel may reach another device: no remote copies, remote signals or barrier semaphores. Data moves between devices by JAX's collectives and lax.ppermute only.
A program may use at most 320 MiB of HBM per device.

```python
import jax
import jax.numpy as jnp
from jax import lax

D = 1536
HEADS = 24
HD = 64
FF = 6144
IMG = 1024
TXT = 152
SEQS = 8
TXT_DEV = 38


def draw_text_owner(key, part):
    row_keys = jax.random.split(key, SEQS)
    shuffled = jax.vmap(lambda row_key: jax.random.permutation(row_key, TXT))(row_keys)
    return (shuffled // TXT_DEV).astype(jnp.int32)


def shard_levels(rng, extent, cuts, least, high):
    def one(position, shards_of):
        heights = jax.random.uniform(jax.random.fold_in(jax.random.fold_in(rng, 6), position), (shards_of,), jnp.float32, least / len(cuts), high / len(cuts))
        return jnp.repeat(jnp.exp(heights), extent[position] // shards_of).reshape((-1,) + (1,) * (len(extent) - position - 1))

    level = one(*cuts[0])
    for cut in cuts[1:]:
        level = level * one(*cut)
    return level


def normal_values(own_key, dims, deviation, reach, pieces=(), kind=jnp.bfloat16):
    values = deviation * jax.random.normal(own_key, dims, jnp.float32)
    if pieces:
        values = values * shard_levels(own_key, dims, pieces, -0.22, 0.18)
    return jnp.clip(values, -reach, reach).astype(kind)


def setup_inputs(seed: int = 0) -> dict:
    key_of = jax.random.split(jax.random.key(seed), 20)
    image_tokens = normal_values(key_of[0], (SEQS, IMG, D), 1.0, 6.0, ((0, 4), (1, 4)))
    text_tokens = normal_values(key_of[1], (SEQS, TXT, D), 1.0, 6.0, ((0, 4),))
    text_owner = draw_text_owner(jax.random.fold_in(key_of[19], 71), 0)
    conditioning = normal_values(key_of[3], (SEQS, D), 1.0, 6.0, (), jnp.float32)
    slot_sequence = jax.random.permutation(key_of[4], SEQS).astype(jnp.int32)
    image_w_mod = normal_values(key_of[5], (D, 6, D), D ** -0.5, 0.15625, ((0, 4),))
    image_b_mod = normal_values(key_of[6], (6, D), 0.5, 3.0)
    image_w_qkv = normal_values(key_of[7], (D, 3, D), D ** -0.5, 0.15625, ((0, 4), (2, 2)))
    image_w_proj = normal_values(key_of[8], (D, D), (max(D // 256, 1)) ** -0.5, 2.5, ((0, 4), (1, 2)))
    image_w_up = normal_values(key_of[9], (D, FF), D ** -0.5, 0.15625, ((0, 4), (1, 2)))
    image_w_down = normal_values(key_of[10], (D, FF), FF ** -0.5, 0.078125, ((0, 4), (1, 2)))
    text_w_mod = normal_values(key_of[11], (D, 6, D), D ** -0.5, 0.15625, ((0, 4),))
    text_b_mod = normal_values(key_of[12], (6, D), 0.5, 3.0)
    text_w_qkv = normal_values(key_of[13], (D, 3, D), D ** -0.5, 0.15625, ((0, 4), (2, 2)))
    text_w_proj = normal_values(key_of[14], (D, D), (max(D // 256, 1)) ** -0.5, 2.5, ((0, 4), (1, 2)))
    text_w_up = normal_values(key_of[15], (D, FF), D ** -0.5, 0.15625, ((0, 4), (1, 2)))
    text_w_down = normal_values(key_of[16], (D, FF), FF ** -0.5, 0.078125, ((0, 4), (1, 2)))
    image_cotangent = normal_values(key_of[17], (SEQS, IMG, D), 1.0, 6.0, ((0, 4), (1, 4)))
    text_cotangent = normal_values(key_of[18], (SEQS, TXT, D), 1.0, 6.0, ((0, 4), (1, 4)))
    return {"image_tokens": image_tokens, "text_tokens": text_tokens, "text_owner": text_owner, "conditioning": conditioning, "slot_sequence": slot_sequence, "image_w_mod": image_w_mod, "image_b_mod": image_b_mod, "image_w_qkv": image_w_qkv, "image_w_proj": image_w_proj, "image_w_up": image_w_up, "image_w_down": image_w_down, "text_w_mod": text_w_mod, "text_b_mod": text_b_mod, "text_w_qkv": text_w_qkv, "text_w_proj": text_w_proj, "text_w_up": text_w_up, "text_w_down": text_w_down, "image_cotangent": image_cotangent, "text_cotangent": text_cotangent}


@jax.custom_vjp
def low(v):
    return lax.optimization_barrier(v.astype(jnp.bfloat16)).astype(jnp.float32)

@jax.custom_vjp
def low_back(v):
    return v

def low_keep(v):
    return (low(v), None)

def low_pass(kept, grad):
    return (grad,)

def back_keep(v):
    return (v, None)

def back_low(kept, grad):
    return (low(grad),)
low.defvjp(low_keep, low_pass)
low_back.defvjp(back_keep, back_low)
exact_mode = lax.Precision.HIGHEST

def layer_norm(values):
    centered = values - lax.optimization_barrier(jnp.mean(values, axis=-1, keepdims=True))
    spread = lax.optimization_barrier(jnp.mean(centered * centered, axis=-1, keepdims=True))
    return centered * lax.rsqrt(spread + 1e-06)

def pre_attention(stream, modul, w_qkv):
    hidden = low(layer_norm(stream) * (1.0 + modul[1]) + modul[0])
    return low_back(low(jnp.einsum('td,dke->tke', hidden, w_qkv, precision=exact_mode)))

def joint_attention(projected):
    length = projected.shape[0]
    query_rows = projected[:, 0].reshape(length, HEADS, HD)
    key_rows = projected[:, 1].reshape(length, HEADS, HD)
    value_rows = projected[:, 2].reshape(length, HEADS, HD)
    scores = low_back(jnp.einsum('qhe,khe->hqk', query_rows, key_rows, precision=exact_mode) * 0.125)
    attn_probs = jax.nn.softmax(scores, axis=-1)
    mixed = jnp.einsum('hqk,khe->qhe', low(attn_probs), value_rows, precision=exact_mode)
    return low_back(low(mixed.reshape(length, D)))

def post_attention(stream, modul, mixed, w_proj, w_up, w_down):
    branch_one = low_back(jnp.einsum('ti,oi->to', mixed, w_proj, precision=exact_mode))
    gated_one = modul[2] * branch_one
    middle = stream + gated_one
    hidden = low(layer_norm(middle) * (1.0 + modul[4]) + modul[3])
    upward = low_back(jnp.einsum('td,df->tf', hidden, w_up, precision=exact_mode))
    activ = low(jax.nn.gelu(upward, approximate=True))
    branch_two = low_back(jnp.einsum('tf,of->to', activ, w_down, precision=exact_mode))
    gated_two = modul[5] * branch_two
    result = middle + gated_two
    squares = jnp.stack([jnp.sum(stream * stream), jnp.sum(gated_one * gated_one), jnp.sum(middle * middle), jnp.sum(gated_two * gated_two), jnp.sum(result * result)])
    return (result, squares)

def reference(image_tokens, text_tokens, text_owner, conditioning, slot_sequence, image_w_mod, image_b_mod, image_w_qkv, image_w_proj, image_w_up, image_w_down, text_w_mod, text_b_mod, text_w_qkv, text_w_proj, text_w_up, text_w_down, image_cotangent, text_cotangent):
    caption_order = jnp.argsort(text_owner, axis=1, stable=True).astype(jnp.int32)
    text_sorted = jnp.take_along_axis(text_tokens.astype(jnp.float32), caption_order[:, :, None], axis=1)
    picker = (slot_sequence[:, None] == jnp.arange(SEQS, dtype=jnp.int32)[None, :]).astype(jnp.float32)
    params = (image_w_mod.astype(jnp.float32), image_b_mod.astype(jnp.float32), image_w_qkv.astype(jnp.float32), image_w_proj.astype(jnp.float32), image_w_up.astype(jnp.float32), image_w_down.astype(jnp.float32), text_w_mod.astype(jnp.float32), text_b_mod.astype(jnp.float32), text_w_qkv.astype(jnp.float32), text_w_proj.astype(jnp.float32), text_w_up.astype(jnp.float32), text_w_down.astype(jnp.float32))

    def forward(image_in, text_in, cond_in, weights):
        cond_slot = jnp.dot(picker, cond_in, precision=exact_mode)
        activ = low(jax.nn.silu(cond_slot))
        image_mod = jnp.einsum('sd,dke->ske', activ, weights[0], precision=exact_mode) + weights[1][None]
        text_mod = jnp.einsum('sd,dke->ske', activ, weights[6], precision=exact_mode) + weights[7][None]

        def one_slot(slot):
            image_x, text_x, mod_image, mod_text = slot
            projected = jnp.concatenate([pre_attention(image_x, mod_image, weights[2]), pre_attention(text_x, mod_text, weights[8])], axis=0)
            mixed = joint_attention(projected)
            image_res, image_sq = post_attention(image_x, mod_image, mixed[:IMG], weights[3], weights[4], weights[5])
            text_res, text_sq = post_attention(text_x, mod_text, mixed[IMG:], weights[9], weights[10], weights[11])
            return (image_res, text_res, jnp.concatenate([image_sq, text_sq]))
        image_res, text_res, squares = lax.map(jax.checkpoint(one_slot), (image_in, text_in, image_mod, text_mod))
        return ((image_res, text_res), squares)
    outputs, vjp_fn, squares = jax.vjp(forward, image_tokens.astype(jnp.float32), text_sorted, conditioning, params, has_aux=True)
    grads = vjp_fn((image_cotangent.astype(jnp.float32), text_cotangent.astype(jnp.float32)))
    param_grads = grads[3]
    totals = lax.optimization_barrier(jnp.sum(squares, axis=0))
    counts = jnp.array([SEQS * IMG * D] * 5 + [SEQS * TXT * D] * 5, dtype=jnp.float32)
    stream_rms = jnp.sqrt(totals / counts)
    return (outputs[0].astype(jnp.bfloat16), outputs[1].astype(jnp.bfloat16), grads[0].astype(jnp.bfloat16), grads[1].astype(jnp.bfloat16), grads[2], param_grads[0], param_grads[1], param_grads[2], param_grads[3], param_grads[4], param_grads[5], param_grads[6], param_grads[7], param_grads[8], param_grads[9], param_grads[10], param_grads[11], stream_rms)
```

```python
import jax
import jax.numpy as jnp
from jax import lax
from jax.sharding import PartitionSpec as P

HD = 64


exact_mode = lax.Precision.HIGHEST


def layer_norm(values):
    centered = values - jnp.mean(values, axis=-1, keepdims=True)
    spread = jnp.mean(centered * centered, axis=-1, keepdims=True)
    return centered * lax.rsqrt(spread + 1e-06)


def modulate(stream, shift_part, scale_part):
    return layer_norm(stream) * (1.0 + scale_part[:, None, :]) + shift_part[:, None, :]


def modulate_back(stream, modul, hidden_grad, shift_index, scale_index):
    unused_value, back_fn = jax.vjp(modulate, stream, modul[:, shift_index], modul[:, scale_index])
    return back_fn(hidden_grad)


def gelu_tanh(values):
    return jax.nn.gelu(values, approximate=True)


def attention_scores(query_rows, key_rows):
    return (
        jnp.einsum("qhe,khe->hqk", query_rows, key_rows, preferred_element_type=jnp.float32) * 0.125
    )


def recompute_probs(scores, row_max, row_total):
    return (
        jnp.exp(scores - jnp.transpose(row_max)[:, :, None]) / jnp.transpose(row_total)[:, :, None]
    )


def attend_one(packed):
    query_rows, key_all, value_all = packed
    scores = attention_scores(query_rows, key_all)
    row_max = jnp.max(scores, axis=-1, keepdims=True)
    expd = jnp.exp(scores - row_max)
    row_total = jnp.sum(expd, axis=-1, keepdims=True)
    attn_probs = (expd / row_total).astype(jnp.bfloat16)
    mixed = jnp.einsum("hqk,khe->qhe", attn_probs, value_all, preferred_element_type=jnp.float32)
    return (
        mixed.astype(jnp.bfloat16),
        jnp.transpose(row_max[..., 0]),
        jnp.transpose(row_total[..., 0]),
    )


def query_side(packed):
    query_rows, key_all, value_all, grad_mixed, row_max, row_total = packed
    attn_probs = recompute_probs(attention_scores(query_rows, key_all), row_max, row_total)
    grad_probs = jnp.einsum(
        "qhe,khe->hqk", grad_mixed, value_all, preferred_element_type=jnp.float32
    )
    row_delta = jnp.sum(attn_probs * grad_probs, axis=-1, keepdims=True)
    grad_scores = (attn_probs * (grad_probs - row_delta)).astype(jnp.bfloat16)
    grad_query = (
        jnp.einsum("hqk,khe->qhe", grad_scores, key_all, preferred_element_type=jnp.float32) * 0.125
    )
    grad_key = (
        jnp.einsum("hqk,qhe->khe", grad_scores, query_rows, preferred_element_type=jnp.float32)
        * 0.125
    )
    grad_value = jnp.einsum(
        "hqk,qhe->khe",
        attn_probs.astype(jnp.bfloat16),
        grad_mixed,
        preferred_element_type=jnp.float32,
    )
    return (grad_query.astype(jnp.bfloat16), grad_key, grad_value)


def mlp_forward(middle, modul, up_full, down_full):
    hidden = modulate(middle, modul[:, 3], modul[:, 4]).astype(jnp.bfloat16)
    upward = jnp.einsum("std,df->stf", hidden, up_full, preferred_element_type=jnp.float32)
    activ = gelu_tanh(upward).astype(jnp.bfloat16)
    partial_sum = jnp.einsum("stf,of->sto", activ, down_full, preferred_element_type=jnp.float32)
    return (hidden, upward, activ, partial_sum)


def mlp_backward(out_grad, modul, branch_two, hidden, upward, activ, up_full, down_full):
    gate_grad = jnp.sum(out_grad * branch_two, axis=1)
    branch_grad = (modul[:, 5][:, None, :] * out_grad).astype(jnp.bfloat16)
    down_grad = jnp.einsum("sto,stf->of", branch_grad, activ, preferred_element_type=jnp.float32)
    activ_grad = jnp.einsum(
        "sto,of->stf", branch_grad, down_full, preferred_element_type=jnp.float32
    )
    unused_value, gelu_back = jax.vjp(gelu_tanh, upward)
    upward_grad = gelu_back(activ_grad)[0].astype(jnp.bfloat16)
    up_grad = jnp.einsum("std,stf->df", hidden, upward_grad, preferred_element_type=jnp.float32)
    hidden_grad = jnp.einsum(
        "stf,df->std", upward_grad, up_full, preferred_element_type=jnp.float32
    )
    return (gate_grad, down_grad, up_grad, hidden_grad)


def proj_backward(mid_grad, modul, branch_one, mixed_rows, proj_full):
    gate_grad = jnp.sum(mid_grad * branch_one, axis=1)
    branch_grad = (modul[:, 2][:, None, :] * mid_grad).astype(jnp.bfloat16)
    proj_grad = jnp.einsum(
        "sqo,sqi->oi", branch_grad, mixed_rows, preferred_element_type=jnp.float32
    )
    mixed_grad = jnp.einsum(
        "sqo,oi->sqi", branch_grad, proj_full, preferred_element_type=jnp.float32
    )
    return (gate_grad, proj_grad, mixed_grad)


def stream_squares(stream, gated_one, middle, gated_two, result):
    return jnp.stack(
        [jnp.sum(member * member) for member in (stream, gated_one, middle, gated_two, result)]
    )


def flip(values, axis, bit):
    return lax.ppermute(
        values, axis, [(place, place ^ bit) for place in range(lax.axis_size(axis))]
    )


def head_sum(partial):
    if lax.axis_size("head") != 2:
        return lax.psum(partial, "head").astype(jnp.float32)
    return partial.astype(jnp.float32) + flip(partial, "head", 1).astype(jnp.float32)


def gather_pair(first, second):
    count = lax.axis_size("tok")
    rank = lax.axis_index("tok")
    parity = lax.rem(lax.axis_index("rep"), 2)
    rows = first.shape[0]
    entries = [(0, 0, first), (0, 1, second)]
    fetched = [(0, jnp.where(parity == 0, first, second))]
    bit = count // 2
    while bit > 1:
        fetched = fetched + [(away ^ bit, flip(part, "tok", bit)) for away, part in fetched]
        bit //= 2
    for away, part in fetched[1:]:
        entries.append((away, parity, part))
        entries.append((away, 1 - parity, flip(part, "rep", 1)))
    entries = entries + [(away ^ 1, which, flip(part, "tok", 1)) for away, which, part in entries]
    whole = jnp.zeros((2, rows * count) + first.shape[1:], first.dtype)
    rest = (0,) * (first.ndim - 1)
    for away, which, part in entries:
        whole = lax.dynamic_update_slice(
            whole, part[None], (which, jnp.bitwise_xor(rank, away) * rows) + rest
        )
    return whole[0], whole[1]


def gather_rows(values, axis):
    pieces = [values]
    bit = lax.axis_size("tok") // 2
    order = [0]
    while bit > 0:
        pieces = pieces + [flip(piece, "tok", bit) for piece in pieces]
        order = order + [place ^ bit for place in order]
        bit //= 2
    by_distance = [pieces[order.index(away)] for away in range(len(order))]
    return jnp.concatenate(by_distance, axis=axis)


def halve(pieces):
    bit = 1
    while bit < lax.axis_size("tok"):
        pieces = {
            away: part.astype(jnp.float32)
            + flip(pieces[away | bit].astype(jnp.bfloat16), "tok", bit).astype(jnp.float32)
            for away, part in pieces.items()
            if not away & bit
        }
        bit *= 2
    return pieces[0]


def scatter_tok(grad):
    count = lax.axis_size("tok")
    rank = lax.axis_index("tok")
    rows = grad.shape[0] // count
    return halve(
        {
            away: lax.dynamic_slice_in_dim(grad, jnp.bitwise_xor(rank, away) * rows, rows, axis=0)
            for away in range(count)
        }
    )


def line_sum(chunks):
    if lax.axis_size("rep") != 4:
        return [lax.psum(part.astype(jnp.bfloat16), "rep").astype(jnp.float32) for part in chunks]
    rank = lax.axis_index("rep")
    inner = (rank == 1) | (rank == 2)
    chunks = [part.astype(jnp.bfloat16) for part in chunks]
    outer_pairs = [(0, 1), (1, 0), (2, 3), (3, 2)]
    total, moved = {}, {}
    count = len(chunks)
    for step in range(count + 2):
        if step < count and step >= 2:
            load = jnp.where(inner, total[step - 2], chunks[step])
            pairs = outer_pairs
        elif step < count:
            load, pairs = chunks[step], [(0, 1), (3, 2)]
        else:
            load, pairs = total[step - 2], [(1, 0), (2, 3)]
        moved[step] = lax.ppermute(load, "rep", pairs)
        if step < count:
            pair = chunks[step].astype(jnp.float32) + moved[step].astype(jnp.float32)
            pair = pair.astype(jnp.bfloat16)
            over = lax.ppermute(pair, "rep", [(1, 2), (2, 1)])
            total[step] = (pair.astype(jnp.float32) + over.astype(jnp.float32)).astype(jnp.bfloat16)
    return [
        jnp.where(inner, total[step], moved[step + 2]).astype(jnp.float32) for step in range(count)
    ]


def tok_total(values):
    bit = 1
    while bit < lax.axis_size("tok"):
        values = values + flip(values, "tok", bit)
        bit *= 2
    return values


def rep_gather(values):
    count = lax.axis_size("rep")
    rank = lax.axis_index("rep")
    pieces = values[None]
    bit = 1
    while bit < count:
        pieces = jnp.concatenate([pieces, flip(pieces, "rep", bit)], axis=0)
        bit *= 2
    return jnp.stack(
        [
            lax.dynamic_index_in_dim(pieces, jnp.bitwise_xor(rank, place), 0, keepdims=False)
            for place in range(count)
        ]
    )


def on_device(
    image_tokens,
    text_tokens,
    text_owner,
    conditioning,
    slot_sequence,
    image_w_mod,
    image_b_mod,
    image_w_qkv,
    image_w_proj,
    image_w_up,
    image_w_down,
    text_w_mod,
    text_b_mod,
    text_w_qkv,
    text_w_proj,
    text_w_up,
    text_w_down,
    image_cotangent,
    text_cotangent,
):
    tok_rank = lax.axis_index("tok")
    rep_rank = lax.axis_index("rep")
    tok_count = lax.axis_size("tok")
    seq_group, image_rows, width = image_tokens.shape
    text_rows = text_cotangent.shape[1]
    slot_total = conditioning.shape[0]
    row_share = image_w_mod.shape[0]
    head_width = image_w_qkv.shape[2]
    head_count = head_width // HD
    local_rows = image_rows + text_rows
    caption_order = jnp.argsort(text_owner, axis=1, stable=True)
    owned_rows = lax.dynamic_slice_in_dim(caption_order, tok_rank * text_rows, text_rows, axis=1)
    text_input = jnp.take_along_axis(text_tokens, owned_rows[:, :, None], axis=1).astype(
        jnp.float32
    )
    image_input = image_tokens.astype(jnp.float32)
    picker = (slot_sequence[:, None] == jnp.arange(slot_total, dtype=jnp.int32)[None, :]).astype(
        jnp.float32
    )
    cond_slots = jnp.dot(picker, conditioning, precision=exact_mode)
    activ_all = jax.nn.silu(cond_slots).astype(jnp.bfloat16)
    activ_group = lax.dynamic_slice_in_dim(activ_all, rep_rank * seq_group, seq_group, axis=0)
    activ_share = lax.dynamic_slice_in_dim(activ_group, tok_rank * row_share, row_share, axis=1)
    both_mod = tok_total(
        jnp.stack(
            [
                jnp.einsum("sd,dke->ske", activ_share, weight, preferred_element_type=jnp.float32)
                for weight in (image_w_mod, text_w_mod)
            ]
        )
    )
    image_mod, text_mod = both_mod[0], both_mod[1]
    image_mod = image_mod + image_b_mod.astype(jnp.float32)[None]
    text_mod = text_mod + text_b_mod.astype(jnp.float32)[None]
    image_qkv, text_qkv = gather_pair(image_w_qkv, text_w_qkv)
    image_proj, text_proj = gather_pair(image_w_proj, text_w_proj)
    text_up, text_down = gather_pair(text_w_up, text_w_down)
    image_up, image_down = gather_pair(image_w_up, image_w_down)
    image_hid_one = modulate(image_input, image_mod[:, 0], image_mod[:, 1]).astype(jnp.bfloat16)
    text_hid_one = modulate(text_input, text_mod[:, 0], text_mod[:, 1]).astype(jnp.bfloat16)
    projected = jnp.concatenate(
        [
            jnp.einsum(
                "std,dke->stke", image_hid_one, image_qkv, preferred_element_type=jnp.float32
            ),
            jnp.einsum("std,dke->stke", text_hid_one, text_qkv, preferred_element_type=jnp.float32),
        ],
        axis=1,
    ).astype(jnp.bfloat16)
    key_all = gather_rows(projected[:, :, 1], 1)
    value_all = gather_rows(projected[:, :, 2], 1)
    key_total = key_all.shape[1]
    query_heads = projected[:, :, 0].reshape(seq_group, local_rows, head_count, HD)
    key_heads = key_all.reshape(seq_group, key_total, head_count, HD)
    value_heads = value_all.reshape(seq_group, key_total, head_count, HD)
    mixed_heads, row_max, row_total = lax.map(attend_one, (query_heads, key_heads, value_heads))
    mixed = mixed_heads.reshape(seq_group, local_rows, head_width)
    image_branch = head_sum(
        jnp.einsum(
            "sqi,oi->sqo", mixed[:, :image_rows], image_proj, preferred_element_type=jnp.float32
        ).astype(jnp.bfloat16)
    )
    text_branch = head_sum(
        jnp.einsum(
            "sqi,oi->sqo", mixed[:, image_rows:], text_proj, preferred_element_type=jnp.float32
        ).astype(jnp.bfloat16)
    )
    image_middle = image_input + image_mod[:, 2][:, None, :] * image_branch
    text_middle = text_input + text_mod[:, 2][:, None, :] * text_branch
    image_hid_two, image_upward, image_activ, image_part = mlp_forward(
        image_middle, image_mod, image_up, image_down
    )
    text_hid_two, text_upward, text_activ, text_part = mlp_forward(
        text_middle, text_mod, text_up, text_down
    )
    image_branch_two, text_branch_two = (
        head_sum(image_part.astype(jnp.bfloat16)),
        head_sum(text_part.astype(jnp.bfloat16)),
    )
    image_result = image_middle + image_mod[:, 5][:, None, :] * image_branch_two
    text_result = text_middle + text_mod[:, 5][:, None, :] * text_branch_two
    square_partial = jnp.concatenate(
        [
            stream_squares(
                image_input,
                image_mod[:, 2][:, None, :] * image_branch,
                image_middle,
                image_mod[:, 5][:, None, :] * image_branch_two,
                image_result,
            ),
            stream_squares(
                text_input,
                text_mod[:, 2][:, None, :] * text_branch,
                text_middle,
                text_mod[:, 5][:, None, :] * text_branch_two,
                text_result,
            ),
        ]
    )
    image_cot = image_cotangent.astype(jnp.float32)
    text_cot = text_cotangent.astype(jnp.float32)
    image_gate_two, image_g_down, image_g_up, image_hid_part = mlp_backward(
        image_cot,
        image_mod,
        image_branch_two,
        image_hid_two,
        image_upward,
        image_activ,
        image_up,
        image_down,
    )
    text_gate_two, text_g_down, text_g_up, text_hid_part = mlp_backward(
        text_cot,
        text_mod,
        text_branch_two,
        text_hid_two,
        text_upward,
        text_activ,
        text_up,
        text_down,
    )
    image_hid_grad, text_hid_grad = (
        head_sum(image_hid_part.astype(jnp.bfloat16)),
        head_sum(text_hid_part.astype(jnp.bfloat16)),
    )
    image_ln_grad, image_shift_two, image_scale_two = modulate_back(
        image_middle, image_mod, image_hid_grad, 3, 4
    )
    text_ln_grad, text_shift_two, text_scale_two = modulate_back(
        text_middle, text_mod, text_hid_grad, 3, 4
    )
    image_mid_grad = image_cot + image_ln_grad
    text_mid_grad = text_cot + text_ln_grad
    image_gate_one, image_g_proj, image_mixed_grad = proj_backward(
        image_mid_grad, image_mod, image_branch, mixed[:, :image_rows], image_proj
    )
    text_gate_one, text_g_proj, text_mixed_grad = proj_backward(
        text_mid_grad, text_mod, text_branch, mixed[:, image_rows:], text_proj
    )
    mixed_grad = jnp.concatenate([image_mixed_grad, text_mixed_grad], axis=1).astype(jnp.bfloat16)
    grad_heads = mixed_grad.reshape(seq_group, local_rows, head_count, HD)
    query_grad, key_grad_all, value_grad_all = lax.map(
        query_side, (query_heads, key_heads, value_heads, grad_heads, row_max, row_total)
    )
    key_grad, value_grad = [
        halve(
            {
                away: whole.reshape(seq_group, key_total, head_width)[
                    :, away * local_rows : (away + 1) * local_rows
                ]
                for away in range(tok_count)
            }
        )
        for whole in (key_grad_all, value_grad_all)
    ]
    qkv_grad = jnp.stack(
        [
            query_grad.reshape(seq_group, local_rows, head_width),
            key_grad.astype(jnp.bfloat16),
            value_grad.astype(jnp.bfloat16),
        ],
        axis=2,
    )
    image_g_qkv = jnp.einsum(
        "std,stke->dke", image_hid_one, qkv_grad[:, :image_rows], preferred_element_type=jnp.float32
    )
    text_g_qkv = jnp.einsum(
        "std,stke->dke", text_hid_one, qkv_grad[:, image_rows:], preferred_element_type=jnp.float32
    )
    image_in_part = jnp.einsum(
        "stke,dke->std", qkv_grad[:, :image_rows], image_qkv, preferred_element_type=jnp.float32
    )
    text_in_part = jnp.einsum(
        "stke,dke->std", qkv_grad[:, image_rows:], text_qkv, preferred_element_type=jnp.float32
    )
    image_in_grad, text_in_grad = (
        head_sum(image_in_part.astype(jnp.bfloat16)),
        head_sum(text_in_part.astype(jnp.bfloat16)),
    )
    image_ln_one, image_shift_one, image_scale_one = modulate_back(
        image_input, image_mod, image_in_grad, 0, 1
    )
    text_ln_one, text_shift_one, text_scale_one = modulate_back(
        text_input, text_mod, text_in_grad, 0, 1
    )
    image_grad = (image_mid_grad + image_ln_one).astype(jnp.bfloat16)
    text_grad = (text_mid_grad + text_ln_one).astype(jnp.bfloat16)
    early = jnp.stack(
        [
            jnp.stack([image_gate_one, image_shift_two, image_scale_two, image_gate_two], axis=1),
            jnp.stack([text_gate_one, text_shift_two, text_scale_two, text_gate_two], axis=1),
        ]
    )
    late = jnp.stack(
        [
            jnp.stack([image_shift_one, image_scale_one], axis=1),
            jnp.stack([text_shift_one, text_scale_one], axis=1),
        ]
    )
    square_row = jnp.pad(square_partial, (0, width - 10))[None]
    early_flat = jnp.concatenate([early.reshape(-1, width), square_row], axis=0)
    early_all = rep_gather(tok_total(early_flat))
    late_all = rep_gather(tok_total(late))
    rep_count = lax.axis_size("rep")
    square_total = jnp.sum(early_all[:, -1, :10], axis=0)
    early_table = jnp.moveaxis(
        early_all[:, :-1].reshape(rep_count, 2, seq_group, 4, width), 0, 1
    ).reshape(2, slot_total, 4, width)
    late_table = jnp.moveaxis(late_all, 0, 1).reshape(2, slot_total, 2, width)
    mod_sum = jnp.concatenate([late_table, early_table], axis=2)
    mlp_shares = [
        scatter_tok(grad) for grad in (text_g_down, text_g_up, image_g_down, image_g_up)
    ]
    half = mlp_shares[0].shape[1] // 2
    mlp_sums = line_sum(
        [part for share in mlp_shares for part in (share[:, :half], share[:, half:])]
    )
    text_down_sum, text_up_sum, image_down_sum, image_up_sum = [
        jnp.concatenate(mlp_sums[place : place + 2], axis=1) for place in (0, 2, 4, 6)
    ]
    text_proj_sum, image_proj_sum = line_sum(
        [scatter_tok(text_g_proj), scatter_tok(image_g_proj)]
    )
    qkv_shares = [scatter_tok(text_g_qkv), scatter_tok(image_g_qkv)]
    qkv_sums = line_sum([share[:, place] for share in qkv_shares for place in range(3)])
    text_qkv_sum = jnp.stack(qkv_sums[:3], axis=1)
    image_qkv_sum = jnp.stack(qkv_sums[3:], axis=1)
    activ_rows = lax.dynamic_slice_in_dim(
        activ_all, tok_rank * row_share, row_share, axis=1
    ).astype(jnp.float32)
    image_g_mod = jnp.einsum("sd,ske->dke", activ_rows, mod_sum[0], precision=exact_mode)
    text_g_mod = jnp.einsum("sd,ske->dke", activ_rows, mod_sum[1], precision=exact_mode)
    image_g_bmod = jnp.sum(mod_sum[0], axis=0)
    text_g_bmod = jnp.sum(mod_sum[1], axis=0)
    activ_grad = jnp.einsum(
        "ske,dke->sd", mod_sum[0], image_w_mod.astype(jnp.float32), precision=exact_mode
    ) + jnp.einsum("ske,dke->sd", mod_sum[1], text_w_mod.astype(jnp.float32), precision=exact_mode)
    cond_rows = lax.dynamic_slice_in_dim(cond_slots, tok_rank * row_share, row_share, axis=1)
    unused_value, silu_back = jax.vjp(jax.nn.silu, cond_rows)
    slot_grad = silu_back(activ_grad)[0]
    cond_grad = jnp.dot(jnp.transpose(picker), slot_grad, precision=exact_mode)
    image_count = float(slot_total * image_rows * tok_count * width)
    text_count = float(slot_total * text_rows * tok_count * width)
    count_table = jnp.concatenate(
        [jnp.full((5,), image_count, jnp.float32), jnp.full((5,), text_count, jnp.float32)]
    )
    stream_rms = jnp.sqrt(square_total / count_table)
    return (
        image_result.astype(jnp.bfloat16),
        text_result.astype(jnp.bfloat16),
        image_grad,
        text_grad,
        cond_grad,
        image_g_mod,
        image_g_bmod,
        image_qkv_sum,
        image_proj_sum,
        image_up_sum,
        image_down_sum,
        text_g_mod,
        text_g_bmod,
        text_qkv_sum,
        text_proj_sum,
        text_up_sum,
        text_down_sum,
        stream_rms,
    )


def solution(mesh):
    in_specs = (
        P("rep", "tok", None),
        P("rep", None, None),
        P("rep", None),
        P(),
        P(),
        P("tok", None, None),
        P(),
        P("tok", None, "head"),
        P("tok", "head"),
        P("tok", "head"),
        P("tok", "head"),
        P("tok", None, None),
        P(),
        P("tok", None, "head"),
        P("tok", "head"),
        P("tok", "head"),
        P("tok", "head"),
        P("rep", "tok", None),
        P("rep", "tok", None),
    )
    out_specs = (
        P("rep", "tok", None),
        P("rep", "tok", None),
        P("rep", "tok", None),
        P("rep", "tok", None),
        P(None, "tok"),
        P("tok", None, None),
        P(),
        P("tok", None, "head"),
        P("tok", "head"),
        P("tok", "head"),
        P("tok", "head"),
        P("tok", None, None),
        P(),
        P("tok", None, "head"),
        P("tok", "head"),
        P("tok", "head"),
        P("tok", "head"),
        P(),
    )
    return jax.shard_map(
        on_device, mesh=mesh, in_specs=in_specs, out_specs=out_specs, check_vma=False
    )
```

```python
import functools

import jax
import jax.numpy as jnp
from jax import lax
from jax.experimental import pallas as pl
from jax.experimental.pallas import tpu as pltpu
from jax.sharding import PartitionSpec as P

HD = 64
LANES = 128
VMEM_LIMIT = 60 * 1024 * 1024

exact_mode = lax.Precision.HIGHEST


def layer_norm(values):
    centered = values - jnp.mean(values, axis=-1, keepdims=True)
    spread = jnp.mean(centered * centered, axis=-1, keepdims=True)
    return centered * lax.rsqrt(spread + 1e-06)


def modulate(stream, shift_part, scale_part):
    return layer_norm(stream) * (1.0 + scale_part[:, None, :]) + shift_part[:, None, :]


def modulate_back(stream, modul, hidden_grad, shift_index, scale_index):
    unused_value, back_fn = jax.vjp(modulate, stream, modul[:, shift_index], modul[:, scale_index])
    return back_fn(hidden_grad)


def stream_squares(stream, gated_one, middle, gated_two, result):
    return jnp.stack(
        [jnp.sum(member * member) for member in (stream, gated_one, middle, gated_two, result)]
    )


def flip(values, axis, bit):
    return lax.ppermute(
        values, axis, [(place, place ^ bit) for place in range(lax.axis_size(axis))]
    )


def head_sum(partial):
    if lax.axis_size("head") != 2:
        return lax.psum(partial, "head").astype(jnp.float32)
    return partial.astype(jnp.float32) + flip(partial, "head", 1).astype(jnp.float32)


def gather_pair(first, second):
    count = lax.axis_size("tok")
    parity = lax.rem(lax.axis_index("rep"), 2)
    fetched = {0: jnp.where(parity == 0, first, second)}
    bit = count // 2
    while bit > 1:
        for away, part in list(fetched.items()):
            fetched[away ^ bit] = flip(part, "tok", bit)
        bit //= 2
    entries = {0: (first, second)}
    for away, part in fetched.items():
        if away:
            entries[away] = (part, flip(part, "rep", 1))
    for away, parts in list(entries.items()):
        entries[away ^ 1] = tuple(flip(part, "tok", 1) for part in parts)
    return entries


def gather_blocks(values):
    pieces = {0: values}
    bit = lax.axis_size("tok") // 2
    while bit > 0:
        for away, part in list(pieces.items()):
            pieces[away ^ bit] = flip(part, "tok", bit)
        bit //= 2
    return [pieces[away] for away in range(len(pieces))]


def halve(pieces):
    bit = 1
    while bit < lax.axis_size("tok"):
        pieces = {
            away: (
                part.astype(jnp.float32)
                + flip(pieces[away | bit], "tok", bit).astype(jnp.float32)
            ).astype(jnp.bfloat16)
            for away, part in pieces.items()
            if not away & bit
        }
        bit *= 2
    return pieces[0]


def scatter_grad(keep, send, rows):
    axis = keep.ndim - 2
    moved = flip(send, "tok", 1)
    pieces = {}
    for place in range(keep.shape[axis] // rows):
        cut = functools.partial(
            lax.slice_in_dim, start_index=place * rows, limit_index=(place + 1) * rows, axis=axis
        )
        pieces[2 * place] = (
            cut(keep).astype(jnp.float32) + cut(moved).astype(jnp.float32)
        ).astype(jnp.bfloat16)
    bit = 2
    while bit < lax.axis_size("tok"):
        pieces = {
            away: (
                part.astype(jnp.float32)
                + flip(pieces[away | bit], "tok", bit).astype(jnp.float32)
            ).astype(jnp.bfloat16)
            for away, part in pieces.items()
            if not away & bit
        }
        bit *= 2
    return pieces[0]


def line_sum(chunks):
    if lax.axis_size("rep") != 4:
        return [lax.psum(part, "rep").astype(jnp.float32) for part in chunks]
    rank = lax.axis_index("rep")
    inner = (rank == 1) | (rank == 2)
    outer_pairs = [(0, 1), (1, 0), (2, 3), (3, 2)]
    total, moved = {}, {}
    count = len(chunks)
    for step in range(count + 2):
        if step < count and step >= 2:
            load = jnp.where(inner, total[step - 2], chunks[step])
            pairs = outer_pairs
        elif step < count:
            load, pairs = chunks[step], [(0, 1), (3, 2)]
        else:
            load, pairs = total[step - 2], [(1, 0), (2, 3)]
        moved[step] = lax.ppermute(load, "rep", pairs)
        if step < count:
            pair = chunks[step].astype(jnp.float32) + moved[step].astype(jnp.float32)
            pair = pair.astype(jnp.bfloat16)
            over = lax.ppermute(pair, "rep", [(1, 2), (2, 1)])
            total[step] = (pair.astype(jnp.float32) + over.astype(jnp.float32)).astype(jnp.bfloat16)
    return [
        jnp.where(inner, total[step], moved[step + 2]).astype(jnp.float32) for step in range(count)
    ]


def tok_total(values):
    bit = 1
    while bit < lax.axis_size("tok"):
        values = values + flip(values, "tok", bit)
        bit *= 2
    return values


def rep_gather(values):
    count = lax.axis_size("rep")
    rank = lax.axis_index("rep")
    pieces = values[None]
    bit = 1
    while bit < count:
        pieces = jnp.concatenate([pieces, flip(pieces, "rep", bit)], axis=0)
        bit *= 2
    return jnp.stack(
        [
            lax.dynamic_index_in_dim(pieces, jnp.bitwise_xor(rank, place), 0, keepdims=False)
            for place in range(count)
        ]
    )


def product(left, right):
    return jnp.dot(left, right, preferred_element_type=jnp.float32)


def product_back(left, right):
    return lax.dot_general(
        left, right, (((1,), (1,)), ((), ())), preferred_element_type=jnp.float32
    )


def weight_list(entries, which):
    arrays = []
    for away in range(len(entries)):
        if which is None or away > 1:
            arrays.extend(entries[away])
        else:
            arrays.append(entries[away][which])
    return arrays


def tile_spec(rank, rows, columns):
    if rank == 3:
        return pl.BlockSpec((1, rows, columns), lambda step: (step, 0, 0))
    return pl.BlockSpec((rows, columns), lambda step: (0, step))


def whole_spec(array):
    zeros = (0,) * array.ndim
    return pl.BlockSpec(array.shape, lambda step: zeros, pipeline_mode=pl.Buffered(1))


def tile_of(ref):
    return ref[0] if len(ref.shape) == 3 else ref[...]


def fill(scratch, spot, refs, which, rows, count):
    rank, parity = spot[0], spot[1]
    refs = list(refs)
    for away in range(count):
        at = pl.ds(pl.multiple_of(jnp.bitwise_xor(rank, away) * rows, rows), rows)
        if away < 2:
            scratch[at, :] = tile_of(refs.pop(0))
        else:
            fetched, swapped = refs.pop(0), refs.pop(0)

            @pl.when(parity == which)
            def use_fetched():
                scratch[at, :] = tile_of(fetched)

            @pl.when(parity != which)
            def use_swapped():
                scratch[at, :] = tile_of(swapped)


def fill_both(scratch_one, scratch_two, spot, refs, rows, count):
    rank, parity = spot[0], spot[1]
    refs = list(refs)
    for away in range(count):
        one, two = refs.pop(0), refs.pop(0)
        at = pl.ds(pl.multiple_of(jnp.bitwise_xor(rank, away) * rows, rows), rows)
        if away < 2:
            scratch_one[at, :] = tile_of(one)
            scratch_two[at, :] = tile_of(two)
        else:

            @pl.when(parity == 0)
            def straight():
                scratch_one[at, :] = tile_of(one)
                scratch_two[at, :] = tile_of(two)

            @pl.when(parity != 0)
            def crossed():
                scratch_one[at, :] = tile_of(two)
                scratch_two[at, :] = tile_of(one)


def put_grad(spot, left_ref, right, keep_ref, send_ref, rows, count):
    rank = spot[0]
    for away in range(count):
        at = pl.ds(pl.multiple_of(jnp.bitwise_xor(rank, away) * rows, rows), rows)
        block = product(left_ref[at, :], right).astype(jnp.bfloat16)
        to = send_ref if away & 1 else keep_ref
        place = (away // 2) * rows
        if len(to.shape) == 3:
            to[0, place : place + rows, :] = block
        else:
            to[place : place + rows, :] = block


def call(kernel, tiles, spot, arrays, specs, outs, out_specs, scratch, flops, moved):
    return pl.pallas_call(
        kernel,
        grid=(tiles,),
        in_specs=[pl.BlockSpec(memory_space=pltpu.SMEM)] + specs,
        out_specs=out_specs,
        out_shape=outs,
        scratch_shapes=scratch,
        compiler_params=pltpu.CompilerParams(
            dimension_semantics=("arbitrary",), vmem_limit_bytes=VMEM_LIMIT
        ),
        cost_estimate=pl.CostEstimate(flops=flops, bytes_accessed=moved, transcendentals=0),
    )(spot, *arrays)


def bf16(*shape):
    return jax.ShapeDtypeStruct(shape, jnp.bfloat16)


def project(spot, rows_in, entries, which, tiles):
    arrays = weight_list(entries, which)
    count = len(entries)
    share, columns = arrays[0].shape[-2], arrays[0].shape[-1]
    if arrays[0].ndim == 2:
        columns //= tiles
    length, width = rows_in.shape

    def kernel(spot_ref, in_ref, *rest):
        refs, out_ref, scratch = rest[:-2], rest[-2], rest[-1]
        fill(scratch, spot_ref, refs, which, share, count)
        out_ref[0] = product(in_ref[...], scratch[...]).astype(jnp.bfloat16)

    return call(
        kernel,
        tiles,
        spot,
        [rows_in] + arrays,
        [whole_spec(rows_in)] + [tile_spec(part.ndim, share, columns) for part in arrays],
        bf16(tiles, length, columns),
        pl.BlockSpec((1, length, columns), lambda step: (step, 0, 0)),
        [pltpu.VMEM((width, columns), jnp.bfloat16)],
        2 * length * width * columns * tiles,
        2 * width * columns * tiles,
    )


def project_back(spot, rows_in, entries, which):
    arrays = weight_list(entries, which)
    count = len(entries)
    share, columns = arrays[0].shape
    length, width = rows_in.shape[0], share * count

    def kernel(spot_ref, in_ref, *rest):
        refs, out_ref, scratch = rest[:-2], rest[-2], rest[-1]
        fill(scratch, spot_ref, refs, which, share, count)
        out_ref[...] = product_back(in_ref[...], scratch[...]).astype(jnp.bfloat16)

    return call(
        kernel,
        1,
        spot,
        [rows_in] + arrays,
        [whole_spec(rows_in)] + [tile_spec(2, share, columns) for part in arrays],
        bf16(length, width),
        pl.BlockSpec((length, width), lambda step: (0, 0)),
        [pltpu.VMEM((width, columns), jnp.bfloat16)],
        2 * length * width * columns,
        2 * width * columns,
    )


def proj_grads(spot, grad_rows, grad_turned, mixed_rows, entries, which):
    arrays = weight_list(entries, which)
    count = len(entries)
    share, columns = arrays[0].shape
    length, width = grad_rows.shape

    def kernel(spot_ref, grad_ref, turned_ref, mixed_ref, *rest):
        refs, (out_ref, keep_ref, send_ref, scratch) = rest[:-4], rest[-4:]
        fill(scratch, spot_ref, refs, which, share, count)
        out_ref[...] = product(grad_ref[...], scratch[...]).astype(jnp.bfloat16)
        put_grad(spot_ref, turned_ref, mixed_ref[...], keep_ref, send_ref, share, count)

    half = width // 2
    return call(
        kernel,
        1,
        spot,
        [grad_rows, grad_turned, mixed_rows] + arrays,
        [whole_spec(grad_rows), whole_spec(grad_turned), whole_spec(mixed_rows)]
        + [tile_spec(2, share, columns) for part in arrays],
        (bf16(length, columns), bf16(half, columns), bf16(half, columns)),
        (
            pl.BlockSpec((length, columns), lambda step: (0, 0)),
            pl.BlockSpec((half, columns), lambda step: (0, 0)),
            pl.BlockSpec((half, columns), lambda step: (0, 0)),
        ),
        [pltpu.VMEM((width, columns), jnp.bfloat16)],
        4 * length * width * columns,
        4 * width * columns,
    )


def qkv_grads(spot, hidden_turned, grads, entries, which):
    arrays = weight_list(entries, which)
    count = len(entries)
    tiles, share, columns = arrays[0].shape
    width, length = hidden_turned.shape

    def kernel(spot_ref, turned_ref, grad_ref, *rest):
        refs, (out_ref, keep_ref, send_ref, scratch, total) = rest[:-5], rest[-5:]
        step = pl.program_id(0)
        fill(scratch, spot_ref, refs, which, share, count)
        part = product_back(grad_ref[0], scratch[...])

        @pl.when(step == 0)
        def begin():
            total[...] = part

        @pl.when(step > 0)
        def add():
            total[...] += part

        @pl.when(step == tiles - 1)
        def finish():
            out_ref[...] = total[...].astype(jnp.bfloat16)

        put_grad(spot_ref, turned_ref, grad_ref[0], keep_ref, send_ref, share, count)

    half = width // 2
    return call(
        kernel,
        tiles,
        spot,
        [hidden_turned, grads] + arrays,
        [whole_spec(hidden_turned), tile_spec(3, length, columns)]
        + [tile_spec(3, share, columns) for part in arrays],
        (bf16(length, width), bf16(tiles, half, columns), bf16(tiles, half, columns)),
        (
            pl.BlockSpec((length, width), lambda step: (0, 0)),
            tile_spec(3, half, columns),
            tile_spec(3, half, columns),
        ),
        [pltpu.VMEM((width, columns), jnp.bfloat16), pltpu.VMEM((length, width), jnp.float32)],
        4 * length * width * columns * tiles,
        4 * width * columns * tiles,
    )


def feed_forward(spot, hidden, hidden_turned, grad, grad_turned, entries):
    arrays = weight_list(entries, None)
    count = len(entries)
    share, units = arrays[0].shape
    columns = 512
    tiles = units // columns
    length, width = hidden.shape

    def kernel(spot_ref, hid_ref, hid_turned_ref, grad_ref, grad_turned_ref, *rest):
        refs, rest = rest[: len(arrays)], rest[len(arrays) :]
        out_ref, back_ref, up_keep, up_send, down_keep, down_send = rest[:6]
        up, down, out_sum, back_sum = rest[6:]
        step = pl.program_id(0)
        fill_both(up, down, spot_ref, refs, share, count)
        upward = product(hid_ref[...], up[...])
        squared = upward * upward
        bent = jnp.tanh(0.7978845608028654 * (upward + 0.044715 * (upward * squared)))
        activ = (0.5 * upward * (1.0 + bent)).astype(jnp.bfloat16)
        slope = 0.5 * (1.0 + bent) + 0.5 * upward * (1.0 - bent * bent) * (
            0.7978845608028654 * (1.0 + 3 * 0.044715 * squared)
        )
        activ_grad = product(grad_ref[...], down[...])
        upward_grad = (activ_grad * slope).astype(jnp.bfloat16)
        out_part = product_back(activ, down[...])
        back_part = product_back(upward_grad, up[...])

        @pl.when(step == 0)
        def begin():
            out_sum[...] = out_part
            back_sum[...] = back_part

        @pl.when(step > 0)
        def add():
            out_sum[...] += out_part
            back_sum[...] += back_part

        @pl.when(step == tiles - 1)
        def finish():
            out_ref[...] = out_sum[...].astype(jnp.bfloat16)
            back_ref[...] = back_sum[...].astype(jnp.bfloat16)

        put_grad(spot_ref, grad_turned_ref, activ, down_keep, down_send, share, count)
        put_grad(spot_ref, hid_turned_ref, upward_grad, up_keep, up_send, share, count)

    half = width // 2
    grad_out = bf16(half, units)
    grad_spec = tile_spec(2, half, columns)
    rows_spec = pl.BlockSpec((length, width), lambda step: (0, 0))
    wholes = [hidden, hidden_turned, grad, grad_turned]
    return call(
        kernel,
        tiles,
        spot,
        wholes + arrays,
        [whole_spec(part) for part in wholes]
        + [tile_spec(2, share, columns) for part in arrays],
        (bf16(length, width), bf16(length, width)) + (grad_out,) * 4,
        (rows_spec, rows_spec) + (grad_spec,) * 4,
        [pltpu.VMEM((width, columns), jnp.bfloat16)] * 2
        + [pltpu.VMEM((length, width), jnp.float32)] * 2,
        12 * length * width * units,
        8 * width * units,
    )


def head_lanes(shape, head):
    lane = lax.broadcasted_iota(jnp.int32, shape, len(shape) - 1)
    return (lane >= head * HD) & (lane < (head + 1) * HD)


def padding(shape, axis, block, real, count):
    place = lax.broadcasted_iota(jnp.int32, shape, axis)
    hidden = (place >= real) & (place < block)
    for other in range(1, count):
        hidden = hidden | ((place >= other * block + real) & (place < (other + 1) * block))
    return hidden


def attend(query, blocks, real):
    seqs, rows, width = query.shape
    count = len(blocks)
    keys = rows * count

    def kernel(query_ref, *rest):
        refs, out_ref = rest[:-1], rest[-1]
        queries = query_ref[0]
        key_all = jnp.concatenate([ref[0, 0] for ref in refs], axis=0)
        value_all = jnp.concatenate([ref[1, 0] for ref in refs], axis=0)
        hidden = padding((1, keys), 1, rows, real, count)
        result = jnp.zeros((rows, LANES), jnp.float32)
        for head in range(LANES // HD):
            mine = head_lanes((rows, LANES), head)
            scores = product_back(jnp.where(mine, queries, jnp.zeros_like(queries)), key_all)
            scores = jnp.where(hidden, -1e30, scores * 0.125)
            expd = jnp.exp(scores - jnp.max(scores, axis=1, keepdims=True))
            share = 1.0 / jnp.sum(expd, axis=1, keepdims=True)
            mixed = product((expd * share).astype(jnp.bfloat16), value_all)
            result = jnp.where(mine, mixed, result)
        out_ref[0] = result.astype(jnp.bfloat16)

    row_spec = pl.BlockSpec((1, rows, LANES), lambda seq, part: (seq, 0, part))
    block_spec = pl.BlockSpec((2, 1, rows, LANES), lambda seq, part: (0, seq, 0, part))
    return pl.pallas_call(
        kernel,
        grid=(seqs, width // LANES),
        in_specs=[row_spec] + [block_spec] * count,
        out_specs=row_spec,
        out_shape=bf16(seqs, rows, width),
        compiler_params=pltpu.CompilerParams(
            dimension_semantics=("arbitrary", "arbitrary"), vmem_limit_bytes=VMEM_LIMIT
        ),
        cost_estimate=pl.CostEstimate(
            flops=4 * seqs * rows * keys * width * 4,
            bytes_accessed=4 * seqs * keys * width,
            transcendentals=seqs * rows * keys * width // HD,
        ),
    )(query, *blocks)


def attend_grads(query, grad, blocks, real):
    seqs, rows, width = query.shape
    count = len(blocks)
    keys = rows * count

    def kernel(query_ref, grad_ref, *rest):
        refs, (query_grad_ref, *block_grads) = rest[:count], rest[count:]
        queries, grads = query_ref[0], grad_ref[0]
        key_all = jnp.concatenate([ref[0, 0] for ref in refs], axis=0)
        value_all = jnp.concatenate([ref[1, 0] for ref in refs], axis=0)
        hidden = padding((keys, 1), 0, rows, real, count)
        query_grad = jnp.zeros((rows, LANES), jnp.float32)
        key_grad = jnp.zeros((keys, LANES), jnp.float32)
        value_grad = jnp.zeros((keys, LANES), jnp.float32)
        for head in range(LANES // HD):
            mine = head_lanes((rows, LANES), head)
            own_query = jnp.where(mine, queries, jnp.zeros_like(queries))
            own_grad = jnp.where(mine, grads, jnp.zeros_like(grads))
            scores = product_back(key_all, own_query)
            scores = jnp.where(hidden, -1e30, scores * 0.125)
            expd = jnp.exp(scores - jnp.max(scores, axis=0, keepdims=True))
            probs = expd * (1.0 / jnp.sum(expd, axis=0, keepdims=True))
            prob_grad = product_back(value_all, own_grad)
            delta = jnp.sum(probs * prob_grad, axis=0, keepdims=True)
            score_grad = (probs * (prob_grad - delta)).astype(jnp.bfloat16)
            value_grad += product(probs.astype(jnp.bfloat16), own_grad)
            key_grad += product(score_grad, own_query)
            back = lax.dot_general(
                score_grad, key_all, (((0,), (0,)), ((), ())), preferred_element_type=jnp.float32
            )
            query_grad = jnp.where(mine, back, query_grad)
        query_grad_ref[0] = (query_grad * 0.125).astype(jnp.bfloat16)
        for place, ref in enumerate(block_grads):
            at = slice(place * rows, (place + 1) * rows)
            ref[0, 0] = (key_grad[at] * 0.125).astype(jnp.bfloat16)
            ref[1, 0] = value_grad[at].astype(jnp.bfloat16)

    row_spec = pl.BlockSpec((1, rows, LANES), lambda seq, part: (seq, 0, part))
    block_spec = pl.BlockSpec((2, 1, rows, LANES), lambda seq, part: (0, seq, 0, part))
    query_grad, *block_grads = pl.pallas_call(
        kernel,
        grid=(seqs, width // LANES),
        in_specs=[row_spec] * 2 + [block_spec] * count,
        out_specs=[row_spec] + [block_spec] * count,
        out_shape=[bf16(seqs, rows, width)] + [bf16(2, seqs, rows, width)] * count,
        compiler_params=pltpu.CompilerParams(
            dimension_semantics=("arbitrary", "arbitrary"), vmem_limit_bytes=VMEM_LIMIT
        ),
        cost_estimate=pl.CostEstimate(
            flops=10 * seqs * rows * keys * width * 4,
            bytes_accessed=8 * seqs * keys * width,
            transcendentals=seqs * rows * keys * width // HD,
        ),
    )(query, grad, *blocks)
    return query_grad, block_grads


def on_device(
    image_tokens,
    text_tokens,
    text_owner,
    conditioning,
    slot_sequence,
    image_w_mod,
    image_b_mod,
    image_w_qkv,
    image_w_proj,
    image_w_up,
    image_w_down,
    text_w_mod,
    text_b_mod,
    text_w_qkv,
    text_w_proj,
    text_w_up,
    text_w_down,
    image_cotangent,
    text_cotangent,
):
    tok_rank = lax.axis_index("tok")
    rep_rank = lax.axis_index("rep")
    rep_count = lax.axis_size("rep")
    tok_count = lax.axis_size("tok")
    seqs, image_rows, width = image_tokens.shape
    text_real = text_cotangent.shape[1]
    text_rows = -(-text_real // 16) * 16
    slots = conditioning.shape[0]
    share = image_w_mod.shape[0]
    heads_width = image_w_qkv.shape[2]
    rows = image_rows + text_rows
    real = image_rows + text_real
    spot = jnp.stack([tok_rank, lax.rem(rep_rank, 2)]).astype(jnp.int32)

    turn = lambda weight: jnp.transpose(weight, (1, 0, 2))
    qkv_weights = gather_pair(turn(image_w_qkv), turn(text_w_qkv))

    picker = (slot_sequence[:, None] == jnp.arange(slots, dtype=jnp.int32)[None, :]).astype(
        jnp.float32
    )
    cond_slots = jnp.dot(picker, conditioning, precision=exact_mode)
    activ_all = jax.nn.silu(cond_slots).astype(jnp.bfloat16)
    activ_group = lax.dynamic_slice_in_dim(activ_all, rep_rank * seqs, seqs, axis=0)
    activ_share = lax.dynamic_slice_in_dim(activ_group, tok_rank * share, share, axis=1)
    both_mod = tok_total(
        jnp.stack(
            [
                jnp.einsum("sd,dke->ske", activ_share, weight, preferred_element_type=jnp.float32)
                for weight in (image_w_mod, text_w_mod)
            ]
        )
    )
    image_mod = both_mod[0] + image_b_mod.astype(jnp.float32)[None]
    text_mod = both_mod[1] + text_b_mod.astype(jnp.float32)[None]

    owned = (text_owner == tok_rank).astype(jnp.float32)
    total_text = text_owner.shape[1]
    before = jnp.dot(
        owned,
        jnp.triu(jnp.ones((total_text, total_text), jnp.float32), 1),
        precision=exact_mode,
    )
    chosen = (
        (before[:, None, :] == jnp.arange(text_rows, dtype=jnp.float32)[None, :, None])
        & (owned[:, None, :] > 0.5)
    ).astype(jnp.bfloat16)
    text_input = jnp.einsum("srt,std->srd", chosen, text_tokens, preferred_element_type=jnp.float32)
    image_input = image_tokens.astype(jnp.float32)
    image_cot = image_cotangent.astype(jnp.float32)
    text_cot = jnp.pad(
        text_cotangent.astype(jnp.float32), ((0, 0), (0, text_rows - text_real), (0, 0))
    )

    flat = lambda values: values.reshape(-1, values.shape[-1])
    image_hid_one = flat(modulate(image_input, image_mod[:, 0], image_mod[:, 1]).astype(jnp.bfloat16))
    text_hid_one = flat(modulate(text_input, text_mod[:, 0], text_mod[:, 1]).astype(jnp.bfloat16))
    image_qkv = project(spot, image_hid_one, qkv_weights, 0, 3)
    text_qkv = project(spot, text_hid_one, qkv_weights, 1, 3)
    by_seq = lambda values: values.reshape(values.shape[:-2] + (seqs, -1, values.shape[-1]))
    both = lambda image, text: jnp.concatenate([by_seq(image), by_seq(text)], axis=-2)
    query = both(image_qkv[0], text_qkv[0])
    blocks = gather_blocks(both(image_qkv[1:], text_qkv[1:]))
    proj_weights = gather_pair(image_w_proj, text_w_proj)
    text_ff = gather_pair(text_w_up, text_w_down)
    image_ff = gather_pair(image_w_up, image_w_down)
    mixed = attend(query, blocks, real)
    image_mixed = flat(mixed[:, :image_rows])
    text_mixed = flat(mixed[:, image_rows:])
    image_branch = by_seq(head_sum(project_back(spot, image_mixed, proj_weights, 0)))
    text_branch = by_seq(head_sum(project_back(spot, text_mixed, proj_weights, 1)))

    def middle_of(stream, modul, branch, cot):
        middle = stream + modul[:, 2][:, None, :] * branch
        hidden = flat(modulate(middle, modul[:, 3], modul[:, 4]).astype(jnp.bfloat16))
        grad = flat((modul[:, 5][:, None, :] * cot).astype(jnp.bfloat16))
        return middle, hidden, grad

    image_middle, image_hid_two, image_db_two = middle_of(
        image_input, image_mod, image_branch, image_cot
    )
    text_middle, text_hid_two, text_db_two = middle_of(text_input, text_mod, text_branch, text_cot)
    image_part, image_back, image_up_keep, image_up_send, image_down_keep, image_down_send = (
        feed_forward(
            spot, image_hid_two, image_hid_two.T, image_db_two, image_db_two.T, image_ff
        )
    )
    text_part, text_back, text_up_keep, text_up_send, text_down_keep, text_down_send = (
        feed_forward(spot, text_hid_two, text_hid_two.T, text_db_two, text_db_two.T, text_ff)
    )
    image_hid_grad = by_seq(head_sum(image_back))
    text_hid_grad = by_seq(head_sum(text_back))
    ff_shares = [
        scatter_grad(text_down_keep, text_down_send, share),
        scatter_grad(text_up_keep, text_up_send, share),
        scatter_grad(image_down_keep, image_down_send, share),
        scatter_grad(image_up_keep, image_up_send, share),
    ]
    image_branch_two = by_seq(head_sum(image_part))
    text_branch_two = by_seq(head_sum(text_part))

    image_ln_grad, image_shift_two, image_scale_two = modulate_back(
        image_middle, image_mod, image_hid_grad, 3, 4
    )
    text_ln_grad, text_shift_two, text_scale_two = modulate_back(
        text_middle, text_mod, text_hid_grad, 3, 4
    )
    image_mid_grad = image_cot + image_ln_grad
    text_mid_grad = text_cot + text_ln_grad
    image_gate_one = jnp.sum(image_mid_grad * image_branch, axis=1)
    text_gate_one = jnp.sum(text_mid_grad * text_branch, axis=1)
    image_db_one = flat((image_mod[:, 2][:, None, :] * image_mid_grad).astype(jnp.bfloat16))
    text_db_one = flat((text_mod[:, 2][:, None, :] * text_mid_grad).astype(jnp.bfloat16))
    image_mixed_grad, image_proj_keep, image_proj_send = proj_grads(
        spot, image_db_one, image_db_one.T, image_mixed, proj_weights, 0
    )
    text_mixed_grad, text_proj_keep, text_proj_send = proj_grads(
        spot, text_db_one, text_db_one.T, text_mixed, proj_weights, 1
    )
    query_grad, block_grads = attend_grads(
        query, both(image_mixed_grad, text_mixed_grad), blocks, real
    )
    block_grad = halve(dict(enumerate(block_grads)))
    image_qkv_grad = jnp.concatenate(
        [query_grad[None, :, :image_rows], block_grad[:, :, :image_rows]], axis=0
    ).reshape(3, -1, heads_width)
    text_qkv_grad = jnp.concatenate(
        [query_grad[None, :, image_rows:], block_grad[:, :, image_rows:]], axis=0
    ).reshape(3, -1, heads_width)
    image_in_part, image_qkv_keep, image_qkv_send = qkv_grads(
        spot, image_hid_one.T, image_qkv_grad, qkv_weights, 0
    )
    text_in_part, text_qkv_keep, text_qkv_send = qkv_grads(
        spot, text_hid_one.T, text_qkv_grad, qkv_weights, 1
    )
    image_in_grad = by_seq(head_sum(image_in_part))
    text_in_grad = by_seq(head_sum(text_in_part))
    image_ln_one, image_shift_one, image_scale_one = modulate_back(
        image_input, image_mod, image_in_grad, 0, 1
    )
    text_ln_one, text_shift_one, text_scale_one = modulate_back(
        text_input, text_mod, text_in_grad, 0, 1
    )
    image_grad = (image_mid_grad + image_ln_one).astype(jnp.bfloat16)
    text_grad = (text_mid_grad + text_ln_one).astype(jnp.bfloat16)[:, :text_real]

    image_gated_one = image_mod[:, 2][:, None, :] * image_branch
    text_gated_one = text_mod[:, 2][:, None, :] * text_branch
    image_gated_two = image_mod[:, 5][:, None, :] * image_branch_two
    text_gated_two = text_mod[:, 5][:, None, :] * text_branch_two
    image_result = image_middle + image_gated_two
    text_result = text_middle + text_gated_two
    image_gate_two = jnp.sum(image_cot * image_branch_two, axis=1)
    text_gate_two = jnp.sum(text_cot * text_branch_two, axis=1)
    squares = jnp.concatenate(
        [
            stream_squares(
                image_input, image_gated_one, image_middle, image_gated_two, image_result
            ),
            stream_squares(
                *[
                    member[:, :text_real]
                    for member in (
                        text_input,
                        text_gated_one,
                        text_middle,
                        text_gated_two,
                        text_result,
                    )
                ]
            ),
        ]
    )

    early = jnp.stack(
        [
            jnp.stack([image_gate_one, image_shift_two, image_scale_two, image_gate_two], axis=1),
            jnp.stack([text_gate_one, text_shift_two, text_scale_two, text_gate_two], axis=1),
        ]
    )
    late = jnp.stack(
        [
            jnp.stack([image_shift_one, image_scale_one], axis=1),
            jnp.stack([text_shift_one, text_scale_one], axis=1),
        ]
    )
    square_row = jnp.pad(squares, (0, width - 10))[None]
    early_flat = jnp.concatenate([early.reshape(-1, width), square_row], axis=0)
    early_all = rep_gather(tok_total(early_flat))
    late_all = rep_gather(tok_total(late))
    square_total = jnp.sum(early_all[:, -1, :10], axis=0)
    early_table = jnp.moveaxis(
        early_all[:, :-1].reshape(rep_count, 2, seqs, 4, width), 0, 1
    ).reshape(2, slots, 4, width)
    late_table = jnp.moveaxis(late_all, 0, 1).reshape(2, slots, 2, width)
    mod_sum = jnp.concatenate([late_table, early_table], axis=2)

    half = ff_shares[0].shape[1] // 2
    ff_sums = line_sum([part for whole in ff_shares for part in (whole[:, :half], whole[:, half:])])
    text_down_sum, text_up_sum, image_down_sum, image_up_sum = [
        jnp.concatenate(ff_sums[place : place + 2], axis=1) for place in (0, 2, 4, 6)
    ]
    text_proj_sum, image_proj_sum = line_sum(
        [
            scatter_grad(text_proj_keep, text_proj_send, share),
            scatter_grad(image_proj_keep, image_proj_send, share),
        ]
    )
    qkv_sums = line_sum(
        [
            part
            for whole in (
                scatter_grad(text_qkv_keep, text_qkv_send, share),
                scatter_grad(image_qkv_keep, image_qkv_send, share),
            )
            for part in whole
        ]
    )
    text_qkv_sum = jnp.stack(qkv_sums[:3], axis=1)
    image_qkv_sum = jnp.stack(qkv_sums[3:], axis=1)

    activ_rows = lax.dynamic_slice_in_dim(activ_all, tok_rank * share, share, axis=1).astype(
        jnp.float32
    )
    image_g_mod = jnp.einsum("sd,ske->dke", activ_rows, mod_sum[0], precision=exact_mode)
    text_g_mod = jnp.einsum("sd,ske->dke", activ_rows, mod_sum[1], precision=exact_mode)
    image_g_bmod = jnp.sum(mod_sum[0], axis=0)
    text_g_bmod = jnp.sum(mod_sum[1], axis=0)
    activ_grad = jnp.einsum(
        "ske,dke->sd", mod_sum[0], image_w_mod.astype(jnp.float32), precision=exact_mode
    ) + jnp.einsum("ske,dke->sd", mod_sum[1], text_w_mod.astype(jnp.float32), precision=exact_mode)
    cond_rows = lax.dynamic_slice_in_dim(cond_slots, tok_rank * share, share, axis=1)
    unused_value, silu_back = jax.vjp(jax.nn.silu, cond_rows)
    slot_grad = silu_back(activ_grad)[0]
    cond_grad = jnp.dot(jnp.transpose(picker), slot_grad, precision=exact_mode)
    image_count = float(slots * image_rows * tok_count * width)
    text_count = float(slots * text_real * tok_count * width)
    counts = jnp.concatenate(
        [jnp.full((5,), image_count, jnp.float32), jnp.full((5,), text_count, jnp.float32)]
    )
    stream_rms = jnp.sqrt(square_total / counts)
    return (
        image_result.astype(jnp.bfloat16),
        text_result[:, :text_real].astype(jnp.bfloat16),
        image_grad,
        text_grad,
        cond_grad,
        image_g_mod,
        image_g_bmod,
        image_qkv_sum,
        image_proj_sum,
        image_up_sum,
        image_down_sum,
        text_g_mod,
        text_g_bmod,
        text_qkv_sum,
        text_proj_sum,
        text_up_sum,
        text_down_sum,
        stream_rms,
    )


def solution(mesh):
    in_specs = (
        P("rep", "tok", None),
        P("rep", None, None),
        P("rep", None),
        P(),
        P(),
        P("tok", None, None),
        P(),
        P("tok", None, "head"),
        P("tok", "head"),
        P("tok", "head"),
        P("tok", "head"),
        P("tok", None, None),
        P(),
        P("tok", None, "head"),
        P("tok", "head"),
        P("tok", "head"),
        P("tok", "head"),
        P("rep", "tok", None),
        P("rep", "tok", None),
    )
    out_specs = (
        P("rep", "tok", None),
        P("rep", "tok", None),
        P("rep", "tok", None),
        P("rep", "tok", None),
        P(None, "tok"),
        P("tok", None, None),
        P(),
        P("tok", None, "head"),
        P("tok", "head"),
        P("tok", "head"),
        P("tok", "head"),
        P("tok", None, None),
        P(),
        P("tok", None, "head"),
        P("tok", "head"),
        P("tok", "head"),
        P("tok", "head"),
        P(),
    )
    return jax.shard_map(
        on_device, mesh=mesh, in_specs=in_specs, out_specs=out_specs, check_vma=False
    )
```

```python
import functools

import jax
import jax.numpy as jnp
from jax import lax
from jax.experimental import pallas as pl
from jax.experimental.pallas import tpu as pltpu
from jax.sharding import PartitionSpec as P

HD = 64
LANES = 128
VMEM_LIMIT = 60 * 1024 * 1024
SMALL_COST = pl.CostEstimate(flops=1024, bytes_accessed=1024, transcendentals=0)

exact_mode = lax.Precision.HIGHEST


def normed(values):
    centered = values - jnp.mean(values, axis=-1, keepdims=True)
    scale = lax.rsqrt(jnp.mean(centered * centered, axis=-1, keepdims=True) + 1e-06)
    return centered * scale, scale


def flip(values, axis, bit):
    return lax.ppermute(
        values, axis, [(place, place ^ bit) for place in range(lax.axis_size(axis))]
    )


def head_pair(partial):
    if lax.axis_size("head") != 2:
        return lax.psum(partial, "head"), jnp.zeros_like(partial)
    return partial, flip(partial, "head", 1)


def after(values, *needed):
    return lax.optimization_barrier((values, *needed))[0]


class Sequence:
    def __init__(self):
        self.last = None

    def then(self, values):
        return values if self.last is None else after(values, self.last)

    def mark(self, output):
        self.last = output
        return output


class Lane:
    def __init__(self, axis, depth):
        self.axis, self.depth, self.over = axis, depth, []

    def flip(self, values, bit):
        if len(self.over) >= self.depth:
            values = after(values, self.over[-self.depth])
        moved = flip(values, self.axis, bit)
        self.over.append(moved)
        return moved


class Part:
    def __init__(self, away, half, array):
        self.away, self.half, self.array = away, half, array


def gather_weight(weight, axis, lane, needed=()):
    parity = lax.rem(lax.axis_index("rep"), 2)
    size = weight.shape[axis] // 2
    held = {0: lax.dynamic_slice_in_dim(weight, parity * size, size, axis=axis)}
    if needed:
        held[0] = after(held[0], *needed)
    bit = lax.axis_size("tok") // 2
    while bit > 1:
        for away, array in list(held.items()):
            held[away ^ bit] = lane.flip(array, bit)
        bit //= 2
    parts = [Part(0, None, weight)]
    for away, array in held.items():
        if away:
            parts += [Part(away, 0, array), Part(away, 1, flip(array, "rep", 1))]
    return parts + [Part(part.away ^ 1, part.half, flip(part.array, "tok", 1)) for part in parts]


def gather_blocks(values, lane):
    pieces = {0: values}
    bit = lax.axis_size("tok") // 2
    while bit > 0:
        for away, part in list(pieces.items()):
            pieces[away ^ bit] = lane.flip(part, bit) if bit > 1 else flip(part, "tok", bit)
        bit //= 2
    return [pieces[away] for away in range(len(pieces))]


def add_blocks(seq, first, second, outputs, kind=jnp.bfloat16):
    width = first.shape[-1]
    flat = lambda values: values.reshape(outputs, -1, width)
    first, second = flat(seq.then(first)), flat(second)
    rows = first.shape[1]
    tile = rows // 2

    def kernel(first_ref, second_ref, *out_refs):
        for place, out_ref in enumerate(out_refs):
            out_ref[...] = (
                first_ref[place].astype(jnp.float32) + second_ref[place].astype(jnp.float32)
            ).astype(kind)

    in_spec = pl.BlockSpec((outputs, tile, width), lambda step: (0, step, 0))
    sums = pl.pallas_call(
        kernel,
        grid=(2,),
        in_specs=[in_spec, in_spec],
        out_specs=[pl.BlockSpec((tile, width), lambda step: (step, 0))] * outputs,
        out_shape=[jax.ShapeDtypeStruct((rows, width), kind)] * outputs,
        compiler_params=pltpu.CompilerParams(
            dimension_semantics=("arbitrary",), vmem_limit_bytes=VMEM_LIMIT
        ),
        cost_estimate=SMALL_COST,
    )(first, second)
    seq.mark(sums[0])
    return sums


def core_sums(seq, keep, moved):
    sums = add_blocks(seq, keep, moved, keep.shape[0])
    return {2 * place: part for place, part in enumerate(sums)}


def chip_moves(seq, pieces, lane):
    bit = 2
    while 2 * bit < lax.axis_size("tok"):
        pieces = {
            away: add_blocks(seq, part, lane.flip(pieces[away | bit], bit), 1)[0]
            for away, part in pieces.items()
            if not away & bit
        }
        bit *= 2
    if bit >= lax.axis_size("tok"):
        return pieces[0], jnp.zeros_like(pieces[0])
    return pieces[0], lane.flip(pieces[bit], bit)


def exchange(pieces, lane):
    count = lax.axis_size("tok")
    rank = lax.axis_index("tok")
    held = {away: [(0, part)] for away, part in pieces.items()}
    bit = count // 2
    while bit > 0:
        leaving = jnp.stack([part for away in held if away & bit for source, part in held[away]])
        moved = lane.flip(leaving, bit) if bit > 1 else flip(leaving, "tok", bit)
        place, kept = 0, {}
        for away in [away for away in held if not away & bit]:
            kept[away] = list(held[away])
            for source, part in held[away | bit]:
                kept[away].append((source ^ bit, moved[place]))
                place += 1
        held = kept
        bit //= 2
    came = jnp.stack([part for source, part in sorted(held[0], key=lambda pair: pair[0])])
    return [
        lax.dynamic_index_in_dim(came, jnp.bitwise_xor(rank, place), 0, keepdims=False)
        for place in range(count)
    ]


class Line:
    def __init__(self, seq):
        self.seq = seq
        self.on_line = lax.axis_size("rep") == 4
        rank = lax.axis_index("rep")
        self.inner = ((rank == 1) | (rank == 2)).astype(jnp.int32).reshape(1)
        self.chunks, self.totals, self.outward = [], {}, {}
        self.place = 0
        self.came, self.pair, self.over = None, None, None

    def outer(self, load, pairs):
        return lax.ppermute(load, "rep", pairs)

    def add(self, chunk):
        self.chunks.append(chunk)
        if self.on_line and len(self.chunks) == 1:
            self.came = self.outer(chunk, [(0, 1), (3, 2)])

    def step(self, final=False):
        if not self.on_line:
            return
        k, seq = self.place, self.seq
        count = len(self.chunks)
        has_pair, has_total, has_next = k < count, 1 <= k <= count, k + 1 < count
        shape = self.chunks[0].shape
        ins, names = [], []
        if has_pair:
            ins += [self.chunks[k], self.came]
        if has_total:
            ins += [self.pair, self.over]
        if has_total and has_next:
            ins += [self.chunks[k + 1]]
        ins[0] = seq.then(ins[0])
        outs = int(has_pair) + int(has_total) * (2 if has_next else 1)
        tile = shape[0] // 2

        def kernel(inner_ref, *refs):
            ins_left, outs_left = list(refs[: len(ins)]), list(refs[len(ins) :])

            def plus(one, two):
                return (one[...].astype(jnp.float32) + two[...].astype(jnp.float32)).astype(
                    jnp.bfloat16
                )

            if has_pair:
                outs_left.pop(0)[...] = plus(ins_left.pop(0), ins_left.pop(0))
            if has_total:
                total = plus(ins_left.pop(0), ins_left.pop(0))
                outs_left.pop(0)[...] = total
                if has_next:
                    load_ref, next_ref = outs_left.pop(0), ins_left.pop(0)

                    @pl.when(inner_ref[0] == 1)
                    def send_total():
                        load_ref[...] = total

                    @pl.when(inner_ref[0] != 1)
                    def send_chunk():
                        load_ref[...] = next_ref[...]

        spec = pl.BlockSpec((tile, shape[1]), lambda step: (step, 0))
        made = list(
            pl.pallas_call(
                kernel,
                grid=(2,),
                in_specs=[pl.BlockSpec(memory_space=pltpu.SMEM)] + [spec] * len(ins),
                out_specs=[spec] * outs,
                out_shape=[bf16(*shape)] * outs,
                compiler_params=pltpu.CompilerParams(
                    dimension_semantics=("arbitrary",), vmem_limit_bytes=VMEM_LIMIT
                ),
                cost_estimate=SMALL_COST,
            )(self.inner, *ins)
        )
        seq.mark(made[0])
        if has_pair:
            self.pair = made.pop(0)
            self.over = lax.ppermute(self.pair, "rep", [(1, 2), (2, 1)])
        if has_total:
            self.totals[k - 1] = made.pop(0)
            if has_next:
                self.came = self.outer(made.pop(0), [(0, 1), (1, 0), (2, 3), (3, 2)])
                self.outward[k - 1] = self.came
            else:
                self.outward[k - 1] = self.outer(self.totals[k - 1], [(1, 0), (2, 3)])
        elif has_next:
            self.came = self.outer(self.chunks[k + 1], [(0, 1), (3, 2)])
        self.place += 1

    def finish(self):
        if not self.on_line:
            return [lax.psum(chunk, "rep").astype(jnp.float32) for chunk in self.chunks]
        while self.place <= len(self.chunks):
            self.step()
        return [
            jnp.where(self.inner[0] == 1, self.totals[k], self.outward[k]).astype(jnp.float32)
            for k in range(len(self.chunks))
        ]


def tok_total(values):
    bit = 1
    while bit < lax.axis_size("tok"):
        values = values + flip(values, "tok", bit)
        bit *= 2
    return values


def rep_gather(values):
    count = lax.axis_size("rep")
    rank = lax.axis_index("rep")
    pieces = values[None]
    bit = 1
    while bit < count:
        pieces = jnp.concatenate([pieces, flip(pieces, "rep", bit)], axis=0)
        bit *= 2
    return jnp.stack(
        [
            lax.dynamic_index_in_dim(pieces, jnp.bitwise_xor(rank, place), 0, keepdims=False)
            for place in range(count)
        ]
    )


def product(left, right):
    return jnp.dot(left, right, preferred_element_type=jnp.float32)


def product_back(left, right):
    return lax.dot_general(
        left, right, (((1,), (1,)), ((), ())), preferred_element_type=jnp.float32
    )


def tile_spec(rank, rows, columns):
    if rank == 3:
        return pl.BlockSpec((1, rows, columns), lambda step: (step, 0, 0))
    return pl.BlockSpec((rows, columns), lambda step: (0, step))


def whole_spec(array):
    zeros = (0,) * array.ndim
    return pl.BlockSpec(array.shape, lambda step: zeros, pipeline_mode=pl.Buffered(1))


def tile_of(ref):
    return ref[0] if len(ref.shape) == 3 else ref[...]


def fill(scratch, spot, parts, refs):
    rank, parity = spot[0], spot[1]
    share = parts[0].array.shape[-2]
    for part, ref in zip(parts, refs, strict=True):
        rows = part.array.shape[-2]
        start = jnp.bitwise_xor(rank, part.away) * share
        if part.half is not None:
            start = start + jnp.bitwise_xor(parity, part.half) * rows
        scratch[pl.ds(pl.multiple_of(start, rows), rows), :] = tile_of(ref)


def fill_one(scratch, spot, parts, refs, which):
    rank, parity = spot[0], spot[1]
    share = parts[0].array.shape[-2]
    for part, ref in zip(parts, refs, strict=True):
        start = pl.multiple_of(jnp.bitwise_xor(rank, part.away) * share, share)

        def lay(start=start, ref=ref):
            scratch[pl.ds(start, share), :] = tile_of(ref)

        if part.half is None:
            lay()
        else:
            pl.when(jnp.bitwise_xor(parity, part.half) == which)(lay)


def one_specs(parts, which):
    return [
        pl.BlockSpec(
            (1,) + part.array.shape[1:],
            functools.partial(lambda at, step: (at, 0, 0), which if part.half is None else 0),
        )
        for part in parts
    ]


def put_grad(spot, left_ref, right, keep_ref, send_ref, rows, count):
    rank = spot[0]
    for away in range(count):
        at = pl.ds(pl.multiple_of(jnp.bitwise_xor(rank, away) * rows, rows), rows)
        block = product(left_ref[at, :], right).astype(jnp.bfloat16)
        to = send_ref if away & 1 else keep_ref
        to[away // 2, 0] = block


def grad_specs(count, rows, columns):
    return pl.BlockSpec((count // 2, 1, rows, columns), lambda step: (0, step, 0, 0))


def call(kernel, tiles, spot, arrays, specs, outs, out_specs, scratch):
    return pl.pallas_call(
        kernel,
        grid=(tiles,),
        in_specs=[pl.BlockSpec(memory_space=pltpu.SMEM)] + specs,
        out_specs=out_specs,
        out_shape=outs,
        scratch_shapes=scratch,
        compiler_params=pltpu.CompilerParams(
            dimension_semantics=("arbitrary",), vmem_limit_bytes=VMEM_LIMIT
        ),
        cost_estimate=SMALL_COST,
    )(spot, *arrays)


def bf16(*shape):
    return jax.ShapeDtypeStruct(shape, jnp.bfloat16)


def project(spot, rows_in, parts):
    arrays = [part.array for part in parts]
    tiles, share, columns = arrays[0].shape
    length, width = rows_in.shape

    def kernel(spot_ref, in_ref, *rest):
        refs, out_ref, scratch = rest[:-2], rest[-2], rest[-1]
        fill(scratch, spot_ref, parts, refs)
        out_ref[0] = product(in_ref[...], scratch[...]).astype(jnp.bfloat16)

    return call(
        kernel,
        tiles,
        spot,
        [rows_in] + arrays,
        [whole_spec(rows_in)] + [tile_spec(3, part.shape[1], columns) for part in arrays],
        bf16(tiles, length, columns),
        pl.BlockSpec((1, length, columns), lambda step: (step, 0, 0)),
        [pltpu.VMEM((width, columns), jnp.bfloat16)],
    )


def project_back(spot, rows_in, parts, which, width):
    arrays = [part.array for part in parts]
    columns = arrays[0].shape[-1]
    length = rows_in.shape[0]

    def kernel(spot_ref, in_ref, *rest):
        refs, out_ref, scratch = rest[:-2], rest[-2], rest[-1]
        fill_one(scratch, spot_ref, parts, refs, which)
        out_ref[...] = product_back(in_ref[...], scratch[...]).astype(jnp.bfloat16)

    return call(
        kernel,
        1,
        spot,
        [rows_in] + arrays,
        [whole_spec(rows_in)] + one_specs(parts, which),
        bf16(length, width),
        pl.BlockSpec((length, width), lambda step: (0, 0)),
        [pltpu.VMEM((width, columns), jnp.bfloat16)],
    )


def proj_grads(spot, grad_rows, mixed_rows, parts, which):
    arrays = [part.array for part in parts]
    share, columns = arrays[0].shape[-2:]
    length, width = grad_rows.shape
    count = width // share

    def kernel(spot_ref, grad_ref, mixed_ref, *rest):
        refs, (out_ref, keep_ref, send_ref, scratch, turned) = rest[:-5], rest[-5:]
        fill_one(scratch, spot_ref, parts, refs, which)
        turned[...] = jnp.transpose(grad_ref[...])
        out_ref[...] = product(grad_ref[...], scratch[...]).astype(jnp.bfloat16)
        put_grad(spot_ref, turned, mixed_ref[...], keep_ref, send_ref, share, count)

    half = bf16(count // 2, 1, share, columns)
    return call(
        kernel,
        1,
        spot,
        [grad_rows, mixed_rows] + arrays,
        [whole_spec(grad_rows), whole_spec(mixed_rows)] + one_specs(parts, which),
        (bf16(length, columns), half, half),
        (pl.BlockSpec((length, columns), lambda step: (0, 0)),)
        + (grad_specs(count, share, columns),) * 2,
        [pltpu.VMEM((width, columns), jnp.bfloat16), pltpu.VMEM((width, length), jnp.bfloat16)],
    )


def qkv_grads(spot, hidden, query_grad, block_grads, parts):
    arrays = [part.array for part in parts]
    tiles, share, columns = arrays[0].shape
    length, width = hidden.shape
    count = width // share

    def kernel(spot_ref, hid_ref, query_ref, block_ref, *rest):
        refs, (out_ref, keep_ref, send_ref, scratch, total, turned, grad) = rest[:-7], rest[-7:]
        step = pl.program_id(0)
        fill(scratch, spot_ref, parts, refs)

        @pl.when(step == 0)
        def first():
            turned[...] = jnp.transpose(hid_ref[...])
            total[...] = jnp.zeros_like(total)
            grad[...] = query_ref[...]

        @pl.when(step > 0)
        def later():
            grad[...] = block_ref[0]

        total[...] += product_back(grad[...], scratch[...])
        put_grad(spot_ref, turned, grad[...], keep_ref, send_ref, share, count)

        @pl.when(step == tiles - 1)
        def finish():
            out_ref[...] = total[...].astype(jnp.bfloat16)

    half = bf16(count // 2, tiles, share, columns)
    return call(
        kernel,
        tiles,
        spot,
        [hidden, query_grad, block_grads] + arrays,
        [
            whole_spec(hidden),
            whole_spec(query_grad),
            pl.BlockSpec((1, length, columns), lambda step: (jnp.maximum(step - 1, 0), 0, 0)),
        ]
        + [tile_spec(3, part.shape[1], columns) for part in arrays],
        (bf16(length, width), half, half),
        (pl.BlockSpec((length, width), lambda step: (0, 0)),)
        + (grad_specs(count, share, columns),) * 2,
        [
            pltpu.VMEM((width, columns), jnp.bfloat16),
            pltpu.VMEM((length, width), jnp.float32),
            pltpu.VMEM((width, length), jnp.bfloat16),
            pltpu.VMEM((length, columns), jnp.bfloat16),
        ],
    )


def gelu_parts(upward):
    squared = upward * upward
    bent = jnp.tanh(0.7978845608028654 * (upward + 0.044715 * (upward * squared)))
    activ = 0.5 * upward * (1.0 + bent)
    slope = 0.5 * (1.0 + bent) + 0.5 * upward * (1.0 - bent * bent) * (
        0.7978845608028654 * (1.0 + 3 * 0.044715 * squared)
    )
    return activ, slope


def feed_forward(spot, hidden, grad, up_parts, down_parts, columns):
    arrays = [part.array for part in up_parts + down_parts]
    share, units = arrays[0].shape
    tiles = units // columns
    length, width = hidden.shape
    count = width // share

    def kernel(spot_ref, hid_ref, grad_ref, *rest):
        refs, rest = rest[: len(arrays)], rest[len(arrays) :]
        out_ref, back_ref, up_keep, up_send, down_keep, down_send = rest[:6]
        up, down, out_sum, back_sum, hid_turned, grad_turned = rest[6:]
        step = pl.program_id(0)

        @pl.when(step == 0)
        def begin():
            hid_turned[...] = jnp.transpose(hid_ref[...])
            grad_turned[...] = jnp.transpose(grad_ref[...])
            out_sum[...] = jnp.zeros_like(out_sum)
            back_sum[...] = jnp.zeros_like(back_sum)

        fill(up, spot_ref, up_parts, refs[: len(up_parts)])
        fill(down, spot_ref, down_parts, refs[len(up_parts) :])
        activ, slope = gelu_parts(product(hid_ref[...], up[...]))
        activ = activ.astype(jnp.bfloat16)
        upward_grad = (product(grad_ref[...], down[...]) * slope).astype(jnp.bfloat16)
        out_sum[...] += product_back(activ, down[...])
        back_sum[...] += product_back(upward_grad, up[...])
        put_grad(spot_ref, grad_turned, activ, down_keep, down_send, share, count)
        put_grad(spot_ref, hid_turned, upward_grad, up_keep, up_send, share, count)

        @pl.when(step == tiles - 1)
        def finish():
            out_ref[...] = out_sum[...].astype(jnp.bfloat16)
            back_ref[...] = back_sum[...].astype(jnp.bfloat16)

    rows_spec = pl.BlockSpec((length, width), lambda step: (0, 0))
    wholes = [hidden, grad]
    return call(
        kernel,
        tiles,
        spot,
        wholes + arrays,
        [whole_spec(part) for part in wholes]
        + [tile_spec(2, part.shape[0], columns) for part in arrays],
        (bf16(length, width), bf16(length, width))
        + (bf16(count // 2, tiles, share, columns),) * 4,
        (rows_spec, rows_spec) + (grad_specs(count, share, columns),) * 4,
        [pltpu.VMEM((width, columns), jnp.bfloat16)] * 2
        + [pltpu.VMEM((length, width), jnp.float32)] * 2
        + [pltpu.VMEM((width, length), jnp.bfloat16)] * 2,
    )


def activate(seq, first, second):
    shape = first.shape
    tile = shape[1] // 2

    def kernel(first_ref, second_ref, out_ref):
        upward = first_ref[0].astype(jnp.float32) + second_ref[0].astype(jnp.float32)
        activ_grad = first_ref[1].astype(jnp.float32) + second_ref[1].astype(jnp.float32)
        activ, slope = gelu_parts(upward)
        out_ref[0] = activ.astype(jnp.bfloat16)
        out_ref[1] = (activ_grad * slope).astype(jnp.bfloat16)

    spec = pl.BlockSpec((2, tile, shape[2]), lambda step: (0, step, 0))
    return seq.mark(
        pl.pallas_call(
            kernel,
            grid=(2,),
            in_specs=[spec, spec],
            out_specs=spec,
            out_shape=bf16(*shape),
            compiler_params=pltpu.CompilerParams(
                dimension_semantics=("arbitrary",), vmem_limit_bytes=VMEM_LIMIT
            ),
            cost_estimate=SMALL_COST,
        )(seq.then(first), second)
    )


def spread_up(spot, rows_in, up_shard, down_shard, count):
    length, share = rows_in.shape[1:]
    columns = up_shard.shape[1] // count

    def kernel(spot_ref, in_ref, up_ref, down_ref, keep_ref, send_ref):
        upward = product(in_ref[0], up_ref[...]).astype(jnp.bfloat16)
        activ_grad = product(in_ref[1], down_ref[...]).astype(jnp.bfloat16)
        odd = pl.program_id(0) % 2

        @pl.when(odd == 0)
        def keep():
            keep_ref[0, 0], keep_ref[0, 1] = upward, activ_grad

        @pl.when(odd != 0)
        def send():
            send_ref[0, 0], send_ref[0, 1] = upward, activ_grad

    shard_spec = pl.BlockSpec(
        (share, columns), lambda step, spot_ref: (0, jnp.bitwise_xor(spot_ref[0], step))
    )
    out_spec = pl.BlockSpec((1, 2, length, columns), lambda step, spot_ref: (step // 2, 0, 0, 0))
    out = bf16(count // 2, 2, length, columns)
    return pl.pallas_call(
        kernel,
        grid_spec=pltpu.PrefetchScalarGridSpec(
            num_scalar_prefetch=1,
            grid=(count,),
            in_specs=[
                pl.BlockSpec(rows_in.shape, lambda step, spot_ref: (0, 0, 0)),
                shard_spec,
                shard_spec,
            ],
            out_specs=[out_spec, out_spec],
        ),
        out_shape=[out, out],
        compiler_params=pltpu.CompilerParams(
            dimension_semantics=("arbitrary",), vmem_limit_bytes=VMEM_LIMIT
        ),
        cost_estimate=SMALL_COST,
    )(spot, rows_in, up_shard, down_shard)


def spread_down(spot, rows_in, blocks, up_shard, down_shard):
    count = len(blocks)
    length, columns = blocks[0].shape[1:]
    share, units = up_shard.shape

    def kernel(spot_ref, in_ref, up_ref, down_ref, *rest):
        refs, (out_ref, up_grad_ref, down_grad_ref) = rest[:count], rest[count:]
        hid_turned, grad_turned = jnp.transpose(in_ref[0]), jnp.transpose(in_ref[1])
        out_sum = jnp.zeros((length, share), jnp.float32)
        back_sum = jnp.zeros((length, share), jnp.float32)
        for away, ref in enumerate(refs):
            place = jnp.bitwise_xor(spot_ref[0], away)
            at = pl.ds(pl.multiple_of(place * columns, columns), columns)
            activ, upward_grad = ref[0], ref[1]
            out_sum += product_back(activ, down_ref[:, at])
            back_sum += product_back(upward_grad, up_ref[:, at])
            up_grad_ref[place] = product(hid_turned, upward_grad).astype(jnp.bfloat16)
            down_grad_ref[place] = product(grad_turned, activ).astype(jnp.bfloat16)
        out_ref[0] = back_sum.astype(jnp.bfloat16)
        out_ref[1] = out_sum.astype(jnp.bfloat16)

    zeros = lambda step: (0, 0, 0)
    arrays = [rows_in, up_shard, down_shard] + list(blocks)
    return call(
        kernel,
        1,
        spot,
        arrays,
        [whole_spec(part) for part in arrays],
        (bf16(2, length, share),) + (bf16(count, share, columns),) * 2,
        (pl.BlockSpec((2, length, share), zeros),)
        + (pl.BlockSpec((count, share, columns), zeros),) * 2,
        [],
    )


def spread_begin(seq, spot, hidden, grad, up_shard, down_shard, lane):
    count = lax.axis_size("tok")
    rank = lax.axis_index("tok")
    share = up_shard.shape[0]
    both = jnp.stack([hidden, grad])
    features = exchange(
        {
            away: lax.dynamic_slice_in_dim(
                both, jnp.bitwise_xor(rank, away) * share, share, axis=2
            )
            for away in range(count)
        },
        lane,
    )
    rows_in = seq.then(jnp.concatenate(features, axis=1))
    keep, send = spread_up(spot, rows_in, up_shard, down_shard, count)
    seq.mark(keep)
    pieces = core_sums(seq, keep, flip(send, "tok", 1))
    shape = (2,) + keep.shape[2:]
    stays, came = chip_moves(seq, pieces, lane)
    active = activate(seq, stays.reshape(shape), came.reshape(shape))
    return rows_in, gather_blocks(active, lane)


def spread_back(both, rows, lane):
    rank = lax.axis_index("tok")
    features = exchange(
        {
            away: lax.dynamic_slice_in_dim(both, jnp.bitwise_xor(rank, away) * rows, rows, axis=1)
            for away in range(lax.axis_size("tok"))
        },
        lane,
    )
    return jnp.concatenate(features, axis=2)


def row_kernel(seq, kernel, modul, rows_in, outs):
    seqs, length, width = rows_in[0].shape
    row_spec = pl.BlockSpec((1, length, width), lambda at: (at, 0, 0))
    sum_spec = pl.BlockSpec((1, 8, width), lambda at: (at, 0, 0))
    made = pl.pallas_call(
        kernel,
        grid=(seqs,),
        in_specs=[pl.BlockSpec((1,) + modul.shape[1:], lambda at: (at, 0, 0))]
        + [row_spec] * len(rows_in),
        out_specs=[sum_spec if kind is None else row_spec for kind in outs],
        out_shape=[
            jax.ShapeDtypeStruct((seqs, 8, width), jnp.float32)
            if kind is None
            else jax.ShapeDtypeStruct((seqs, length, width), kind)
            for kind in outs
        ],
        compiler_params=pltpu.CompilerParams(
            dimension_semantics=("arbitrary",), vmem_limit_bytes=VMEM_LIMIT
        ),
        cost_estimate=SMALL_COST,
    )(modul, seq.then(rows_in[0]), *rows_in[1:])
    seq.mark(made[0])
    return made


def wide(ref):
    return ref[0].astype(jnp.float32)


def put_sums(ref, rows):
    ref[0] = jnp.zeros_like(ref[0])
    for place, row in enumerate(rows):
        ref[0, place : place + 1] = jnp.sum(row, axis=0, keepdims=True)


def back_through(values, grad, scale_part):
    norm, factor = normed(values)
    inner = grad * (1.0 + scale_part)
    own = jnp.mean(inner, axis=-1, keepdims=True)
    along = jnp.mean(inner * norm, axis=-1, keepdims=True)
    return (inner - own - norm * along) * factor, norm


def first_hidden(seq, modul, stream):
    def kernel(mod_ref, x_ref, out_ref):
        norm, factor = normed(wide(x_ref))
        out_ref[0] = (norm * (1.0 + mod_ref[0, 1:2]) + mod_ref[0, 0:1]).astype(jnp.bfloat16)

    return row_kernel(seq, kernel, modul, [stream], [jnp.bfloat16])[0]


def middle_hidden(seq, modul, stream, branch, cot):
    def kernel(mod_ref, x_ref, one_ref, two_ref, cot_ref, hid_ref, grad_ref):
        middle = wide(x_ref) + mod_ref[0, 2:3] * (wide(one_ref) + wide(two_ref))
        norm, factor = normed(middle)
        hid_ref[0] = (norm * (1.0 + mod_ref[0, 4:5]) + mod_ref[0, 3:4]).astype(jnp.bfloat16)
        grad_ref[0] = (mod_ref[0, 5:6] * wide(cot_ref)).astype(jnp.bfloat16)

    return row_kernel(seq, kernel, modul, [stream, *branch, cot], [jnp.bfloat16, jnp.bfloat16])


def middle_grads(seq, modul, stream, branch, cot, hidden_grad):
    def kernel(mod_ref, x_ref, one_ref, two_ref, cot_ref, hid_ref, other_ref, mid_out, out, sums):
        branch_sum = wide(one_ref) + wide(two_ref)
        middle = wide(x_ref) + mod_ref[0, 2:3] * branch_sum
        grad = wide(hid_ref) + wide(other_ref)
        through, norm = back_through(middle, grad, mod_ref[0, 4:5])
        mid_grad = wide(cot_ref) + through
        mid_out[0] = mid_grad
        out[0] = (mod_ref[0, 2:3] * mid_grad).astype(jnp.bfloat16)
        put_sums(sums, [mid_grad * branch_sum, grad, grad * norm])

    return row_kernel(
        seq,
        kernel,
        modul,
        [stream, *branch, cot, *hidden_grad],
        [jnp.float32, jnp.bfloat16, None],
    )


def input_grads(seq, modul, stream, mid_grad, hidden_grad):
    def kernel(mod_ref, x_ref, mid_ref, hid_ref, other_ref, out, sums):
        grad = wide(hid_ref) + wide(other_ref)
        through, norm = back_through(wide(x_ref), grad, mod_ref[0, 1:2])
        out[0] = (mid_ref[0] + through).astype(jnp.bfloat16)
        put_sums(sums, [grad, grad * norm])

    return row_kernel(
        seq, kernel, modul, [stream, mid_grad, *hidden_grad], [jnp.bfloat16, None]
    )


def results(seq, modul, stream, branch, second, cot, real):
    def kernel(mod_ref, x_ref, one_ref, two_ref, three_ref, four_ref, cot_ref, out, sums):
        start = wide(x_ref)
        gated_one = mod_ref[0, 2:3] * (wide(one_ref) + wide(two_ref))
        middle = start + gated_one
        branch_two = wide(three_ref) + wide(four_ref)
        gated_two = mod_ref[0, 5:6] * branch_two
        result = middle + gated_two
        out[0] = result.astype(jnp.bfloat16)
        shown = lax.broadcasted_iota(jnp.int32, start.shape, 0) < real
        put_sums(
            sums,
            [wide(cot_ref) * branch_two]
            + [
                jnp.where(shown, member * member, 0.0)
                for member in (start, gated_one, middle, gated_two, result)
            ],
        )

    return row_kernel(
        seq, kernel, modul, [stream, *branch, *second, cot], [jnp.bfloat16, None]
    )


def head_lanes(shape, head):
    lane = lax.broadcasted_iota(jnp.int32, shape, len(shape) - 1)
    return (lane >= head * HD) & (lane < (head + 1) * HD)


def padding(shape, axis, image_rows, text_rows, real, count):
    place = lax.broadcasted_iota(jnp.int32, shape, axis) - image_rows * count
    hidden = (place >= real) & (place < text_rows)
    for other in range(1, count):
        hidden = hidden | (
            (place >= other * text_rows + real) & (place < (other + 1) * text_rows)
        )
    return hidden


def attention_specs(image, text):
    row = [
        pl.BlockSpec((1, rows, LANES), lambda seq, part: (seq, 0, part))
        for rows in (image.shape[1], text.shape[1])
    ]
    block = [
        pl.BlockSpec((2, 1, rows, LANES), lambda seq, part: (0, seq, 0, part))
        for rows in (image.shape[1], text.shape[1])
    ]
    return row, block


def joint(refs, index):
    return jnp.concatenate([ref[index] for ref in refs], axis=0)


def attend(image, text, image_blocks, text_blocks, real):
    seqs, image_rows, width = image.shape
    text_rows = text.shape[1]
    rows = image_rows + text_rows
    count = len(image_blocks)
    keys = rows * count

    def kernel(*rest):
        refs, (image_out, text_out) = rest[:-2], rest[-2:]
        queries = joint(refs[:2], 0)
        key_all = joint(refs[2:], (0, 0))
        value_all = joint(refs[2:], (1, 0))
        hidden = padding((1, keys), 1, image_rows, text_rows, real, count)
        result = jnp.zeros((rows, LANES), jnp.float32)
        for head in range(LANES // HD):
            mine = head_lanes((rows, LANES), head)
            scores = product_back(jnp.where(mine, queries, jnp.zeros_like(queries)), key_all)
            scores = jnp.where(hidden, -1e30, scores * 0.125)
            expd = jnp.exp(scores - jnp.max(scores, axis=1, keepdims=True))
            share = 1.0 / jnp.sum(expd, axis=1, keepdims=True)
            mixed = product((expd * share).astype(jnp.bfloat16), value_all)
            result = jnp.where(mine, mixed, result)
        image_out[0] = result[:image_rows].astype(jnp.bfloat16)
        text_out[0] = result[image_rows:].astype(jnp.bfloat16)

    row, block = attention_specs(image, text)
    return pl.pallas_call(
        kernel,
        grid=(seqs, width // LANES),
        in_specs=row + [block[0]] * count + [block[1]] * count,
        out_specs=row,
        out_shape=[bf16(*image.shape), bf16(*text.shape)],
        compiler_params=pltpu.CompilerParams(
            dimension_semantics=("arbitrary", "arbitrary"), vmem_limit_bytes=VMEM_LIMIT
        ),
        cost_estimate=SMALL_COST,
    )(image, text, *image_blocks, *text_blocks)


def attend_grads(queries_in, grads_in, image_blocks, text_blocks, real, seq):
    image, text = queries_in
    image_rows, width = image.shape[1:]
    text_rows = text.shape[1]
    rows = image_rows + text_rows
    count = len(image_blocks)
    keys = rows * count

    def kernel(*rest):
        refs, (image_out, text_out, image_keep, image_send, text_keep, text_send) = (
            rest[:-6],
            rest[-6:],
        )
        queries = joint(refs[:2], 0)
        grads = joint(refs[2:4], 0)
        key_all = joint(refs[4:], (0, 0))
        value_all = joint(refs[4:], (1, 0))
        hidden = padding((keys, 1), 0, image_rows, text_rows, real, count)
        query_grad = jnp.zeros((rows, LANES), jnp.float32)
        key_grad = jnp.zeros((keys, LANES), jnp.float32)
        value_grad = jnp.zeros((keys, LANES), jnp.float32)
        for head in range(LANES // HD):
            mine = head_lanes((rows, LANES), head)
            own_query = jnp.where(mine, queries, jnp.zeros_like(queries))
            own_grad = jnp.where(mine, grads, jnp.zeros_like(grads))
            scores = product_back(key_all, own_query)
            scores = jnp.where(hidden, -1e30, scores * 0.125)
            expd = jnp.exp(scores - jnp.max(scores, axis=0, keepdims=True))
            probs = expd * (1.0 / jnp.sum(expd, axis=0, keepdims=True))
            prob_grad = product_back(value_all, own_grad)
            delta = jnp.sum(probs * prob_grad, axis=0, keepdims=True)
            score_grad = (probs * (prob_grad - delta)).astype(jnp.bfloat16)
            value_grad += product(probs.astype(jnp.bfloat16), own_grad)
            key_grad += product(score_grad, own_query)
            back = lax.dot_general(
                score_grad, key_all, (((0,), (0,)), ((), ())), preferred_element_type=jnp.float32
            )
            query_grad = jnp.where(mine, back, query_grad)
        query_grad = (query_grad * 0.125).astype(jnp.bfloat16)
        image_out[0] = query_grad[:image_rows]
        text_out[0] = query_grad[image_rows:]
        key_grad = (key_grad * 0.125).astype(jnp.bfloat16)
        value_grad = value_grad.astype(jnp.bfloat16)
        for away in range(count):
            at = slice(away * image_rows, (away + 1) * image_rows)
            to = image_send if away & 1 else image_keep
            to[away // 2, 0], to[away // 2, 1] = key_grad[at], value_grad[at]
            first = count * image_rows + away * text_rows
            at = slice(first, first + text_rows)
            to = text_send if away & 1 else text_keep
            to[away // 2, 0], to[away // 2, 1] = key_grad[at], value_grad[at]

    def row_spec(length, at):
        return pl.BlockSpec((1, length, LANES), lambda part: (at, 0, part))

    def block_spec(length):
        return pl.BlockSpec((2, 1, length, LANES), lambda part: (0, seq, 0, part))

    def owner_spec(length):
        return pl.BlockSpec((count // 2, 2, length, LANES), lambda part: (0, 0, 0, part))

    sizes = (image_rows, text_rows)
    owners = [length for length in sizes for side in range(2)]
    return pl.pallas_call(
        kernel,
        grid=(width // LANES,),
        in_specs=[row_spec(length, seq) for length in sizes] * 2
        + [block_spec(image_rows)] * count
        + [block_spec(text_rows)] * count,
        out_specs=[row_spec(length, 0) for length in sizes]
        + [owner_spec(length) for length in owners],
        out_shape=[bf16(1, length, width) for length in sizes]
        + [bf16(count // 2, 2, length, width) for length in owners],
        compiler_params=pltpu.CompilerParams(
            dimension_semantics=("arbitrary",), vmem_limit_bytes=VMEM_LIMIT
        ),
        cost_estimate=SMALL_COST,
    )(image, text, *grads_in, *image_blocks, *text_blocks)


def on_device(
    image_tokens,
    text_tokens,
    text_owner,
    conditioning,
    slot_sequence,
    image_w_mod,
    image_b_mod,
    image_w_qkv,
    image_w_proj,
    image_w_up,
    image_w_down,
    text_w_mod,
    text_b_mod,
    text_w_qkv,
    text_w_proj,
    text_w_up,
    text_w_down,
    image_cotangent,
    text_cotangent,
):
    tok_rank = lax.axis_index("tok")
    rep_rank = lax.axis_index("rep")
    rep_count = lax.axis_size("rep")
    tok_count = lax.axis_size("tok")
    seqs, image_rows, width = image_tokens.shape
    text_real = text_cotangent.shape[1]
    text_rows = -(-text_real // 16) * 16
    slots = conditioning.shape[0]
    share = image_w_mod.shape[0]
    heads_width = image_w_qkv.shape[2]
    spot = jnp.stack([tok_rank, lax.rem(rep_rank, 2)]).astype(jnp.int32)

    turn = lambda weight: jnp.transpose(weight, (1, 0, 2))
    chips = Lane("tok", 2)
    image_qkv_parts = gather_weight(turn(image_w_qkv), 1, chips)

    picker = (slot_sequence[:, None] == jnp.arange(slots, dtype=jnp.int32)[None, :]).astype(
        jnp.float32
    )
    cond_slots = jnp.dot(picker, conditioning, precision=exact_mode)
    activ_all = jax.nn.silu(cond_slots).astype(jnp.bfloat16)
    activ_group = lax.dynamic_slice_in_dim(activ_all, rep_rank * seqs, seqs, axis=0)
    activ_share = lax.dynamic_slice_in_dim(activ_group, tok_rank * share, share, axis=1)
    both_mod = tok_total(
        jnp.stack(
            [
                jnp.einsum("sd,dke->ske", activ_share, weight, preferred_element_type=jnp.float32)
                for weight in (image_w_mod, text_w_mod)
            ]
        )
    )
    image_mod = both_mod[0] + image_b_mod.astype(jnp.float32)[None]
    text_mod = both_mod[1] + text_b_mod.astype(jnp.float32)[None]

    text_qkv_parts = gather_weight(turn(text_w_qkv), 1, chips, (both_mod,))
    proj_parts = gather_weight(jnp.stack([image_w_proj, text_w_proj]), 0, chips)

    owned = (text_owner == tok_rank).astype(jnp.float32)
    total_text = text_owner.shape[1]
    before = jnp.dot(
        owned,
        jnp.triu(jnp.ones((total_text, total_text), jnp.float32), 1),
        precision=exact_mode,
    )
    chosen = (
        (before[:, None, :] == jnp.arange(text_rows, dtype=jnp.float32)[None, :, None])
        & (owned[:, None, :] > 0.5)
    ).astype(jnp.bfloat16)
    text_input = jnp.einsum(
        "srt,std->srd", chosen, text_tokens, preferred_element_type=jnp.float32
    ).astype(jnp.bfloat16)
    text_cot = jnp.pad(text_cotangent, ((0, 0), (0, text_rows - text_real), (0, 0)))

    seq = Sequence()
    flat = lambda values: values.reshape(-1, values.shape[-1])
    by_seq = lambda values: values.reshape(values.shape[:-2] + (seqs, -1, values.shape[-1]))
    both = lambda pair: tuple(by_seq(part) for part in pair)
    heads = lambda partial: both(head_pair(partial))

    image_hid_one = flat(first_hidden(seq, image_mod, image_tokens))
    image_qkv = seq.mark(project(spot, image_hid_one, image_qkv_parts))
    image_blocks = gather_blocks(by_seq(image_qkv[1:]), chips)
    text_hid_one = flat(first_hidden(seq, text_mod, text_input))
    text_qkv = seq.mark(project(spot, text_hid_one, text_qkv_parts))
    text_blocks = gather_blocks(by_seq(text_qkv[1:]), chips)
    image_up_parts = gather_weight(image_w_up, 0, chips)
    image_down_parts = gather_weight(image_w_down, 0, chips)
    image_query, text_query = by_seq(image_qkv[0]), by_seq(text_qkv[0])
    image_mix, text_mix = attend(image_query, text_query, image_blocks, text_blocks, text_real)
    image_mixed, text_mixed = flat(image_mix), flat(text_mix)
    text_out = seq.mark(project_back(spot, text_mixed, proj_parts, 1, width))
    text_branch = heads(text_out)
    image_out = seq.mark(project_back(spot, seq.then(image_mixed), proj_parts, 0, width))
    image_branch = heads(image_out)

    text_hid_two, text_db_two = middle_hidden(seq, text_mod, text_input, text_branch, text_cot)
    text_in, text_active = spread_begin(
        seq, spot, flat(text_hid_two), flat(text_db_two), text_w_up, text_w_down, chips
    )
    image_hid_two, image_db_two = middle_hidden(
        seq, image_mod, image_tokens, image_branch, image_cotangent
    )
    image_part, image_back, image_up_keep, image_up_send, image_down_keep, image_down_send = (
        feed_forward(
            spot,
            flat(image_hid_two),
            flat(image_db_two),
            image_up_parts,
            image_down_parts,
            heads_width,
        )
    )
    seq.mark(image_back)
    image_hid_grad = heads(image_back)
    down_moved = flip(image_down_send, "tok", 1)
    up_moved = flip(image_up_send, "tok", 1)
    text_sums, text_up_grad, text_down_grad = spread_down(
        spot, seq.then(text_in), text_active, text_w_up, text_w_down
    )
    seq.mark(text_sums)
    line = Line(seq)
    for whole in (text_down_grad, text_up_grad):
        for place in range(2):
            line.add(flat(whole.reshape(2, -1, share, whole.shape[-1])[place]))
    image_down_pieces = core_sums(seq, image_down_keep, down_moved)
    image_down_pair = chip_moves(seq, image_down_pieces, chips)
    text_back, text_part = spread_back(text_sums, flat(text_input).shape[0], chips)
    text_hid_grad = heads(text_back)
    image_up_pieces = core_sums(seq, image_up_keep, up_moved)
    image_up_pair = chip_moves(seq, image_up_pieces, chips)

    image_mid_grad, image_db_one, image_mid_sums = middle_grads(
        seq, image_mod, image_tokens, image_branch, image_cotangent, image_hid_grad
    )
    image_mixed_grad, image_proj_keep, image_proj_send = proj_grads(
        spot, flat(image_db_one), image_mixed, proj_parts, 0
    )
    seq.mark(image_mixed_grad)
    line.step()
    text_mid_grad, text_db_one, text_mid_sums = middle_grads(
        seq, text_mod, text_input, text_branch, text_cot, text_hid_grad
    )
    text_mixed_grad, text_proj_keep, text_proj_send = proj_grads(
        spot, flat(text_db_one), text_mixed, proj_parts, 1
    )
    seq.mark(text_mixed_grad)
    grads_all = []
    mix_grads = (by_seq(image_mixed_grad), by_seq(text_mixed_grad))
    for at in range(seqs):
        made = attend_grads(
            (image_query, text_query),
            (seq.then(mix_grads[0]), mix_grads[1]),
            image_blocks,
            text_blocks,
            text_real,
            at,
        )
        seq.mark(made[0])
        grads_all.append(made)
        line.step()
        if at == 0:
            for part in add_blocks(seq, *image_down_pair, 2):
                line.add(part)
    image_query_grad, text_query_grad, *block_grads = [
        jnp.stack(parts, axis=-3) for parts in zip(*grads_all)
    ]
    text_pieces = core_sums(seq, block_grads[2], flip(block_grads[3], "tok", 1))
    text_moves = chip_moves(seq, text_pieces, chips)
    image_pieces = core_sums(seq, block_grads[0], flip(block_grads[1], "tok", 1))
    image_moves = chip_moves(seq, image_pieces, chips)
    for part in add_blocks(seq, *image_up_pair, 2):
        line.add(part)
    line.step()
    tail = Line(seq)
    proj_pairs = [
        chip_moves(seq, core_sums(seq, keep, flip(send, "tok", 1)), chips)
        for keep, send in ((image_proj_keep, image_proj_send), (text_proj_keep, text_proj_send))
    ]
    pair_of = lambda values: values.reshape(2, -1, heads_width)
    text_block_grad = pair_of(add_blocks(seq, *text_moves, 1)[0])
    text_in_part, text_qkv_keep, text_qkv_send = qkv_grads(
        spot, text_hid_one, flat(text_query_grad[0]), text_block_grad, text_qkv_parts
    )
    seq.mark(text_in_part)
    image_block_grad = pair_of(add_blocks(seq, *image_moves, 1)[0])
    image_in_part, image_qkv_keep, image_qkv_send = qkv_grads(
        spot, image_hid_one, flat(image_query_grad[0]), image_block_grad, image_qkv_parts
    )
    seq.mark(image_in_part)
    line.step()
    qkv_pairs = [
        chip_moves(seq, core_sums(seq, keep, flip(send, "tok", 1)), chips)
        for keep, send in ((image_qkv_keep, image_qkv_send), (text_qkv_keep, text_qkv_send))
    ]
    text_in_grad = heads(text_in_part)
    image_in_grad = heads(image_in_part)
    text_second = heads(after(text_part, image_in_part))
    image_second = heads(after(image_part, image_in_part))
    line.step()
    image_proj_share, text_proj_share = [add_blocks(seq, *pair, 1)[0] for pair in proj_pairs]
    line.step()
    text_grad, text_in_sums = input_grads(
        seq, text_mod, text_input, text_mid_grad, text_in_grad
    )
    image_grad, image_in_sums = input_grads(
        seq, image_mod, image_tokens, image_mid_grad, image_in_grad
    )
    line.step()
    ff_sums = line.finish()
    tail.add(image_proj_share)
    tail.add(text_proj_share)
    for part in add_blocks(seq, *qkv_pairs[0], 3):
        tail.add(part)
    tail.step()
    text_result, text_out_sums = results(
        seq, text_mod, text_input, text_branch, text_second, text_cot, text_real
    )
    image_result, image_out_sums = results(
        seq, image_mod, image_tokens, image_branch, image_second, image_cotangent, image_rows
    )
    tail.step()
    for part in add_blocks(seq, *qkv_pairs[1], 3):
        tail.add(part)
    tail_sums = tail.finish()
    columns_of = lambda place: jnp.concatenate(
        [
            column
            for part in ff_sums[place : place + 2]
            for column in part.reshape(-1, share, part.shape[-1])
        ],
        axis=1,
    )
    text_down_sum, text_up_sum, image_down_sum, image_up_sum = map(columns_of, (0, 2, 4, 6))
    image_proj_sum, text_proj_sum = tail_sums[:2]
    image_qkv_sum = jnp.stack(tail_sums[2:5], axis=1)
    text_qkv_sum = jnp.stack(tail_sums[5:], axis=1)

    early = jnp.stack(
        [
            jnp.concatenate([mid_sums[:, :3], out_sums[:, :1]], axis=1)
            for mid_sums, out_sums in (
                (image_mid_sums, image_out_sums),
                (text_mid_sums, text_out_sums),
            )
        ]
    )
    late = jnp.stack([image_in_sums[:, :2], text_in_sums[:, :2]])
    squares = jnp.concatenate(
        [jnp.sum(out_sums[:, 1:6], axis=(0, 2)) for out_sums in (image_out_sums, text_out_sums)]
    )
    square_row = jnp.pad(squares, (0, width - 10))[None]
    all_sums = jnp.concatenate(
        [early.reshape(-1, width), late.reshape(-1, width), square_row], axis=0
    )
    all_sums = rep_gather(tok_total(all_sums))
    square_total = jnp.sum(all_sums[:, -1, :10], axis=0)
    early_table = jnp.moveaxis(
        all_sums[:, : 8 * seqs].reshape(rep_count, 2, seqs, 4, width), 0, 1
    ).reshape(2, slots, 4, width)
    late_table = jnp.moveaxis(
        all_sums[:, 8 * seqs : -1].reshape(rep_count, 2, seqs, 2, width), 0, 1
    ).reshape(2, slots, 2, width)
    mod_sum = jnp.concatenate([late_table, early_table], axis=2)

    activ_rows = lax.dynamic_slice_in_dim(activ_all, tok_rank * share, share, axis=1).astype(
        jnp.float32
    )
    image_g_mod = jnp.einsum("sd,ske->dke", activ_rows, mod_sum[0], precision=exact_mode)
    text_g_mod = jnp.einsum("sd,ske->dke", activ_rows, mod_sum[1], precision=exact_mode)
    image_g_bmod = jnp.sum(mod_sum[0], axis=0)
    text_g_bmod = jnp.sum(mod_sum[1], axis=0)
    activ_grad = jnp.einsum(
        "ske,dke->sd", mod_sum[0], image_w_mod.astype(jnp.float32), precision=exact_mode
    ) + jnp.einsum("ske,dke->sd", mod_sum[1], text_w_mod.astype(jnp.float32), precision=exact_mode)
    cond_rows = lax.dynamic_slice_in_dim(cond_slots, tok_rank * share, share, axis=1)
    unused_value, silu_back = jax.vjp(jax.nn.silu, cond_rows)
    slot_grad = silu_back(activ_grad)[0]
    cond_grad = jnp.dot(jnp.transpose(picker), slot_grad, precision=exact_mode)
    image_count = float(slots * image_rows * tok_count * width)
    text_count = float(slots * text_real * tok_count * width)
    counts = jnp.concatenate(
        [jnp.full((5,), image_count, jnp.float32), jnp.full((5,), text_count, jnp.float32)]
    )
    stream_rms = jnp.sqrt(square_total / counts)
    return (
        image_result,
        text_result[:, :text_real],
        image_grad,
        text_grad[:, :text_real],
        cond_grad,
        image_g_mod,
        image_g_bmod,
        image_qkv_sum,
        image_proj_sum,
        image_up_sum,
        image_down_sum,
        text_g_mod,
        text_g_bmod,
        text_qkv_sum,
        text_proj_sum,
        text_up_sum,
        text_down_sum,
        stream_rms,
    )


def solution(mesh):
    in_specs = (
        P("rep", "tok", None),
        P("rep", None, None),
        P("rep", None),
        P(),
        P(),
        P("tok", None, None),
        P(),
        P("tok", None, "head"),
        P("tok", "head"),
        P("tok", "head"),
        P("tok", "head"),
        P("tok", None, None),
        P(),
        P("tok", None, "head"),
        P("tok", "head"),
        P("tok", "head"),
        P("tok", "head"),
        P("rep", "tok", None),
        P("rep", "tok", None),
    )
    out_specs = (
        P("rep", "tok", None),
        P("rep", "tok", None),
        P("rep", "tok", None),
        P("rep", "tok", None),
        P(None, "tok"),
        P("tok", None, None),
        P(),
        P("tok", None, "head"),
        P("tok", "head"),
        P("tok", "head"),
        P("tok", "head"),
        P("tok", None, None),
        P(),
        P("tok", None, "head"),
        P("tok", "head"),
        P("tok", "head"),
        P("tok", "head"),
        P(),
    )
    return jax.shard_map(
        on_device, mesh=mesh, in_specs=in_specs, out_specs=out_specs, check_vma=False
    )
```

```python
import functools

import jax
import jax.numpy as jnp
from jax import lax
from jax.experimental import pallas as pl
from jax.experimental.pallas import tpu as pltpu
from jax.sharding import PartitionSpec as P

HD = 64
LANES = 128
VMEM_LIMIT = 60 * 1024 * 1024
SMALL_COST = pl.CostEstimate(flops=1024, bytes_accessed=1024, transcendentals=0)

exact_mode = lax.Precision.HIGHEST


def normed(values):
    centered = values - jnp.mean(values, axis=-1, keepdims=True)
    scale = lax.rsqrt(jnp.mean(centered * centered, axis=-1, keepdims=True) + 1e-06)
    return centered * scale, scale


def flip(values, axis, bit):
    return lax.ppermute(
        values, axis, [(place, place ^ bit) for place in range(lax.axis_size(axis))]
    )


def head_pair(partial):
    if lax.axis_size("head") != 2:
        return lax.psum(partial, "head"), jnp.zeros_like(partial)
    return partial, flip(partial, "head", 1)


def after(values, *needed):
    return lax.optimization_barrier((values, *needed))[0]


class Sequence:
    def __init__(self):
        self.last = None

    def then(self, values):
        return values if self.last is None else after(values, *self.last)

    def mark(self, output, *moves):
        self.last = (output, *moves)
        return output


class Lane:
    def __init__(self, axis, depth):
        self.axis, self.depth, self.over = axis, depth, []

    def flip(self, values, bit):
        if len(self.over) >= self.depth:
            values = after(values, self.over[-self.depth])
        moved = flip(values, self.axis, bit)
        self.over.append(moved)
        return moved


class Part:
    def __init__(self, away, half, array):
        self.away, self.half, self.array = away, half, array


def fetch(weight, axis, lane, needed=()):
    parity = lax.rem(lax.axis_index("rep"), 2)
    size = weight.shape[axis] // 2
    held = {0: lax.dynamic_slice_in_dim(weight, parity * size, size, axis=axis)}
    if needed:
        held[0] = after(held[0], *needed)
    bit = lax.axis_size("tok") // 2
    while bit > 1:
        for away, array in list(held.items()):
            held[away ^ bit] = lane.flip(array, bit)
        bit //= 2
    del held[0]
    return held


def share_out(weight, own, held, needed=()):
    parts = []
    for away, array in held.items():
        parts += [Part(away, 0, array), Part(away, 1, flip(array, "rep", 1))]
    others = [
        Part(
            part.away ^ 1,
            part.half,
            flip(after(part.array, *needed) if needed else part.array, "tok", 1),
        )
        for part in parts
    ]
    swapped = [part.array for part in parts if part.half == 1]
    return [Part(0, None, weight)] + parts + [Part(1, None, own)] + others, swapped


def gather_blocks(values, lane):
    pieces = {0: values}
    bit = lax.axis_size("tok") // 2
    while bit > 0:
        for away, part in list(pieces.items()):
            pieces[away ^ bit] = lane.flip(part, bit) if bit > 1 else flip(part, "tok", bit)
        bit //= 2
    return [pieces[away] for away in range(len(pieces))]


def add_blocks(seq, first, second, outputs, kind=jnp.bfloat16):
    width = first.shape[-1]
    flat = lambda values: values.reshape(outputs, -1, width)
    first, second = flat(seq.then(first)), flat(second)
    rows = first.shape[1]
    tile = rows // 2

    def kernel(first_ref, second_ref, *out_refs):
        for place, out_ref in enumerate(out_refs):
            out_ref[...] = (
                first_ref[place].astype(jnp.float32) + second_ref[place].astype(jnp.float32)
            ).astype(kind)

    in_spec = pl.BlockSpec((outputs, tile, width), lambda step: (0, step, 0))
    sums = pl.pallas_call(
        kernel,
        grid=(2,),
        in_specs=[in_spec, in_spec],
        out_specs=[pl.BlockSpec((tile, width), lambda step: (step, 0))] * outputs,
        out_shape=[jax.ShapeDtypeStruct((rows, width), kind)] * outputs,
        compiler_params=pltpu.CompilerParams(
            dimension_semantics=("arbitrary",), vmem_limit_bytes=VMEM_LIMIT
        ),
        cost_estimate=SMALL_COST,
    )(first, second)
    seq.mark(sums[0])
    return sums


def core_sums(seq, keep, moved):
    sums = add_blocks(seq, keep, moved, keep.shape[0])
    return {2 * place: part for place, part in enumerate(sums)}


def core_sums_joined(seq, keeps, moved):
    pieces, pair, rows, width = keeps[0].shape
    pairs = len(keeps)

    def kernel(*refs):
        for at in range(pairs):
            for place in range(pieces):
                refs[2 * pairs + place][at] = (
                    refs[at][place].astype(jnp.float32)
                    + refs[pairs + at][place].astype(jnp.float32)
                ).astype(jnp.bfloat16)

    spec = pl.BlockSpec((pieces, 1, rows, width), lambda step: (0, step, 0, 0))
    sums = pl.pallas_call(
        kernel,
        grid=(pair,),
        in_specs=[spec] * (2 * pairs),
        out_specs=[pl.BlockSpec((pairs, 1, rows, width), lambda step: (0, step, 0, 0))] * pieces,
        out_shape=[bf16(pairs, pair, rows, width)] * pieces,
        compiler_params=pltpu.CompilerParams(
            dimension_semantics=("arbitrary",), vmem_limit_bytes=VMEM_LIMIT
        ),
        cost_estimate=SMALL_COST,
    )(seq.then(keeps[0]), *keeps[1:], *moved)
    seq.mark(sums[0])
    return {2 * place: part.reshape(-1, width) for place, part in enumerate(sums)}


def add_split(seq, first, second, groups, top):
    width = first.shape[-1]
    first, second = seq.then(first).reshape(groups, -1, width), second.reshape(groups, -1, width)
    rows = first.shape[1]

    def kernel(first_ref, second_ref, top_ref, bottom_ref):
        total = (first_ref[0].astype(jnp.float32) + second_ref[0].astype(jnp.float32)).astype(
            jnp.bfloat16
        )
        top_ref[0], bottom_ref[0] = total[:top], total[top:]

    spec = lambda length: pl.BlockSpec((1, length, width), lambda step: (step, 0, 0))
    parts = pl.pallas_call(
        kernel,
        grid=(groups,),
        in_specs=[spec(rows), spec(rows)],
        out_specs=[spec(top), spec(rows - top)],
        out_shape=[bf16(groups, top, width), bf16(groups, rows - top, width)],
        compiler_params=pltpu.CompilerParams(
            dimension_semantics=("arbitrary",), vmem_limit_bytes=VMEM_LIMIT
        ),
        cost_estimate=SMALL_COST,
    )(first, second)
    seq.mark(parts[0])
    return parts


def chip_moves(seq, pieces, lane):
    bit = 2
    while 2 * bit < lax.axis_size("tok"):
        pieces = {
            away: add_blocks(seq, part, lane.flip(pieces[away | bit], bit), 1)[0]
            for away, part in pieces.items()
            if not away & bit
        }
        bit *= 2
    if bit >= lax.axis_size("tok"):
        return pieces[0], jnp.zeros_like(pieces[0])
    return pieces[0], lane.flip(pieces[bit], bit)


def exchange(pieces):
    return [pieces[0]] + [flip(part, "tok", 1 + place) for place, part in enumerate(pieces[1:])]


class Line:
    def __init__(self, seq):
        self.seq = seq
        self.on_line = lax.axis_size("rep") == 4
        rank = lax.axis_index("rep")
        self.inner = ((rank == 1) | (rank == 2)).astype(jnp.int32).reshape(1)
        self.chunks, self.totals, self.outward = [], {}, {}
        self.place = 0
        self.came, self.pair, self.over = None, None, None

    def outer(self, load, pairs):
        return lax.ppermute(load, "rep", pairs)

    def add(self, chunk):
        self.chunks.append(chunk)
        if self.on_line and len(self.chunks) == 1:
            self.came = self.outer(chunk, [(0, 1), (3, 2)])

    def step(self, final=False):
        if not self.on_line or not self.chunks or self.place > len(self.chunks):
            return
        k, seq = self.place, self.seq
        count = len(self.chunks)
        has_pair, has_total, has_next = k < count, 1 <= k <= count, k + 1 < count
        shape = self.chunks[0].shape
        ins, names = [], []
        if has_pair:
            ins += [self.chunks[k], self.came]
        if has_total:
            ins += [self.pair, self.over]
        if has_total and has_next:
            ins += [self.chunks[k + 1]]
        ins[0] = seq.then(ins[0])
        outs = int(has_pair) + int(has_total) * (2 if has_next else 1)
        tile = shape[0] // 2

        def kernel(inner_ref, *refs):
            ins_left, outs_left = list(refs[: len(ins)]), list(refs[len(ins) :])

            def plus(one, two):
                return (one[...].astype(jnp.float32) + two[...].astype(jnp.float32)).astype(
                    jnp.bfloat16
                )

            if has_pair:
                outs_left.pop(0)[...] = plus(ins_left.pop(0), ins_left.pop(0))
            if has_total:
                total = plus(ins_left.pop(0), ins_left.pop(0))
                outs_left.pop(0)[...] = total
                if has_next:
                    load_ref, next_ref = outs_left.pop(0), ins_left.pop(0)

                    @pl.when(inner_ref[0] == 1)
                    def send_total():
                        load_ref[...] = total

                    @pl.when(inner_ref[0] != 1)
                    def send_chunk():
                        load_ref[...] = next_ref[...]

        spec = pl.BlockSpec((tile, shape[1]), lambda step: (step, 0))
        made = list(
            pl.pallas_call(
                kernel,
                grid=(2,),
                in_specs=[pl.BlockSpec(memory_space=pltpu.SMEM)] + [spec] * len(ins),
                out_specs=[spec] * outs,
                out_shape=[bf16(*shape)] * outs,
                compiler_params=pltpu.CompilerParams(
                    dimension_semantics=("arbitrary",), vmem_limit_bytes=VMEM_LIMIT
                ),
                cost_estimate=SMALL_COST,
            )(self.inner, *ins)
        )
        seq.mark(made[0])
        if has_pair:
            self.pair = made.pop(0)
            self.over = lax.ppermute(self.pair, "rep", [(1, 2), (2, 1)])
        if has_total:
            self.totals[k - 1] = made.pop(0)
            if has_next:
                self.came = self.outer(made.pop(0), [(0, 1), (1, 0), (2, 3), (3, 2)])
                self.outward[k - 1] = self.came
            else:
                self.outward[k - 1] = self.outer(self.totals[k - 1], [(1, 0), (2, 3)])
        elif has_next:
            self.came = self.outer(self.chunks[k + 1], [(0, 1), (3, 2)])
        self.place += 1

    def finish(self):
        if not self.on_line:
            return [lax.psum(chunk, "rep").astype(jnp.float32) for chunk in self.chunks]
        while self.place <= len(self.chunks):
            self.step()
        return [
            jnp.where(self.inner[0] == 1, self.totals[k], self.outward[k]).astype(jnp.float32)
            for k in range(len(self.chunks))
        ]


def tok_total(values, *needed):
    bit = 1
    while bit < lax.axis_size("tok"):
        if bit == 2 and needed:
            values = after(values, *needed)
        values = values + flip(values, "tok", bit)
        bit *= 2
    return values


def rep_gather(values):
    count = lax.axis_size("rep")
    rank = lax.axis_index("rep")
    pieces = values[None]
    bit = 1
    while bit < count:
        pieces = jnp.concatenate([pieces, flip(pieces, "rep", bit)], axis=0)
        bit *= 2
    return jnp.stack(
        [
            lax.dynamic_index_in_dim(pieces, jnp.bitwise_xor(rank, place), 0, keepdims=False)
            for place in range(count)
        ]
    )


def product(left, right):
    return jnp.dot(left, right, preferred_element_type=jnp.float32)


def product_back(left, right):
    return lax.dot_general(
        left, right, (((1,), (1,)), ((), ())), preferred_element_type=jnp.float32
    )


def tile_spec(rank, rows, columns):
    if rank == 3:
        return pl.BlockSpec((1, rows, columns), lambda step: (step, 0, 0))
    return pl.BlockSpec((rows, columns), lambda step: (0, step))


def whole_spec(array):
    zeros = (0,) * array.ndim
    return pl.BlockSpec(array.shape, lambda step: zeros, pipeline_mode=pl.Buffered(1))


def tile_of(ref):
    return ref[0] if len(ref.shape) == 3 else ref[...]


def fill(scratch, spot, parts, refs):
    rank, parity = spot[0], spot[1]
    share = parts[0].array.shape[-2]
    for part, ref in zip(parts, refs, strict=True):
        rows = part.array.shape[-2]
        start = jnp.bitwise_xor(rank, part.away) * share
        if part.half is not None:
            start = start + jnp.bitwise_xor(parity, part.half) * rows
        scratch[pl.ds(pl.multiple_of(start, rows), rows), :] = tile_of(ref)


def fill_one(scratch, spot, parts, refs, which):
    rank, parity = spot[0], spot[1]
    share = parts[0].array.shape[-2]
    for part, ref in zip(parts, refs, strict=True):
        start = pl.multiple_of(jnp.bitwise_xor(rank, part.away) * share, share)

        def lay(start=start, ref=ref):
            scratch[pl.ds(start, share), :] = tile_of(ref)

        if part.half is None:
            lay()
        else:
            pl.when(jnp.bitwise_xor(parity, part.half) == which)(lay)


def one_specs(parts, which):
    return [
        pl.BlockSpec(
            (1,) + part.array.shape[1:],
            functools.partial(lambda at, step: (at, 0, 0), which if part.half is None else 0),
        )
        for part in parts
    ]


def put_grad(spot, left_ref, right, keep_ref, send_ref, rows, count):
    rank = spot[0]
    for away in range(count):
        at = pl.ds(pl.multiple_of(jnp.bitwise_xor(rank, away) * rows, rows), rows)
        block = product(left_ref[at, :], right).astype(jnp.bfloat16)
        to = send_ref if away & 1 else keep_ref
        to[away // 2, 0] = block


def grad_specs(count, rows, columns):
    return pl.BlockSpec((count // 2, 1, rows, columns), lambda step: (0, step, 0, 0))


def call(kernel, tiles, spot, arrays, specs, outs, out_specs, scratch):
    return pl.pallas_call(
        kernel,
        grid=(tiles,),
        in_specs=[pl.BlockSpec(memory_space=pltpu.SMEM)] + specs,
        out_specs=out_specs,
        out_shape=outs,
        scratch_shapes=scratch,
        compiler_params=pltpu.CompilerParams(
            dimension_semantics=("arbitrary",), vmem_limit_bytes=VMEM_LIMIT
        ),
        cost_estimate=SMALL_COST,
    )(spot, *arrays)


def bf16(*shape):
    return jax.ShapeDtypeStruct(shape, jnp.bfloat16)


def project(spot, rows_in, parts):
    arrays = [part.array for part in parts]
    tiles, share, columns = arrays[0].shape
    length, width = rows_in.shape

    def kernel(spot_ref, in_ref, *rest):
        refs, out_ref, scratch = rest[:-2], rest[-2], rest[-1]
        fill(scratch, spot_ref, parts, refs)
        out_ref[0] = product(in_ref[...], scratch[...]).astype(jnp.bfloat16)

    return call(
        kernel,
        tiles,
        spot,
        [rows_in] + arrays,
        [whole_spec(rows_in)] + [tile_spec(3, part.shape[1], columns) for part in arrays],
        bf16(tiles, length, columns),
        pl.BlockSpec((1, length, columns), lambda step: (step, 0, 0)),
        [pltpu.VMEM((width, columns), jnp.bfloat16)],
    )


def project_back(spot, rows_in, parts, which, width):
    arrays = [part.array for part in parts]
    columns = arrays[0].shape[-1]
    length = rows_in.shape[0]

    def kernel(spot_ref, in_ref, *rest):
        refs, out_ref, scratch = rest[:-2], rest[-2], rest[-1]
        fill_one(scratch, spot_ref, parts, refs, which)
        out_ref[...] = product_back(in_ref[...], scratch[...]).astype(jnp.bfloat16)

    return call(
        kernel,
        1,
        spot,
        [rows_in] + arrays,
        [whole_spec(rows_in)] + one_specs(parts, which),
        bf16(length, width),
        pl.BlockSpec((length, width), lambda step: (0, 0)),
        [pltpu.VMEM((width, columns), jnp.bfloat16)],
    )


def proj_grads(spot, grad_rows, mixed_rows, parts, which):
    arrays = [part.array for part in parts]
    share, columns = arrays[0].shape[-2:]
    length, width = grad_rows.shape
    count = width // share

    def kernel(spot_ref, grad_ref, mixed_ref, *rest):
        refs, (out_ref, keep_ref, send_ref, scratch, turned) = rest[:-5], rest[-5:]
        fill_one(scratch, spot_ref, parts, refs, which)
        turned[...] = jnp.transpose(grad_ref[...])
        out_ref[...] = product(grad_ref[...], scratch[...]).astype(jnp.bfloat16)
        put_grad(spot_ref, turned, mixed_ref[...], keep_ref, send_ref, share, count)

    half = bf16(count // 2, 1, share, columns)
    return call(
        kernel,
        1,
        spot,
        [grad_rows, mixed_rows] + arrays,
        [whole_spec(grad_rows), whole_spec(mixed_rows)] + one_specs(parts, which),
        (bf16(length, columns), half, half),
        (pl.BlockSpec((length, columns), lambda step: (0, 0)),)
        + (grad_specs(count, share, columns),) * 2,
        [pltpu.VMEM((width, columns), jnp.bfloat16), pltpu.VMEM((width, length), jnp.bfloat16)],
    )


def qkv_grads(spot, hidden, query_grads, block_grads, parts):
    arrays = [part.array for part in parts]
    tiles, share, columns = arrays[0].shape
    length, width = hidden.shape
    count = width // share

    seqs, rows = len(query_grads), query_grads[0].shape[1]

    def kernel(spot_ref, hid_ref, *rest):
        query_refs, block_refs, rest = rest[:seqs], rest[seqs : 2 * seqs], rest[2 * seqs :]
        refs, (out_ref, keep_ref, send_ref, scratch, total, turned, grad) = rest[:-7], rest[-7:]
        step = pl.program_id(0)
        fill(scratch, spot_ref, parts, refs)

        @pl.when(step == 0)
        def first():
            turned[...] = jnp.transpose(hid_ref[...])
            total[...] = jnp.zeros_like(total)
            for at, ref in enumerate(query_refs):
                grad[at * rows : (at + 1) * rows] = ref[0]

        @pl.when(step > 0)
        def later():
            for at, ref in enumerate(block_refs):
                grad[at * rows : (at + 1) * rows] = ref[0]

        total[...] += product_back(grad[...], scratch[...])
        put_grad(spot_ref, turned, grad[...], keep_ref, send_ref, share, count)

        @pl.when(step == tiles - 1)
        def finish():
            out_ref[...] = total[...].astype(jnp.bfloat16)

    half = bf16(count // 2, tiles, share, columns)
    return call(
        kernel,
        tiles,
        spot,
        [hidden, *query_grads] + [block_grads] * seqs + arrays,
        [whole_spec(hidden)]
        + [whole_spec(part) for part in query_grads]
        + [
            pl.BlockSpec(
                (1, rows, columns),
                functools.partial(lambda at, step: (2 * at + jnp.maximum(step - 1, 0), 0, 0), at),
            )
            for at in range(seqs)
        ]
        + [tile_spec(3, part.shape[1], columns) for part in arrays],
        (bf16(length, width), half, half),
        (pl.BlockSpec((length, width), lambda step: (0, 0)),)
        + (grad_specs(count, share, columns),) * 2,
        [
            pltpu.VMEM((width, columns), jnp.bfloat16),
            pltpu.VMEM((length, width), jnp.float32),
            pltpu.VMEM((width, length), jnp.bfloat16),
            pltpu.VMEM((length, columns), jnp.bfloat16),
        ],
    )


def gelu_parts(upward):
    squared = upward * upward
    bent = jnp.tanh(0.7978845608028654 * (upward + 0.044715 * (upward * squared)))
    activ = 0.5 * upward * (1.0 + bent)
    slope = 0.5 * (1.0 + bent) + 0.5 * upward * (1.0 - bent * bent) * (
        0.7978845608028654 * (1.0 + 3 * 0.044715 * squared)
    )
    return activ, slope


def feed_forward(spot, hidden, grad, up_parts, down_parts, columns):
    arrays = [part.array for part in up_parts + down_parts]
    share, units = arrays[0].shape
    tiles = units // columns
    length, width = hidden.shape
    count = width // share

    def kernel(spot_ref, hid_ref, grad_ref, *rest):
        refs, rest = rest[: len(arrays)], rest[len(arrays) :]
        out_ref, back_ref, up_keep, up_send, down_keep, down_send = rest[:6]
        up, down, out_sum, back_sum, hid_turned, grad_turned = rest[6:]
        step = pl.program_id(0)

        @pl.when(step == 0)
        def begin():
            hid_turned[...] = jnp.transpose(hid_ref[...])
            grad_turned[...] = jnp.transpose(grad_ref[...])
            out_sum[...] = jnp.zeros_like(out_sum)
            back_sum[...] = jnp.zeros_like(back_sum)

        fill(up, spot_ref, up_parts, refs[: len(up_parts)])
        fill(down, spot_ref, down_parts, refs[len(up_parts) :])
        activ, slope = gelu_parts(product(hid_ref[...], up[...]))
        activ = activ.astype(jnp.bfloat16)
        upward_grad = (product(grad_ref[...], down[...]) * slope).astype(jnp.bfloat16)
        out_sum[...] += product_back(activ, down[...])
        back_sum[...] += product_back(upward_grad, up[...])
        put_grad(spot_ref, grad_turned, activ, down_keep, down_send, share, count)
        put_grad(spot_ref, hid_turned, upward_grad, up_keep, up_send, share, count)

        @pl.when(step == tiles - 1)
        def finish():
            out_ref[...] = out_sum[...].astype(jnp.bfloat16)
            back_ref[...] = back_sum[...].astype(jnp.bfloat16)

    rows_spec = pl.BlockSpec((length, width), lambda step: (0, 0))
    wholes = [hidden, grad]
    return call(
        kernel,
        tiles,
        spot,
        wholes + arrays,
        [whole_spec(part) for part in wholes]
        + [tile_spec(2, part.shape[0], columns) for part in arrays],
        (bf16(length, width), bf16(length, width))
        + (bf16(count // 2, tiles, share, columns),) * 4,
        (rows_spec, rows_spec) + (grad_specs(count, share, columns),) * 4,
        [pltpu.VMEM((width, columns), jnp.bfloat16)] * 2
        + [pltpu.VMEM((length, width), jnp.float32)] * 2
        + [pltpu.VMEM((width, length), jnp.bfloat16)] * 2,
    )


def activate(seq, first, second):
    shape = first.shape
    tile = shape[1] // 2

    def kernel(first_ref, second_ref, out_ref):
        upward = first_ref[0].astype(jnp.float32) + second_ref[0].astype(jnp.float32)
        activ_grad = first_ref[1].astype(jnp.float32) + second_ref[1].astype(jnp.float32)
        activ, slope = gelu_parts(upward)
        out_ref[0] = activ.astype(jnp.bfloat16)
        out_ref[1] = (activ_grad * slope).astype(jnp.bfloat16)

    spec = pl.BlockSpec((2, tile, shape[2]), lambda step: (0, step, 0))
    return seq.mark(
        pl.pallas_call(
            kernel,
            grid=(2,),
            in_specs=[spec, spec],
            out_specs=spec,
            out_shape=bf16(*shape),
            compiler_params=pltpu.CompilerParams(
                dimension_semantics=("arbitrary",), vmem_limit_bytes=VMEM_LIMIT
            ),
            cost_estimate=SMALL_COST,
        )(seq.then(first), second)
    )


def middle_spread(seq, spot, modul, stream, branch, cot, count):
    seqs, length, width = stream.shape
    share = width // count

    def kernel(spot_ref, mod_ref, x_ref, one_ref, two_ref, cot_ref, *rest):
        outs, hid_all, grad_all = rest[:-2], rest[-2], rest[-1]
        middle = wide(x_ref) + mod_ref[0, 2:3] * (wide(one_ref) + wide(two_ref))
        norm, factor = normed(middle)
        hid_all[...] = (norm * (1.0 + mod_ref[0, 4:5]) + mod_ref[0, 3:4]).astype(jnp.bfloat16)
        grad_all[...] = (mod_ref[0, 5:6] * wide(cot_ref)).astype(jnp.bfloat16)
        for away, out in enumerate(outs):
            at = pl.multiple_of(jnp.bitwise_xor(spot_ref[0], away) * share, LANES)
            out[0, 0] = hid_all[:, pl.ds(at, share)]
            out[1, 0] = grad_all[:, pl.ds(at, share)]

    row_spec = pl.BlockSpec((1, length, width), lambda at: (at, 0, 0))
    made = pl.pallas_call(
        kernel,
        grid=(seqs,),
        in_specs=[
            pl.BlockSpec(memory_space=pltpu.SMEM),
            pl.BlockSpec((1,) + modul.shape[1:], lambda at: (at, 0, 0)),
        ]
        + [row_spec] * 4,
        out_specs=[pl.BlockSpec((2, 1, length, share), lambda at: (0, at, 0, 0))] * count,
        out_shape=[bf16(2, seqs, length, share)] * count,
        scratch_shapes=[pltpu.VMEM((length, width), jnp.bfloat16)] * 2,
        compiler_params=pltpu.CompilerParams(
            dimension_semantics=("arbitrary",), vmem_limit_bytes=VMEM_LIMIT
        ),
        cost_estimate=SMALL_COST,
    )(spot, modul, seq.then(stream), *branch, cot)
    seq.mark(made[0])
    return [part.reshape(2, -1, share) for part in made]


def lay_rows(spot, refs, scratch):
    rows = refs[0].shape[1]
    for away, ref in enumerate(refs):
        at = pl.multiple_of(jnp.bitwise_xor(spot[0], away) * rows, rows)
        scratch[:, pl.ds(at, rows), :] = ref[...]


def spread_up(seq, spot, features, up_shard, down_shard):
    count = len(features)
    rows, share = features[0].shape[1:]
    length = rows * count
    columns = up_shard.shape[1] // count

    def kernel(spot_ref, up_ref, down_ref, *rest):
        refs, (keep_ref, send_ref, rows_in) = rest[:count], rest[count:]

        @pl.when(pl.program_id(0) == 0)
        def begin():
            lay_rows(spot_ref, refs, rows_in)

        upward = product(rows_in[0], up_ref[...]).astype(jnp.bfloat16)
        activ_grad = product(rows_in[1], down_ref[...]).astype(jnp.bfloat16)
        odd = pl.program_id(0) % 2

        @pl.when(odd == 0)
        def keep():
            keep_ref[0, 0], keep_ref[0, 1] = upward, activ_grad

        @pl.when(odd != 0)
        def send():
            send_ref[0, 0], send_ref[0, 1] = upward, activ_grad

    shard_spec = pl.BlockSpec(
        (share, columns), lambda step, spot_ref: (0, jnp.bitwise_xor(spot_ref[0], step))
    )
    out_spec = pl.BlockSpec((1, 2, length, columns), lambda step, spot_ref: (step // 2, 0, 0, 0))
    out = bf16(count // 2, 2, length, columns)
    keep, send = pl.pallas_call(
        kernel,
        grid_spec=pltpu.PrefetchScalarGridSpec(
            num_scalar_prefetch=1,
            grid=(count,),
            in_specs=[shard_spec, shard_spec]
            + [pl.BlockSpec(part.shape, lambda step, spot_ref: (0, 0, 0)) for part in features],
            out_specs=[out_spec, out_spec],
            scratch_shapes=[pltpu.VMEM((2, length, share), jnp.bfloat16)],
        ),
        out_shape=[out, out],
        compiler_params=pltpu.CompilerParams(
            dimension_semantics=("arbitrary",), vmem_limit_bytes=VMEM_LIMIT
        ),
        cost_estimate=SMALL_COST,
    )(spot, up_shard, down_shard, seq.then(features[0]), *features[1:])
    seq.mark(keep)
    return keep, send


def spread_down(spot, features, blocks, up_shard, down_shard):
    count = len(blocks)
    length, columns = blocks[0].shape[1:]
    share, units = up_shard.shape
    rows = length // count

    def kernel(spot_ref, up_ref, down_ref, *rest):
        feature_refs, refs, rest = rest[:count], rest[count : 2 * count], rest[2 * count :]
        outs, (up_grad_ref, down_grad_ref, rows_in, sums) = rest[:count], rest[count:]
        lay_rows(spot_ref, feature_refs, rows_in)
        hid_turned, grad_turned = jnp.transpose(rows_in[0]), jnp.transpose(rows_in[1])
        out_sum = jnp.zeros((length, share), jnp.float32)
        back_sum = jnp.zeros((length, share), jnp.float32)
        for away, ref in enumerate(refs):
            place = jnp.bitwise_xor(spot_ref[0], away)
            at = pl.ds(pl.multiple_of(place * columns, columns), columns)
            activ, upward_grad = ref[0], ref[1]
            out_sum += product_back(activ, down_ref[:, at])
            back_sum += product_back(upward_grad, up_ref[:, at])
            up_grad_ref[place] = product(hid_turned, upward_grad).astype(jnp.bfloat16)
            down_grad_ref[place] = product(grad_turned, activ).astype(jnp.bfloat16)
        sums[0] = back_sum.astype(jnp.bfloat16)
        sums[1] = out_sum.astype(jnp.bfloat16)
        for away, out in enumerate(outs):
            at = pl.multiple_of(jnp.bitwise_xor(spot_ref[0], away) * rows, rows)
            out[...] = sums[:, pl.ds(at, rows), :]

    zeros = lambda step: (0, 0, 0)
    arrays = [up_shard, down_shard] + list(features) + list(blocks)
    *sums, up_grad, down_grad = call(
        kernel,
        1,
        spot,
        arrays,
        [whole_spec(part) for part in arrays],
        (bf16(2, rows, share),) * count + (bf16(count, share, columns),) * 2,
        (pl.BlockSpec((2, rows, share), zeros),) * count
        + (pl.BlockSpec((count, share, columns), zeros),) * 2,
        [pltpu.VMEM((2, length, share), jnp.bfloat16)] * 2,
    )
    return sums, up_grad, down_grad


def gather_features(seq, spot, pieces):
    count = len(pieces)
    rows, share = pieces[0].shape[1:]

    def kernel(spot_ref, *rest):
        refs, outs = rest[:count], rest[count:]
        for away, ref in enumerate(refs):
            at = pl.multiple_of(jnp.bitwise_xor(spot_ref[0], away) * share, LANES)
            for place, out in enumerate(outs):
                out[:, pl.ds(at, share)] = ref[place]

    out_spec = pl.BlockSpec((rows, share * count), lambda step: (0, 0))
    arrays = [seq.then(pieces[0])] + list(pieces[1:])
    made = call(
        kernel,
        1,
        spot,
        arrays,
        [whole_spec(part) for part in arrays],
        (bf16(rows, share * count),) * 2,
        (out_spec, out_spec),
        [],
    )
    seq.mark(made[0])
    return made


def row_kernel(seq, kernel, modul, rows_in, outs):
    seqs, length, width = rows_in[0].shape
    row_spec = pl.BlockSpec((1, length, width), lambda at: (at, 0, 0))
    sum_spec = pl.BlockSpec((1, 8, width), lambda at: (at, 0, 0))
    made = pl.pallas_call(
        kernel,
        grid=(seqs,),
        in_specs=[pl.BlockSpec((1,) + modul.shape[1:], lambda at: (at, 0, 0))]
        + [row_spec] * len(rows_in),
        out_specs=[sum_spec if kind is None else row_spec for kind in outs],
        out_shape=[
            jax.ShapeDtypeStruct((seqs, 8, width), jnp.float32)
            if kind is None
            else jax.ShapeDtypeStruct((seqs, length, width), kind)
            for kind in outs
        ],
        compiler_params=pltpu.CompilerParams(
            dimension_semantics=("arbitrary",), vmem_limit_bytes=VMEM_LIMIT
        ),
        cost_estimate=SMALL_COST,
    )(modul, seq.then(rows_in[0]), *rows_in[1:])
    seq.mark(made[0])
    return made


def wide(ref):
    return ref[0].astype(jnp.float32)


def put_sums(ref, rows):
    ref[0] = jnp.zeros_like(ref[0])
    for place, row in enumerate(rows):
        ref[0, place : place + 1] = jnp.sum(row, axis=0, keepdims=True)


def back_through(values, grad, scale_part):
    norm, factor = normed(values)
    inner = grad * (1.0 + scale_part)
    own = jnp.mean(inner, axis=-1, keepdims=True)
    along = jnp.mean(inner * norm, axis=-1, keepdims=True)
    return (inner - own - norm * along) * factor, norm


def first_hidden(seq, modul, stream):
    def kernel(mod_ref, x_ref, out_ref):
        norm, factor = normed(wide(x_ref))
        out_ref[0] = (norm * (1.0 + mod_ref[0, 1:2]) + mod_ref[0, 0:1]).astype(jnp.bfloat16)

    return row_kernel(seq, kernel, modul, [stream], [jnp.bfloat16])[0]


def middle_hidden(seq, modul, stream, branch, cot):
    def kernel(mod_ref, x_ref, one_ref, two_ref, cot_ref, hid_ref, grad_ref):
        middle = wide(x_ref) + mod_ref[0, 2:3] * (wide(one_ref) + wide(two_ref))
        norm, factor = normed(middle)
        hid_ref[0] = (norm * (1.0 + mod_ref[0, 4:5]) + mod_ref[0, 3:4]).astype(jnp.bfloat16)
        grad_ref[0] = (mod_ref[0, 5:6] * wide(cot_ref)).astype(jnp.bfloat16)

    return row_kernel(seq, kernel, modul, [stream, *branch, cot], [jnp.bfloat16, jnp.bfloat16])


def middle_grads(seq, modul, stream, branch, cot, hidden_grad):
    def kernel(mod_ref, x_ref, one_ref, two_ref, cot_ref, hid_ref, other_ref, mid_out, out, sums):
        branch_sum = wide(one_ref) + wide(two_ref)
        middle = wide(x_ref) + mod_ref[0, 2:3] * branch_sum
        grad = wide(hid_ref) + wide(other_ref)
        through, norm = back_through(middle, grad, mod_ref[0, 4:5])
        mid_grad = wide(cot_ref) + through
        mid_out[0] = mid_grad
        out[0] = (mod_ref[0, 2:3] * mid_grad).astype(jnp.bfloat16)
        put_sums(sums, [mid_grad * branch_sum, grad, grad * norm])

    return row_kernel(
        seq,
        kernel,
        modul,
        [stream, *branch, cot, *hidden_grad],
        [jnp.float32, jnp.bfloat16, None],
    )


def input_grads(seq, modul, stream, mid_grad, hidden_grad):
    def kernel(mod_ref, x_ref, mid_ref, hid_ref, other_ref, out, sums):
        grad = wide(hid_ref) + wide(other_ref)
        through, norm = back_through(wide(x_ref), grad, mod_ref[0, 1:2])
        out[0] = (mid_ref[0] + through).astype(jnp.bfloat16)
        put_sums(sums, [grad, grad * norm])

    return row_kernel(
        seq, kernel, modul, [stream, mid_grad, *hidden_grad], [jnp.bfloat16, None]
    )


def results(seq, modul, stream, branch, second, cot, real):
    def kernel(mod_ref, x_ref, one_ref, two_ref, three_ref, four_ref, cot_ref, out, sums):
        start = wide(x_ref)
        gated_one = mod_ref[0, 2:3] * (wide(one_ref) + wide(two_ref))
        middle = start + gated_one
        branch_two = wide(three_ref) + wide(four_ref)
        gated_two = mod_ref[0, 5:6] * branch_two
        result = middle + gated_two
        out[0] = result.astype(jnp.bfloat16)
        shown = lax.broadcasted_iota(jnp.int32, start.shape, 0) < real
        put_sums(
            sums,
            [wide(cot_ref) * branch_two]
            + [
                jnp.where(shown, member * member, 0.0)
                for member in (start, gated_one, middle, gated_two, result)
            ],
        )

    return row_kernel(
        seq, kernel, modul, [stream, *branch, *second, cot], [jnp.bfloat16, None]
    )


def head_lanes(shape, head):
    lane = lax.broadcasted_iota(jnp.int32, shape, len(shape) - 1)
    return (lane >= head * HD) & (lane < (head + 1) * HD)


def padding(shape, axis, image_rows, text_rows, real, count):
    place = lax.broadcasted_iota(jnp.int32, shape, axis) - image_rows * count
    hidden = (place >= real) & (place < text_rows)
    for other in range(1, count):
        hidden = hidden | (
            (place >= other * text_rows + real) & (place < (other + 1) * text_rows)
        )
    return hidden


def attention_specs(image, text):
    row = [
        pl.BlockSpec((1, rows, LANES), lambda seq, part: (seq, 0, part))
        for rows in (image.shape[1], text.shape[1])
    ]
    block = [
        pl.BlockSpec((2, 1, rows, LANES), lambda seq, part: (0, seq, 0, part))
        for rows in (image.shape[1], text.shape[1])
    ]
    return row, block


def joint(refs, index):
    return jnp.concatenate([ref[index] for ref in refs], axis=0)


def attend(image, text, image_blocks, text_blocks, real):
    seqs, image_rows, width = image.shape
    text_rows = text.shape[1]
    rows = image_rows + text_rows
    count = len(image_blocks)
    keys = rows * count

    def kernel(*rest):
        refs, (image_out, text_out) = rest[:-2], rest[-2:]
        queries = joint(refs[:2], 0)
        key_all = joint(refs[2:], (0, 0))
        value_all = joint(refs[2:], (1, 0))
        hidden = padding((1, keys), 1, image_rows, text_rows, real, count)
        result = jnp.zeros((rows, LANES), jnp.float32)
        for head in range(LANES // HD):
            mine = head_lanes((rows, LANES), head)
            scores = product_back(jnp.where(mine, queries, jnp.zeros_like(queries)), key_all)
            scores = jnp.where(hidden, -1e30, scores * 0.125)
            expd = jnp.exp(scores - jnp.max(scores, axis=1, keepdims=True))
            share = 1.0 / jnp.sum(expd, axis=1, keepdims=True)
            mixed = product((expd * share).astype(jnp.bfloat16), value_all)
            result = jnp.where(mine, mixed, result)
        image_out[0] = result[:image_rows].astype(jnp.bfloat16)
        text_out[0] = result[image_rows:].astype(jnp.bfloat16)

    row, block = attention_specs(image, text)
    return pl.pallas_call(
        kernel,
        grid=(seqs, width // LANES),
        in_specs=row + [block[0]] * count + [block[1]] * count,
        out_specs=row,
        out_shape=[bf16(*image.shape), bf16(*text.shape)],
        compiler_params=pltpu.CompilerParams(
            dimension_semantics=("arbitrary", "arbitrary"), vmem_limit_bytes=VMEM_LIMIT
        ),
        cost_estimate=SMALL_COST,
    )(image, text, *image_blocks, *text_blocks)


def attend_grads(queries_in, grads_in, image_blocks, text_blocks, real, seq):
    image, text = queries_in
    image_rows, width = image.shape[1:]
    text_rows = text.shape[1]
    rows = image_rows + text_rows
    count = len(image_blocks)
    keys = rows * count

    def kernel(*rest):
        refs, (image_out, text_out, keep_ref, send_ref) = rest[:-4], rest[-4:]
        queries = joint(refs[:2], 0)
        grads = joint(refs[2:4], 0)
        key_all = joint(refs[4:], (0, 0))
        value_all = joint(refs[4:], (1, 0))
        hidden = padding((keys, 1), 0, image_rows, text_rows, real, count)
        query_grad = jnp.zeros((rows, LANES), jnp.float32)
        key_grad = jnp.zeros((keys, LANES), jnp.float32)
        value_grad = jnp.zeros((keys, LANES), jnp.float32)
        for head in range(LANES // HD):
            mine = head_lanes((rows, LANES), head)
            own_query = jnp.where(mine, queries, jnp.zeros_like(queries))
            own_grad = jnp.where(mine, grads, jnp.zeros_like(grads))
            scores = product_back(key_all, own_query)
            scores = jnp.where(hidden, -1e30, scores * 0.125)
            expd = jnp.exp(scores - jnp.max(scores, axis=0, keepdims=True))
            probs = expd * (1.0 / jnp.sum(expd, axis=0, keepdims=True))
            prob_grad = product_back(value_all, own_grad)
            delta = jnp.sum(probs * prob_grad, axis=0, keepdims=True)
            score_grad = (probs * (prob_grad - delta)).astype(jnp.bfloat16)
            value_grad += product(probs.astype(jnp.bfloat16), own_grad)
            key_grad += product(score_grad, own_query)
            back = lax.dot_general(
                score_grad, key_all, (((0,), (0,)), ((), ())), preferred_element_type=jnp.float32
            )
            query_grad = jnp.where(mine, back, query_grad)
        query_grad = (query_grad * 0.125).astype(jnp.bfloat16)
        image_out[0] = query_grad[:image_rows]
        text_out[0] = query_grad[image_rows:]
        key_grad = (key_grad * 0.125).astype(jnp.bfloat16)
        value_grad = value_grad.astype(jnp.bfloat16)
        for away in range(count):
            to, place = (send_ref if away & 1 else keep_ref), away // 2
            at = slice(away * image_rows, (away + 1) * image_rows)
            to[place, 0, :image_rows], to[place, 1, :image_rows] = key_grad[at], value_grad[at]
            first = count * image_rows + away * text_rows
            at = slice(first, first + text_rows)
            to[place, 0, image_rows:], to[place, 1, image_rows:] = key_grad[at], value_grad[at]

    def row_spec(length, at):
        return pl.BlockSpec((1, length, LANES), lambda part: (at, 0, part))

    def block_spec(length):
        return pl.BlockSpec((2, 1, length, LANES), lambda part: (0, seq, 0, part))

    def owner_spec(length):
        return pl.BlockSpec((count // 2, 2, length, LANES), lambda part: (0, 0, 0, part))

    sizes = (image_rows, text_rows)
    return pl.pallas_call(
        kernel,
        grid=(width // LANES,),
        in_specs=[row_spec(length, seq) for length in sizes] * 2
        + [block_spec(image_rows)] * count
        + [block_spec(text_rows)] * count,
        out_specs=[row_spec(length, 0) for length in sizes]
        + [owner_spec(rows)] * 2,
        out_shape=[bf16(1, length, width) for length in sizes]
        + [bf16(count // 2, 2, rows, width)] * 2,
        compiler_params=pltpu.CompilerParams(
            dimension_semantics=("arbitrary",), vmem_limit_bytes=VMEM_LIMIT
        ),
        cost_estimate=SMALL_COST,
    )(image, text, *grads_in, *image_blocks, *text_blocks)


def on_device(
    image_tokens,
    text_tokens,
    text_owner,
    conditioning,
    slot_sequence,
    image_w_mod,
    image_b_mod,
    image_w_qkv,
    image_w_proj,
    image_w_up,
    image_w_down,
    text_w_mod,
    text_b_mod,
    text_w_qkv,
    text_w_proj,
    text_w_up,
    text_w_down,
    image_cotangent,
    text_cotangent,
):
    tok_rank = lax.axis_index("tok")
    rep_rank = lax.axis_index("rep")
    rep_count = lax.axis_size("rep")
    tok_count = lax.axis_size("tok")
    seqs, image_rows, width = image_tokens.shape
    text_real = text_cotangent.shape[1]
    text_rows = -(-text_real // 16) * 16
    slots = conditioning.shape[0]
    share = image_w_mod.shape[0]
    heads_width = image_w_qkv.shape[2]
    spot = jnp.stack([tok_rank, lax.rem(rep_rank, 2)]).astype(jnp.int32)

    turn = lambda weight: jnp.transpose(weight, (1, 0, 2))
    chips = Lane("tok", 2)
    proj_stack = jnp.stack([image_w_proj, text_w_proj])
    qkv_held = fetch(turn(image_w_qkv), 1, chips)
    qkv_own, text_own = flip(turn(image_w_qkv), "tok", 1), flip(turn(text_w_qkv), "tok", 1)
    image_qkv_parts, unused = share_out(turn(image_w_qkv), qkv_own, qkv_held)

    picker = (slot_sequence[:, None] == jnp.arange(slots, dtype=jnp.int32)[None, :]).astype(
        jnp.float32
    )
    cond_slots = jnp.dot(picker, conditioning, precision=exact_mode)
    activ_all = jax.nn.silu(cond_slots).astype(jnp.bfloat16)
    activ_group = lax.dynamic_slice_in_dim(activ_all, rep_rank * seqs, seqs, axis=0)
    activ_share = lax.dynamic_slice_in_dim(activ_group, tok_rank * share, share, axis=1)
    both_mod = tok_total(
        jnp.stack(
            [
                jnp.einsum("sd,dke->ske", activ_share, weight, preferred_element_type=jnp.float32)
                for weight in (image_w_mod, text_w_mod)
            ]
        ),
        *qkv_held.values(),
    )
    image_mod = both_mod[0] + image_b_mod.astype(jnp.float32)[None]
    text_mod = both_mod[1] + text_b_mod.astype(jnp.float32)[None]

    text_held = fetch(turn(text_w_qkv), 1, chips, (both_mod,))

    owned = (text_owner == tok_rank).astype(jnp.float32)
    total_text = text_owner.shape[1]
    before = jnp.dot(
        owned,
        jnp.triu(jnp.ones((total_text, total_text), jnp.float32), 1),
        precision=exact_mode,
    )
    chosen = (
        (before[:, None, :] == jnp.arange(text_rows, dtype=jnp.float32)[None, :, None])
        & (owned[:, None, :] > 0.5)
    ).astype(jnp.bfloat16)
    text_input = jnp.einsum(
        "srt,std->srd", chosen, text_tokens, preferred_element_type=jnp.float32
    ).astype(jnp.bfloat16)
    text_cot = jnp.pad(text_cotangent, ((0, 0), (0, text_rows - text_real), (0, 0)))

    seq = Sequence()
    flat = lambda values: values.reshape(-1, values.shape[-1])
    by_seq = lambda values: values.reshape(values.shape[:-2] + (seqs, -1, values.shape[-1]))
    both = lambda pair: tuple(by_seq(part) for part in pair)
    heads = lambda partial: both(head_pair(partial))

    image_hid_one = flat(first_hidden(seq, image_mod, image_tokens))
    image_qkv = seq.mark(
        project(spot, after(seq.then(image_hid_one), *text_held.values()), image_qkv_parts)
    )
    image_blocks = gather_blocks(by_seq(image_qkv[1:]), chips)
    text_qkv_parts, unused = share_out(turn(text_w_qkv), text_own, text_held, (image_qkv,))
    text_hid_one = flat(first_hidden(seq, text_mod, text_input))
    text_qkv = project(spot, seq.then(text_hid_one), text_qkv_parts)
    text_blocks = gather_blocks(by_seq(text_qkv[1:]), chips)
    cores = Lane("tok", 1)
    owned_shards = [
        cores.flip(after(weight, image_qkv), 1)
        for weight in (image_w_up, image_w_down, proj_stack)
    ]
    up_own, down_own, proj_own = owned_shards
    seq.mark(text_qkv, *owned_shards)
    proj_parts, unused = share_out(proj_stack, proj_own, fetch(proj_stack, 0, chips, (text_qkv,)))
    up_held = fetch(image_w_up, 0, chips)
    down_held = fetch(image_w_down, 0, chips)
    image_up_parts, up_swapped = share_out(image_w_up, up_own, up_held)
    image_down_parts, down_swapped = share_out(image_w_down, down_own, down_held)
    image_query, text_query = by_seq(image_qkv[0]), by_seq(text_qkv[0])
    image_mix, text_mix = attend(
        image_query, seq.then(text_query), image_blocks, text_blocks, text_real
    )
    seq.mark(image_mix, *up_held.values())
    image_mixed, text_mixed = flat(image_mix), flat(text_mix)
    text_out = seq.mark(project_back(spot, seq.then(text_mixed), proj_parts, 1, width))
    text_branch = heads(text_out)
    image_out = project_back(spot, seq.then(image_mixed), proj_parts, 0, width)
    seq.mark(image_out, *down_held.values())
    image_branch = heads(image_out)

    text_features = exchange(
        middle_spread(seq, spot, text_mod, text_input, text_branch, text_cot, tok_count)
    )
    image_hid_two, image_db_two = middle_hidden(
        seq, image_mod, image_tokens, image_branch, image_cotangent
    )
    seq.mark(image_hid_two, *up_swapped, *down_swapped)
    text_keep, text_send = spread_up(seq, spot, text_features, text_w_up, text_w_down)
    text_pieces = core_sums(seq, text_keep, flip(text_send, "tok", 1))
    text_stays, text_came = chip_moves(seq, text_pieces, chips)
    image_part, image_back, image_up_keep, image_up_send, image_down_keep, image_down_send = (
        feed_forward(
            spot,
            seq.then(flat(image_hid_two)),
            flat(image_db_two),
            image_up_parts,
            image_down_parts,
            heads_width,
        )
    )
    seq.mark(image_back)
    shape = (2,) + text_keep.shape[2:]
    text_act = activate(seq, text_stays.reshape(shape), text_came.reshape(shape))
    text_active = gather_blocks(text_act, chips)
    image_hid_grad = heads(after(image_back, text_act))
    image_down_send = after(image_down_send, text_act)
    image_up_send = after(image_up_send, text_act)
    chips = Lane("tok", 3)
    image_down_pieces = core_sums(seq, image_down_keep, flip(image_down_send, "tok", 1))
    image_down_pair = chip_moves(seq, image_down_pieces, chips)
    image_up_pieces = core_sums(seq, image_up_keep, flip(image_up_send, "tok", 1))
    image_up_pair = chip_moves(seq, image_up_pieces, chips)
    text_sums, text_up_grad, text_down_grad = spread_down(
        spot,
        [seq.then(text_features[0])] + text_features[1:],
        text_active,
        text_w_up,
        text_w_down,
    )
    seq.mark(text_sums[0])
    text_back_pieces = exchange(text_sums)
    line = Line(seq)
    if line.on_line:
        for whole in (text_down_grad, text_up_grad):
            for place in range(2):
                line.add(flat(whole.reshape(2, -1, share, whole.shape[-1])[place]))
        text_totals = None
    else:
        text_totals = [lax.psum(part, "rep") for part in (text_down_grad, text_up_grad)]

    image_mid_grad, image_db_one, image_mid_sums = middle_grads(
        seq, image_mod, image_tokens, image_branch, image_cotangent, image_hid_grad
    )
    text_back, text_part = gather_features(seq, spot, text_back_pieces)
    text_hid_grad = heads(text_back)
    image_mixed_grad, image_proj_keep, image_proj_send = proj_grads(
        spot, seq.then(flat(image_db_one)), image_mixed, proj_parts, 0
    )
    seq.mark(image_mixed_grad)
    text_mid_grad, text_db_one, text_mid_sums = middle_grads(
        seq, text_mod, text_input, text_branch, text_cot, text_hid_grad
    )
    text_mixed_grad, text_proj_keep, text_proj_send = proj_grads(
        spot, seq.then(flat(text_db_one)), text_mixed, proj_parts, 1
    )
    seq.mark(text_mixed_grad)
    line.step()
    proj_pieces = [
        core_sums(seq, keep, flip(send, "tok", 1))
        for keep, send in ((image_proj_keep, image_proj_send), (text_proj_keep, text_proj_send))
    ]
    made_grads, moved_grads = [], []
    mix_grads = (by_seq(image_mixed_grad), by_seq(text_mixed_grad))
    for at in range(seqs):
        made = attend_grads(
            (image_query, text_query),
            (seq.then(mix_grads[0]), mix_grads[1]),
            image_blocks,
            text_blocks,
            text_real,
            at,
        )
        made_grads.append(made)
        seq.mark(made[0])
        if at == 0 or at == seqs - 1:
            for part in add_blocks(seq, *(image_up_pair if at else image_down_pair), 2):
                line.add(part)
        if at == 0 and seqs == 1:
            for part in add_blocks(seq, *image_up_pair, 2):
                line.add(part)
        line.step()
        moved_grads.append(flip(after(made[3], *seq.last), "tok", 1))
    block_move = chip_moves(
        seq, core_sums_joined(seq, [made[2] for made in made_grads], moved_grads), chips
    )
    line.step()
    tail = Line(seq)
    block_grads = add_split(seq, *block_move, 2 * seqs, image_rows)
    proj_pairs = [chip_moves(seq, pieces, chips) for pieces in proj_pieces]
    image_in_part, image_qkv_keep, image_qkv_send = qkv_grads(
        spot,
        seq.then(image_hid_one),
        [made[0] for made in made_grads],
        block_grads[0],
        image_qkv_parts,
    )
    seq.mark(image_in_part)
    text_in_part, text_qkv_keep, text_qkv_send = qkv_grads(
        spot,
        seq.then(text_hid_one),
        [made[1] for made in made_grads],
        block_grads[1],
        text_qkv_parts,
    )
    seq.mark(text_in_part)
    qkv_pairs = [
        chip_moves(seq, core_sums(seq, keep, flip(send, "tok", 1)), chips)
        for keep, send in ((image_qkv_keep, image_qkv_send), (text_qkv_keep, text_qkv_send))
    ]
    line.step()
    image_in_grad = heads(image_in_part)
    text_in_grad = heads(text_in_part)
    image_proj_share, text_proj_share = [add_blocks(seq, *pair, 1)[0] for pair in proj_pairs]
    line.step()
    image_grad, image_in_sums = input_grads(
        seq, image_mod, image_tokens, image_mid_grad, image_in_grad
    )
    text_grad, text_in_sums = input_grads(
        seq, text_mod, text_input, text_mid_grad, text_in_grad
    )
    text_second = heads(after(text_part, image_in_sums))
    image_second = heads(after(image_part, image_in_sums))
    image_qkv_shares = add_blocks(seq, *qkv_pairs[0], 3)
    line.step()
    text_qkv_shares = add_blocks(seq, *qkv_pairs[1], 3)
    line.step()
    for part in [image_proj_share, text_proj_share, *image_qkv_shares, *text_qkv_shares]:
        tail.add(part)
    text_result, text_out_sums = results(
        seq, text_mod, text_input, text_branch, text_second, text_cot, text_real
    )
    image_result, image_out_sums = results(
        seq, image_mod, image_tokens, image_branch, image_second, image_cotangent, image_rows
    )
    line.step()
    line_sums = line.finish()
    tail_sums = tail.finish()
    columns_of = lambda parts: jnp.concatenate(
        [
            column.astype(jnp.float32)
            for part in parts
            for column in part.reshape(-1, share, part.shape[-1])
        ],
        axis=1,
    )
    if text_totals is None:
        text_totals = [jnp.concatenate(line_sums[at : at + 2]) for at in (0, 2)]
        text_totals = [part.reshape(tok_count, share, -1) for part in text_totals]
        line_sums = line_sums[4:]
    text_down_sum, text_up_sum = [columns_of([part]) for part in text_totals]
    image_down_sum, image_up_sum = columns_of(line_sums[:2]), columns_of(line_sums[2:])
    image_proj_sum, text_proj_sum = tail_sums[:2]
    image_qkv_sum = jnp.stack(tail_sums[2:5], axis=1)
    text_qkv_sum = jnp.stack(tail_sums[5:], axis=1)

    early = jnp.stack(
        [
            jnp.concatenate([mid_sums[:, :3], out_sums[:, :1]], axis=1)
            for mid_sums, out_sums in (
                (image_mid_sums, image_out_sums),
                (text_mid_sums, text_out_sums),
            )
        ]
    )
    late = jnp.stack([image_in_sums[:, :2], text_in_sums[:, :2]])
    squares = jnp.concatenate(
        [jnp.sum(out_sums[:, 1:6], axis=(0, 2)) for out_sums in (image_out_sums, text_out_sums)]
    )
    square_row = jnp.pad(squares, (0, width - 10))[None]
    all_sums = jnp.concatenate(
        [early.reshape(-1, width), late.reshape(-1, width), square_row], axis=0
    )
    all_sums = rep_gather(tok_total(all_sums))
    square_total = jnp.sum(all_sums[:, -1, :10], axis=0)
    early_table = jnp.moveaxis(
        all_sums[:, : 8 * seqs].reshape(rep_count, 2, seqs, 4, width), 0, 1
    ).reshape(2, slots, 4, width)
    late_table = jnp.moveaxis(
        all_sums[:, 8 * seqs : -1].reshape(rep_count, 2, seqs, 2, width), 0, 1
    ).reshape(2, slots, 2, width)
    mod_sum = jnp.concatenate([late_table, early_table], axis=2)

    activ_rows = lax.dynamic_slice_in_dim(activ_all, tok_rank * share, share, axis=1).astype(
        jnp.float32
    )
    image_g_mod = jnp.einsum("sd,ske->dke", activ_rows, mod_sum[0], precision=exact_mode)
    text_g_mod = jnp.einsum("sd,ske->dke", activ_rows, mod_sum[1], precision=exact_mode)
    image_g_bmod = jnp.sum(mod_sum[0], axis=0)
    text_g_bmod = jnp.sum(mod_sum[1], axis=0)
    activ_grad = jnp.einsum(
        "ske,dke->sd", mod_sum[0], image_w_mod.astype(jnp.float32), precision=exact_mode
    ) + jnp.einsum("ske,dke->sd", mod_sum[1], text_w_mod.astype(jnp.float32), precision=exact_mode)
    cond_rows = lax.dynamic_slice_in_dim(cond_slots, tok_rank * share, share, axis=1)
    unused_value, silu_back = jax.vjp(jax.nn.silu, cond_rows)
    slot_grad = silu_back(activ_grad)[0]
    cond_grad = jnp.dot(jnp.transpose(picker), slot_grad, precision=exact_mode)
    image_count = float(slots * image_rows * tok_count * width)
    text_count = float(slots * text_real * tok_count * width)
    counts = jnp.concatenate(
        [jnp.full((5,), image_count, jnp.float32), jnp.full((5,), text_count, jnp.float32)]
    )
    stream_rms = jnp.sqrt(square_total / counts)
    return (
        image_result,
        text_result[:, :text_real],
        image_grad,
        text_grad[:, :text_real],
        cond_grad,
        image_g_mod,
        image_g_bmod,
        image_qkv_sum,
        image_proj_sum,
        image_up_sum,
        image_down_sum,
        text_g_mod,
        text_g_bmod,
        text_qkv_sum,
        text_proj_sum,
        text_up_sum,
        text_down_sum,
        stream_rms,
    )


def solution(mesh):
    in_specs = (
        P("rep", "tok", None),
        P("rep", None, None),
        P("rep", None),
        P(),
        P(),
        P("tok", None, None),
        P(),
        P("tok", None, "head"),
        P("tok", "head"),
        P("tok", "head"),
        P("tok", "head"),
        P("tok", None, None),
        P(),
        P("tok", None, "head"),
        P("tok", "head"),
        P("tok", "head"),
        P("tok", "head"),
        P("rep", "tok", None),
        P("rep", "tok", None),
    )
    out_specs = (
        P("rep", "tok", None),
        P("rep", "tok", None),
        P("rep", "tok", None),
        P("rep", "tok", None),
        P(None, "tok"),
        P("tok", None, None),
        P(),
        P("tok", None, "head"),
        P("tok", "head"),
        P("tok", "head"),
        P("tok", "head"),
        P("tok", None, None),
        P(),
        P("tok", None, "head"),
        P("tok", "head"),
        P("tok", "head"),
        P("tok", "head"),
        P(),
    )
    return jax.shard_map(
        on_device, mesh=mesh, in_specs=in_specs, out_specs=out_specs, check_vma=False
    )
```

```python
import functools

import jax
import jax.numpy as jnp
from jax import lax
from jax.experimental import pallas as pl
from jax.experimental.pallas import tpu as pltpu
from jax.sharding import PartitionSpec as P

HD = 64
LANES = 128
VMEM_LIMIT = 60 * 1024 * 1024
SMALL_COST = pl.CostEstimate(flops=1024, bytes_accessed=1024, transcendentals=0)

exact_mode = lax.Precision.HIGHEST


def normed(values):
    centered = values - jnp.mean(values, axis=-1, keepdims=True)
    scale = lax.rsqrt(jnp.mean(centered * centered, axis=-1, keepdims=True) + 1e-06)
    return centered * scale, scale


def flip(values, axis, bit):
    return lax.ppermute(
        values, axis, [(place, place ^ bit) for place in range(lax.axis_size(axis))]
    )


def head_pair(partial):
    if lax.axis_size("head") != 2:
        return lax.psum(partial, "head"), jnp.zeros_like(partial)
    return partial, flip(partial, "head", 1)


def after(values, *needed):
    return lax.optimization_barrier((values, *needed))[0]


class Sequence:
    def __init__(self):
        self.last = None

    def then(self, values):
        return values if self.last is None else after(values, *self.last)

    def mark(self, output, *moves):
        self.last = (output, *moves)
        return output


class Lane:
    def __init__(self, axis, depth):
        self.axis, self.depth, self.over = axis, depth, []

    def flip(self, values, bit):
        if len(self.over) >= self.depth:
            values = after(values, self.over[-self.depth])
        moved = flip(values, self.axis, bit)
        self.over.append(moved)
        return moved


class Part:
    def __init__(self, away, half, array):
        self.away, self.half, self.array = away, half, array


def fetch(weight, axis, lane, needed=()):
    parity = lax.rem(lax.axis_index("rep"), 2)
    size = weight.shape[axis] // 2
    held = {0: lax.dynamic_slice_in_dim(weight, parity * size, size, axis=axis)}
    if needed:
        held[0] = after(held[0], *needed)
    bit = lax.axis_size("tok") // 2
    while bit > 1:
        for away, array in list(held.items()):
            held[away ^ bit] = lane.flip(array, bit)
        bit //= 2
    del held[0]
    return held


def share_out(weight, own, held, needed=(), first=()):
    parts = []
    for away, array in held.items():
        leaving = after(array, *first) if first else array
        parts += [Part(away, 0, array), Part(away, 1, flip(leaving, "rep", 1))]
    others = [
        Part(
            part.away ^ 1,
            part.half,
            flip(after(part.array, *needed) if needed else part.array, "tok", 1),
        )
        for part in parts
    ]
    swapped = [part.array for part in parts if part.half == 1]
    return [Part(0, None, weight)] + parts + [Part(1, None, own)] + others, swapped


def gather_blocks(values, lane, needed=()):
    pieces = {0: values}
    bit = lax.axis_size("tok") // 2
    while bit > 0:
        for away, part in list(pieces.items()):
            if bit > 1:
                pieces[away ^ bit] = lane.flip(part, bit)
            else:
                part = after(part, *needed) if away and needed else part
                pieces[away ^ bit] = flip(part, "tok", bit)
        bit //= 2
    return [pieces[away] for away in range(len(pieces))]


def add_blocks(seq, first, second, outputs, kind=jnp.bfloat16):
    width = first.shape[-1]
    flat = lambda values: values.reshape(outputs, -1, width)
    first, second = flat(seq.then(first)), flat(second)
    rows = first.shape[1]
    tile = rows // 2

    def kernel(first_ref, second_ref, *out_refs):
        for place, out_ref in enumerate(out_refs):
            out_ref[...] = (
                first_ref[place].astype(jnp.float32) + second_ref[place].astype(jnp.float32)
            ).astype(kind)

    in_spec = pl.BlockSpec((outputs, tile, width), lambda step: (0, step, 0))
    sums = pl.pallas_call(
        kernel,
        grid=(2,),
        in_specs=[in_spec, in_spec],
        out_specs=[pl.BlockSpec((tile, width), lambda step: (step, 0))] * outputs,
        out_shape=[jax.ShapeDtypeStruct((rows, width), kind)] * outputs,
        compiler_params=pltpu.CompilerParams(
            dimension_semantics=("arbitrary",), vmem_limit_bytes=VMEM_LIMIT
        ),
        cost_estimate=SMALL_COST,
    )(first, second)
    seq.mark(sums[0])
    return sums


def core_sums(seq, keep, moved):
    sums = add_blocks(seq, keep, moved, keep.shape[0])
    return {2 * place: part for place, part in enumerate(sums)}


def core_sums_joined(seq, keeps, moved):
    pieces, pair, rows, width = keeps[0].shape
    pairs = len(keeps)

    def kernel(*refs):
        for at in range(pairs):
            for place in range(pieces):
                refs[2 * pairs + place][at] = (
                    refs[at][place].astype(jnp.float32)
                    + refs[pairs + at][place].astype(jnp.float32)
                ).astype(jnp.bfloat16)

    spec = pl.BlockSpec((pieces, 1, rows, width), lambda step: (0, step, 0, 0))
    sums = pl.pallas_call(
        kernel,
        grid=(pair,),
        in_specs=[spec] * (2 * pairs),
        out_specs=[pl.BlockSpec((pairs, 1, rows, width), lambda step: (0, step, 0, 0))] * pieces,
        out_shape=[bf16(pairs, pair, rows, width)] * pieces,
        compiler_params=pltpu.CompilerParams(
            dimension_semantics=("arbitrary",), vmem_limit_bytes=VMEM_LIMIT
        ),
        cost_estimate=SMALL_COST,
    )(seq.then(keeps[0]), *keeps[1:], *moved)
    seq.mark(sums[0])
    return {2 * place: part.reshape(-1, width) for place, part in enumerate(sums)}


def add_split(seq, first, second, groups, top):
    width = first.shape[-1]
    first, second = seq.then(first).reshape(groups, -1, width), second.reshape(groups, -1, width)
    rows = first.shape[1]

    def kernel(first_ref, second_ref, top_ref, bottom_ref):
        total = (first_ref[0].astype(jnp.float32) + second_ref[0].astype(jnp.float32)).astype(
            jnp.bfloat16
        )
        top_ref[0], bottom_ref[0] = total[:top], total[top:]

    spec = lambda length: pl.BlockSpec((1, length, width), lambda step: (step, 0, 0))
    parts = pl.pallas_call(
        kernel,
        grid=(groups,),
        in_specs=[spec(rows), spec(rows)],
        out_specs=[spec(top), spec(rows - top)],
        out_shape=[bf16(groups, top, width), bf16(groups, rows - top, width)],
        compiler_params=pltpu.CompilerParams(
            dimension_semantics=("arbitrary",), vmem_limit_bytes=VMEM_LIMIT
        ),
        cost_estimate=SMALL_COST,
    )(first, second)
    seq.mark(parts[0])
    return parts


def chip_moves(seq, pieces, lane):
    bit = 2
    while 2 * bit < lax.axis_size("tok"):
        pieces = {
            away: add_blocks(seq, part, lane.flip(pieces[away | bit], bit), 1)[0]
            for away, part in pieces.items()
            if not away & bit
        }
        bit *= 2
    if bit >= lax.axis_size("tok"):
        return pieces[0], jnp.zeros_like(pieces[0])
    return pieces[0], lane.flip(pieces[bit], bit)


def exchange(pieces):
    return [pieces[0]] + [flip(part, "tok", 1 + place) for place, part in enumerate(pieces[1:])]


class Line:
    def __init__(self, seq):
        self.seq = seq
        self.on_line = lax.axis_size("rep") == 4
        rank = lax.axis_index("rep")
        self.inner = ((rank == 1) | (rank == 2)).astype(jnp.int32).reshape(1)
        self.chunks, self.totals, self.outward = [], {}, {}
        self.place = 0
        self.came, self.pair, self.over = None, None, None

    def outer(self, load, pairs):
        return lax.ppermute(load, "rep", pairs)

    def add(self, chunk):
        self.chunks.append(chunk)
        if self.on_line and len(self.chunks) == 1:
            self.came = self.outer(chunk, [(0, 1), (3, 2)])

    def step(self, final=False):
        if not self.on_line or not self.chunks or self.place > len(self.chunks):
            return
        k, seq = self.place, self.seq
        count = len(self.chunks)
        has_pair, has_total, has_next = k < count, 1 <= k <= count, k + 1 < count
        shape = self.chunks[0].shape
        ins, names = [], []
        if has_pair:
            ins += [self.chunks[k], self.came]
        if has_total:
            ins += [self.pair, self.over]
        if has_total and has_next:
            ins += [self.chunks[k + 1]]
        ins[0] = seq.then(ins[0])
        outs = int(has_pair) + int(has_total) * (2 if has_next else 1)
        tile = shape[0] // 2

        def kernel(inner_ref, *refs):
            ins_left, outs_left = list(refs[: len(ins)]), list(refs[len(ins) :])

            def plus(one, two):
                return (one[...].astype(jnp.float32) + two[...].astype(jnp.float32)).astype(
                    jnp.bfloat16
                )

            if has_pair:
                outs_left.pop(0)[...] = plus(ins_left.pop(0), ins_left.pop(0))
            if has_total:
                total = plus(ins_left.pop(0), ins_left.pop(0))
                outs_left.pop(0)[...] = total
                if has_next:
                    load_ref, next_ref = outs_left.pop(0), ins_left.pop(0)

                    @pl.when(inner_ref[0] == 1)
                    def send_total():
                        load_ref[...] = total

                    @pl.when(inner_ref[0] != 1)
                    def send_chunk():
                        load_ref[...] = next_ref[...]

        spec = pl.BlockSpec((tile, shape[1]), lambda step: (step, 0))
        made = list(
            pl.pallas_call(
                kernel,
                grid=(2,),
                in_specs=[pl.BlockSpec(memory_space=pltpu.SMEM)] + [spec] * len(ins),
                out_specs=[spec] * outs,
                out_shape=[bf16(*shape)] * outs,
                compiler_params=pltpu.CompilerParams(
                    dimension_semantics=("arbitrary",), vmem_limit_bytes=VMEM_LIMIT
                ),
                cost_estimate=SMALL_COST,
            )(self.inner, *ins)
        )
        seq.mark(made[0])
        if has_pair:
            self.pair = made.pop(0)
            self.over = lax.ppermute(self.pair, "rep", [(1, 2), (2, 1)])
        if has_total:
            self.totals[k - 1] = made.pop(0)
            if has_next:
                self.came = self.outer(made.pop(0), [(0, 1), (1, 0), (2, 3), (3, 2)])
                self.outward[k - 1] = self.came
            else:
                self.outward[k - 1] = self.outer(self.totals[k - 1], [(1, 0), (2, 3)])
        elif has_next:
            self.came = self.outer(self.chunks[k + 1], [(0, 1), (3, 2)])
        self.place += 1

    def finish(self):
        if not self.on_line:
            return [lax.psum(chunk, "rep").astype(jnp.float32) for chunk in self.chunks]
        while self.place <= len(self.chunks):
            self.step()
        return [
            jnp.where(self.inner[0] == 1, self.totals[k], self.outward[k]).astype(jnp.float32)
            for k in range(len(self.chunks))
        ]


def tok_total(values, *needed):
    bit = 1
    while bit < lax.axis_size("tok"):
        if bit == 2 and needed:
            values = after(values, *needed)
        values = values + flip(values, "tok", bit)
        bit *= 2
    return values


def rep_gather(values, needed):
    count = lax.axis_size("rep")
    rank = lax.axis_index("rep")
    pieces = values[None]
    bit = 1
    while bit < count:
        moved = flip(pieces, "rep", bit)
        if needed:
            moved = after(moved, needed.pop(0))
        pieces = jnp.concatenate([pieces, moved], axis=0)
        bit *= 2
    return jnp.stack(
        [
            lax.dynamic_index_in_dim(pieces, jnp.bitwise_xor(rank, place), 0, keepdims=False)
            for place in range(count)
        ]
    )


def product(left, right):
    return jnp.dot(left, right, preferred_element_type=jnp.float32)


def product_back(left, right):
    return lax.dot_general(
        left, right, (((1,), (1,)), ((), ())), preferred_element_type=jnp.float32
    )


def tile_spec(rank, rows, columns):
    if rank == 3:
        return pl.BlockSpec((1, rows, columns), lambda step: (step, 0, 0))
    return pl.BlockSpec((rows, columns), lambda step: (0, step))


def whole_spec(array):
    zeros = (0,) * array.ndim
    return pl.BlockSpec(array.shape, lambda step: zeros, pipeline_mode=pl.Buffered(1))


def tile_of(ref):
    return ref[0] if len(ref.shape) == 3 else ref[...]


def fill(scratch, spot, parts, refs):
    rank, parity = spot[0], spot[1]
    share = parts[0].array.shape[-2]
    for part, ref in zip(parts, refs, strict=True):
        rows = part.array.shape[-2]
        start = jnp.bitwise_xor(rank, part.away) * share
        if part.half is not None:
            start = start + jnp.bitwise_xor(parity, part.half) * rows
        scratch[pl.ds(pl.multiple_of(start, rows), rows), :] = tile_of(ref)


def fill_one(scratch, spot, parts, refs, which):
    rank, parity = spot[0], spot[1]
    share = parts[0].array.shape[-2]
    for part, ref in zip(parts, refs, strict=True):
        start = pl.multiple_of(jnp.bitwise_xor(rank, part.away) * share, share)

        def lay(start=start, ref=ref):
            scratch[pl.ds(start, share), :] = tile_of(ref)

        if part.half is None:
            lay()
        else:
            pl.when(jnp.bitwise_xor(parity, part.half) == which)(lay)


def one_specs(parts, which):
    return [
        pl.BlockSpec(
            (1,) + part.array.shape[1:],
            functools.partial(lambda at, step: (at, 0, 0), which if part.half is None else 0),
        )
        for part in parts
    ]


def put_grad(spot, left_ref, right, keep_ref, send_ref, rows, count):
    rank = spot[0]
    for away in range(count):
        at = pl.ds(pl.multiple_of(jnp.bitwise_xor(rank, away) * rows, rows), rows)
        block = product(left_ref[at, :], right).astype(jnp.bfloat16)
        to = send_ref if away & 1 else keep_ref
        to[away // 2, 0] = block


def grad_specs(count, rows, columns):
    return pl.BlockSpec((count // 2, 1, rows, columns), lambda step: (0, step, 0, 0))


def call(kernel, tiles, spot, arrays, specs, outs, out_specs, scratch):
    return pl.pallas_call(
        kernel,
        grid=(tiles,),
        in_specs=[pl.BlockSpec(memory_space=pltpu.SMEM)] + specs,
        out_specs=out_specs,
        out_shape=outs,
        scratch_shapes=scratch,
        compiler_params=pltpu.CompilerParams(
            dimension_semantics=("arbitrary",), vmem_limit_bytes=VMEM_LIMIT
        ),
        cost_estimate=SMALL_COST,
    )(spot, *arrays)


def bf16(*shape):
    return jax.ShapeDtypeStruct(shape, jnp.bfloat16)


def project(spot, rows_in, parts):
    arrays = [part.array for part in parts]
    tiles, share, columns = arrays[0].shape
    length, width = rows_in.shape

    def kernel(spot_ref, in_ref, *rest):
        refs, out_ref, scratch = rest[:-2], rest[-2], rest[-1]
        fill(scratch, spot_ref, parts, refs)
        out_ref[0] = product(in_ref[...], scratch[...]).astype(jnp.bfloat16)

    return call(
        kernel,
        tiles,
        spot,
        [rows_in] + arrays,
        [whole_spec(rows_in)] + [tile_spec(3, part.shape[1], columns) for part in arrays],
        bf16(tiles, length, columns),
        pl.BlockSpec((1, length, columns), lambda step: (step, 0, 0)),
        [pltpu.VMEM((width, columns), jnp.bfloat16)],
    )


def project_back(spot, rows_in, parts, which, width):
    arrays = [part.array for part in parts]
    columns = arrays[0].shape[-1]
    length = rows_in.shape[0]

    def kernel(spot_ref, in_ref, *rest):
        refs, out_ref, scratch = rest[:-2], rest[-2], rest[-1]
        fill_one(scratch, spot_ref, parts, refs, which)
        out_ref[...] = product_back(in_ref[...], scratch[...]).astype(jnp.bfloat16)

    return call(
        kernel,
        1,
        spot,
        [rows_in] + arrays,
        [whole_spec(rows_in)] + one_specs(parts, which),
        bf16(length, width),
        pl.BlockSpec((length, width), lambda step: (0, 0)),
        [pltpu.VMEM((width, columns), jnp.bfloat16)],
    )


def proj_grads(spot, grad_rows, mixed_rows, parts, which):
    arrays = [part.array for part in parts]
    share, columns = arrays[0].shape[-2:]
    length, width = grad_rows.shape
    count = width // share

    def kernel(spot_ref, grad_ref, mixed_ref, *rest):
        refs, (out_ref, keep_ref, send_ref, scratch, turned) = rest[:-5], rest[-5:]
        fill_one(scratch, spot_ref, parts, refs, which)
        turned[...] = jnp.transpose(grad_ref[...])
        out_ref[...] = product(grad_ref[...], scratch[...]).astype(jnp.bfloat16)
        put_grad(spot_ref, turned, mixed_ref[...], keep_ref, send_ref, share, count)

    half = bf16(count // 2, 1, share, columns)
    return call(
        kernel,
        1,
        spot,
        [grad_rows, mixed_rows] + arrays,
        [whole_spec(grad_rows), whole_spec(mixed_rows)] + one_specs(parts, which),
        (bf16(length, columns), half, half),
        (pl.BlockSpec((length, columns), lambda step: (0, 0)),)
        + (grad_specs(count, share, columns),) * 2,
        [pltpu.VMEM((width, columns), jnp.bfloat16), pltpu.VMEM((width, length), jnp.bfloat16)],
    )


def qkv_grads(spot, hidden, query_grads, block_grads, parts):
    arrays = [part.array for part in parts]
    tiles, share, columns = arrays[0].shape
    length, width = hidden.shape
    count = width // share

    seqs, rows = len(query_grads), query_grads[0].shape[1]

    def kernel(spot_ref, hid_ref, *rest):
        query_refs, block_refs, rest = rest[:seqs], rest[seqs : 2 * seqs], rest[2 * seqs :]
        refs, (out_ref, keep_ref, send_ref, scratch, total, turned, grad) = rest[:-7], rest[-7:]
        step = pl.program_id(0)
        fill(scratch, spot_ref, parts, refs)

        @pl.when(step == 0)
        def first():
            turned[...] = jnp.transpose(hid_ref[...])
            total[...] = jnp.zeros_like(total)
            for at, ref in enumerate(query_refs):
                grad[at * rows : (at + 1) * rows] = ref[0]

        @pl.when(step > 0)
        def later():
            for at, ref in enumerate(block_refs):
                grad[at * rows : (at + 1) * rows] = ref[0]

        total[...] += product_back(grad[...], scratch[...])
        put_grad(spot_ref, turned, grad[...], keep_ref, send_ref, share, count)

        @pl.when(step == tiles - 1)
        def finish():
            out_ref[...] = total[...].astype(jnp.bfloat16)

    half = bf16(count // 2, tiles, share, columns)
    return call(
        kernel,
        tiles,
        spot,
        [hidden, *query_grads] + [block_grads] * seqs + arrays,
        [whole_spec(hidden)]
        + [whole_spec(part) for part in query_grads]
        + [
            pl.BlockSpec(
                (1, rows, columns),
                functools.partial(lambda at, step: (2 * at + jnp.maximum(step - 1, 0), 0, 0), at),
            )
            for at in range(seqs)
        ]
        + [tile_spec(3, part.shape[1], columns) for part in arrays],
        (bf16(length, width), half, half),
        (pl.BlockSpec((length, width), lambda step: (0, 0)),)
        + (grad_specs(count, share, columns),) * 2,
        [
            pltpu.VMEM((width, columns), jnp.bfloat16),
            pltpu.VMEM((length, width), jnp.float32),
            pltpu.VMEM((width, length), jnp.bfloat16),
            pltpu.VMEM((length, columns), jnp.bfloat16),
        ],
    )


def gelu_parts(upward):
    squared = upward * upward
    bent = jnp.tanh(0.7978845608028654 * (upward + 0.044715 * (upward * squared)))
    activ = 0.5 * upward * (1.0 + bent)
    slope = 0.5 * (1.0 + bent) + 0.5 * upward * (1.0 - bent * bent) * (
        0.7978845608028654 * (1.0 + 3 * 0.044715 * squared)
    )
    return activ, slope


def feed_forward(spot, hidden, grad, up_parts, down_parts, columns):
    arrays = [part.array for part in up_parts + down_parts]
    share, units = arrays[0].shape
    tiles = units // columns
    length, width = hidden.shape
    count = width // share

    def kernel(spot_ref, hid_ref, grad_ref, *rest):
        refs, rest = rest[: len(arrays)], rest[len(arrays) :]
        out_ref, back_ref, up_keep, up_send, down_keep, down_send = rest[:6]
        up, down, out_sum, back_sum, hid_turned, grad_turned = rest[6:]
        step = pl.program_id(0)

        @pl.when(step == 0)
        def begin():
            hid_turned[...] = jnp.transpose(hid_ref[...])
            grad_turned[...] = jnp.transpose(grad_ref[...])
            out_sum[...] = jnp.zeros_like(out_sum)
            back_sum[...] = jnp.zeros_like(back_sum)

        fill(up, spot_ref, up_parts, refs[: len(up_parts)])
        fill(down, spot_ref, down_parts, refs[len(up_parts) :])
        activ, slope = gelu_parts(product(hid_ref[...], up[...]))
        activ = activ.astype(jnp.bfloat16)
        upward_grad = (product(grad_ref[...], down[...]) * slope).astype(jnp.bfloat16)
        out_sum[...] += product_back(activ, down[...])
        back_sum[...] += product_back(upward_grad, up[...])
        put_grad(spot_ref, grad_turned, activ, down_keep, down_send, share, count)
        put_grad(spot_ref, hid_turned, upward_grad, up_keep, up_send, share, count)

        @pl.when(step == tiles - 1)
        def finish():
            out_ref[...] = out_sum[...].astype(jnp.bfloat16)
            back_ref[...] = back_sum[...].astype(jnp.bfloat16)

    rows_spec = pl.BlockSpec((length, width), lambda step: (0, 0))
    wholes = [hidden, grad]
    return call(
        kernel,
        tiles,
        spot,
        wholes + arrays,
        [whole_spec(part) for part in wholes]
        + [tile_spec(2, part.shape[0], columns) for part in arrays],
        (bf16(length, width), bf16(length, width))
        + (bf16(count // 2, tiles, share, columns),) * 4,
        (rows_spec, rows_spec) + (grad_specs(count, share, columns),) * 4,
        [pltpu.VMEM((width, columns), jnp.bfloat16)] * 2
        + [pltpu.VMEM((length, width), jnp.float32)] * 2
        + [pltpu.VMEM((width, length), jnp.bfloat16)] * 2,
    )


def activate(seq, first, second):
    shape = first.shape
    tile = shape[1] // 2

    def kernel(first_ref, second_ref, out_ref):
        upward = first_ref[0].astype(jnp.float32) + second_ref[0].astype(jnp.float32)
        activ_grad = first_ref[1].astype(jnp.float32) + second_ref[1].astype(jnp.float32)
        activ, slope = gelu_parts(upward)
        out_ref[0] = activ.astype(jnp.bfloat16)
        out_ref[1] = (activ_grad * slope).astype(jnp.bfloat16)

    spec = pl.BlockSpec((2, tile, shape[2]), lambda step: (0, step, 0))
    return seq.mark(
        pl.pallas_call(
            kernel,
            grid=(2,),
            in_specs=[spec, spec],
            out_specs=spec,
            out_shape=bf16(*shape),
            compiler_params=pltpu.CompilerParams(
                dimension_semantics=("arbitrary",), vmem_limit_bytes=VMEM_LIMIT
            ),
            cost_estimate=SMALL_COST,
        )(seq.then(first), second)
    )


def middle_spread(seq, spot, modul, stream, branch, cot, count):
    seqs, length, width = stream.shape
    share = width // count

    def kernel(spot_ref, mod_ref, x_ref, one_ref, two_ref, cot_ref, *rest):
        outs, hid_all, grad_all = rest[:-2], rest[-2], rest[-1]
        middle = wide(x_ref) + mod_ref[0, 2:3] * (wide(one_ref) + wide(two_ref))
        norm, factor = normed(middle)
        hid_all[...] = (norm * (1.0 + mod_ref[0, 4:5]) + mod_ref[0, 3:4]).astype(jnp.bfloat16)
        grad_all[...] = (mod_ref[0, 5:6] * wide(cot_ref)).astype(jnp.bfloat16)
        for away, out in enumerate(outs):
            at = pl.multiple_of(jnp.bitwise_xor(spot_ref[0], away) * share, LANES)
            out[0, 0] = hid_all[:, pl.ds(at, share)]
            out[1, 0] = grad_all[:, pl.ds(at, share)]

    row_spec = pl.BlockSpec((1, length, width), lambda at: (at, 0, 0))
    made = pl.pallas_call(
        kernel,
        grid=(seqs,),
        in_specs=[
            pl.BlockSpec(memory_space=pltpu.SMEM),
            pl.BlockSpec((1,) + modul.shape[1:], lambda at: (at, 0, 0)),
        ]
        + [row_spec] * 4,
        out_specs=[pl.BlockSpec((2, 1, length, share), lambda at: (0, at, 0, 0))] * count,
        out_shape=[bf16(2, seqs, length, share)] * count,
        scratch_shapes=[pltpu.VMEM((length, width), jnp.bfloat16)] * 2,
        compiler_params=pltpu.CompilerParams(
            dimension_semantics=("arbitrary",), vmem_limit_bytes=VMEM_LIMIT
        ),
        cost_estimate=SMALL_COST,
    )(spot, modul, seq.then(stream), *branch, cot)
    seq.mark(made[0])
    return [part.reshape(2, -1, share) for part in made]


def lay_rows(spot, refs, scratch):
    rows = refs[0].shape[1]
    for away, ref in enumerate(refs):
        at = pl.multiple_of(jnp.bitwise_xor(spot[0], away) * rows, rows)
        scratch[:, pl.ds(at, rows), :] = ref[...]


def spread_up(seq, spot, features, up_shard, down_shard):
    count = len(features)
    rows, share = features[0].shape[1:]
    length = rows * count
    columns = up_shard.shape[1] // count

    def kernel(spot_ref, up_ref, down_ref, *rest):
        refs, (keep_ref, send_ref, rows_in) = rest[:count], rest[count:]

        @pl.when(pl.program_id(0) == 0)
        def begin():
            lay_rows(spot_ref, refs, rows_in)

        upward = product(rows_in[0], up_ref[...]).astype(jnp.bfloat16)
        activ_grad = product(rows_in[1], down_ref[...]).astype(jnp.bfloat16)
        odd = pl.program_id(0) % 2

        @pl.when(odd == 0)
        def keep():
            keep_ref[0, 0], keep_ref[0, 1] = upward, activ_grad

        @pl.when(odd != 0)
        def send():
            send_ref[0, 0], send_ref[0, 1] = upward, activ_grad

    shard_spec = pl.BlockSpec(
        (share, columns), lambda step, spot_ref: (0, jnp.bitwise_xor(spot_ref[0], step))
    )
    out_spec = pl.BlockSpec((1, 2, length, columns), lambda step, spot_ref: (step // 2, 0, 0, 0))
    out = bf16(count // 2, 2, length, columns)
    keep, send = pl.pallas_call(
        kernel,
        grid_spec=pltpu.PrefetchScalarGridSpec(
            num_scalar_prefetch=1,
            grid=(count,),
            in_specs=[shard_spec, shard_spec]
            + [pl.BlockSpec(part.shape, lambda step, spot_ref: (0, 0, 0)) for part in features],
            out_specs=[out_spec, out_spec],
            scratch_shapes=[pltpu.VMEM((2, length, share), jnp.bfloat16)],
        ),
        out_shape=[out, out],
        compiler_params=pltpu.CompilerParams(
            dimension_semantics=("arbitrary",), vmem_limit_bytes=VMEM_LIMIT
        ),
        cost_estimate=SMALL_COST,
    )(spot, up_shard, down_shard, seq.then(features[0]), *features[1:])
    seq.mark(keep)
    return keep, send


def spread_down(spot, features, blocks, up_shard, down_shard):
    count = len(blocks)
    length, columns = blocks[0].shape[1:]
    share, units = up_shard.shape
    rows = length // count

    def kernel(spot_ref, up_ref, down_ref, *rest):
        feature_refs, refs, rest = rest[:count], rest[count : 2 * count], rest[2 * count :]
        outs, (up_grad_ref, down_grad_ref, rows_in, sums) = rest[:count], rest[count:]
        lay_rows(spot_ref, feature_refs, rows_in)
        hid_turned, grad_turned = jnp.transpose(rows_in[0]), jnp.transpose(rows_in[1])
        out_sum = jnp.zeros((length, share), jnp.float32)
        back_sum = jnp.zeros((length, share), jnp.float32)
        for away, ref in enumerate(refs):
            place = jnp.bitwise_xor(spot_ref[0], away)
            at = pl.ds(pl.multiple_of(place * columns, columns), columns)
            activ, upward_grad = ref[0], ref[1]
            out_sum += product_back(activ, down_ref[:, at])
            back_sum += product_back(upward_grad, up_ref[:, at])
            up_grad_ref[place] = product(hid_turned, upward_grad).astype(jnp.bfloat16)
            down_grad_ref[place] = product(grad_turned, activ).astype(jnp.bfloat16)
        sums[0] = back_sum.astype(jnp.bfloat16)
        sums[1] = out_sum.astype(jnp.bfloat16)
        for away, out in enumerate(outs):
            at = pl.multiple_of(jnp.bitwise_xor(spot_ref[0], away) * rows, rows)
            out[...] = sums[:, pl.ds(at, rows), :]

    zeros = lambda step: (0, 0, 0)
    arrays = [up_shard, down_shard] + list(features) + list(blocks)
    *sums, up_grad, down_grad = call(
        kernel,
        1,
        spot,
        arrays,
        [whole_spec(part) for part in arrays],
        (bf16(2, rows, share),) * count + (bf16(count, share, columns),) * 2,
        (pl.BlockSpec((2, rows, share), zeros),) * count
        + (pl.BlockSpec((count, share, columns), zeros),) * 2,
        [pltpu.VMEM((2, length, share), jnp.bfloat16)] * 2,
    )
    return sums, up_grad, down_grad


def gather_features(seq, spot, pieces):
    count = len(pieces)
    rows, share = pieces[0].shape[1:]

    def kernel(spot_ref, *rest):
        refs, outs = rest[:count], rest[count:]
        for away, ref in enumerate(refs):
            at = pl.multiple_of(jnp.bitwise_xor(spot_ref[0], away) * share, LANES)
            for place, out in enumerate(outs):
                out[:, pl.ds(at, share)] = ref[place]

    out_spec = pl.BlockSpec((rows, share * count), lambda step: (0, 0))
    arrays = [seq.then(pieces[0])] + list(pieces[1:])
    made = call(
        kernel,
        1,
        spot,
        arrays,
        [whole_spec(part) for part in arrays],
        (bf16(rows, share * count),) * 2,
        (out_spec, out_spec),
        [],
    )
    seq.mark(made[0])
    return made


def row_kernel(seq, kernel, modul, rows_in, outs):
    seqs, length, width = rows_in[0].shape
    row_spec = pl.BlockSpec((1, length, width), lambda at: (at, 0, 0))
    sum_spec = pl.BlockSpec((1, 8, width), lambda at: (at, 0, 0))
    made = pl.pallas_call(
        kernel,
        grid=(seqs,),
        in_specs=[pl.BlockSpec((1,) + modul.shape[1:], lambda at: (at, 0, 0))]
        + [row_spec] * len(rows_in),
        out_specs=[sum_spec if kind is None else row_spec for kind in outs],
        out_shape=[
            jax.ShapeDtypeStruct((seqs, 8, width), jnp.float32)
            if kind is None
            else jax.ShapeDtypeStruct((seqs, length, width), kind)
            for kind in outs
        ],
        compiler_params=pltpu.CompilerParams(
            dimension_semantics=("arbitrary",), vmem_limit_bytes=VMEM_LIMIT
        ),
        cost_estimate=SMALL_COST,
    )(modul, seq.then(rows_in[0]), *rows_in[1:])
    seq.mark(made[0])
    return made


def wide(ref):
    return ref[0].astype(jnp.float32)


def put_sums(ref, rows):
    ref[0] = jnp.zeros_like(ref[0])
    for place, row in enumerate(rows):
        ref[0, place : place + 1] = jnp.sum(row, axis=0, keepdims=True)


def back_through(values, grad, scale_part):
    norm, factor = normed(values)
    inner = grad * (1.0 + scale_part)
    own = jnp.mean(inner, axis=-1, keepdims=True)
    along = jnp.mean(inner * norm, axis=-1, keepdims=True)
    return (inner - own - norm * along) * factor, norm


def first_hidden(seq, modul, stream):
    def kernel(mod_ref, x_ref, out_ref):
        norm, factor = normed(wide(x_ref))
        out_ref[0] = (norm * (1.0 + mod_ref[0, 1:2]) + mod_ref[0, 0:1]).astype(jnp.bfloat16)

    return row_kernel(seq, kernel, modul, [stream], [jnp.bfloat16])[0]


def middle_hidden(seq, modul, stream, branch, cot):
    def kernel(mod_ref, x_ref, one_ref, two_ref, cot_ref, hid_ref, grad_ref):
        middle = wide(x_ref) + mod_ref[0, 2:3] * (wide(one_ref) + wide(two_ref))
        norm, factor = normed(middle)
        hid_ref[0] = (norm * (1.0 + mod_ref[0, 4:5]) + mod_ref[0, 3:4]).astype(jnp.bfloat16)
        grad_ref[0] = (mod_ref[0, 5:6] * wide(cot_ref)).astype(jnp.bfloat16)

    return row_kernel(seq, kernel, modul, [stream, *branch, cot], [jnp.bfloat16, jnp.bfloat16])


def middle_grads(seq, modul, stream, branch, cot, hidden_grad):
    def kernel(mod_ref, x_ref, one_ref, two_ref, cot_ref, hid_ref, other_ref, mid_out, out, sums):
        branch_sum = wide(one_ref) + wide(two_ref)
        middle = wide(x_ref) + mod_ref[0, 2:3] * branch_sum
        grad = wide(hid_ref) + wide(other_ref)
        through, norm = back_through(middle, grad, mod_ref[0, 4:5])
        mid_grad = wide(cot_ref) + through
        mid_out[0] = mid_grad
        out[0] = (mod_ref[0, 2:3] * mid_grad).astype(jnp.bfloat16)
        put_sums(sums, [mid_grad * branch_sum, grad, grad * norm])

    return row_kernel(
        seq,
        kernel,
        modul,
        [stream, *branch, cot, *hidden_grad],
        [jnp.float32, jnp.bfloat16, None],
    )


def input_grads(seq, modul, stream, mid_grad, hidden_grad):
    def kernel(mod_ref, x_ref, mid_ref, hid_ref, other_ref, out, sums):
        grad = wide(hid_ref) + wide(other_ref)
        through, norm = back_through(wide(x_ref), grad, mod_ref[0, 1:2])
        out[0] = (mid_ref[0] + through).astype(jnp.bfloat16)
        put_sums(sums, [grad, grad * norm])

    return row_kernel(
        seq, kernel, modul, [stream, mid_grad, *hidden_grad], [jnp.bfloat16, None]
    )


def results(seq, modul, stream, branch, second, cot, real):
    def kernel(mod_ref, x_ref, one_ref, two_ref, three_ref, four_ref, cot_ref, out, sums):
        start = wide(x_ref)
        gated_one = mod_ref[0, 2:3] * (wide(one_ref) + wide(two_ref))
        middle = start + gated_one
        branch_two = wide(three_ref) + wide(four_ref)
        gated_two = mod_ref[0, 5:6] * branch_two
        result = middle + gated_two
        out[0] = result.astype(jnp.bfloat16)
        shown = lax.broadcasted_iota(jnp.int32, start.shape, 0) < real
        put_sums(
            sums,
            [wide(cot_ref) * branch_two]
            + [
                jnp.where(shown, member * member, 0.0)
                for member in (start, gated_one, middle, gated_two, result)
            ],
        )

    return row_kernel(
        seq, kernel, modul, [stream, *branch, *second, cot], [jnp.bfloat16, None]
    )


def head_lanes(shape, head):
    lane = lax.broadcasted_iota(jnp.int32, shape, len(shape) - 1)
    return (lane >= head * HD) & (lane < (head + 1) * HD)


def padding(shape, axis, image_rows, text_rows, real, count):
    place = lax.broadcasted_iota(jnp.int32, shape, axis) - image_rows * count
    hidden = (place >= real) & (place < text_rows)
    for other in range(1, count):
        hidden = hidden | (
            (place >= other * text_rows + real) & (place < (other + 1) * text_rows)
        )
    return hidden


def attention_specs(image, text):
    row = [
        pl.BlockSpec((1, rows, LANES), lambda seq, part: (seq, 0, part))
        for rows in (image.shape[1], text.shape[1])
    ]
    block = [
        pl.BlockSpec((2, 1, rows, LANES), lambda seq, part: (0, seq, 0, part))
        for rows in (image.shape[1], text.shape[1])
    ]
    return row, block


def joint(refs, index):
    return jnp.concatenate([ref[index] for ref in refs], axis=0)


def attend(image, text, image_blocks, text_blocks, real):
    seqs, image_rows, width = image.shape
    text_rows = text.shape[1]
    rows = image_rows + text_rows
    count = len(image_blocks)
    keys = rows * count

    def kernel(*rest):
        refs, (image_out, text_out) = rest[:-2], rest[-2:]
        queries = joint(refs[:2], 0)
        key_all = joint(refs[2:], (0, 0))
        value_all = joint(refs[2:], (1, 0))
        hidden = padding((1, keys), 1, image_rows, text_rows, real, count)
        result = jnp.zeros((rows, LANES), jnp.float32)
        for head in range(LANES // HD):
            mine = head_lanes((rows, LANES), head)
            scores = product_back(jnp.where(mine, queries, jnp.zeros_like(queries)), key_all)
            scores = jnp.where(hidden, -1e30, scores * 0.125)
            expd = jnp.exp(scores - jnp.max(scores, axis=1, keepdims=True))
            share = 1.0 / jnp.sum(expd, axis=1, keepdims=True)
            mixed = product((expd * share).astype(jnp.bfloat16), value_all)
            result = jnp.where(mine, mixed, result)
        image_out[0] = result[:image_rows].astype(jnp.bfloat16)
        text_out[0] = result[image_rows:].astype(jnp.bfloat16)

    row, block = attention_specs(image, text)
    return pl.pallas_call(
        kernel,
        grid=(seqs, width // LANES),
        in_specs=row + [block[0]] * count + [block[1]] * count,
        out_specs=row,
        out_shape=[bf16(*image.shape), bf16(*text.shape)],
        compiler_params=pltpu.CompilerParams(
            dimension_semantics=("arbitrary", "arbitrary"), vmem_limit_bytes=VMEM_LIMIT
        ),
        cost_estimate=SMALL_COST,
    )(image, text, *image_blocks, *text_blocks)


def attend_grads(queries_in, grads_in, image_blocks, text_blocks, real, seq):
    image, text = queries_in
    image_rows, width = image.shape[1:]
    text_rows = text.shape[1]
    rows = image_rows + text_rows
    count = len(image_blocks)
    keys = rows * count

    def kernel(*rest):
        refs, (image_out, text_out, keep_ref, send_ref) = rest[:-4], rest[-4:]
        queries = joint(refs[:2], 0)
        grads = joint(refs[2:4], 0)
        key_all = joint(refs[4:], (0, 0))
        value_all = joint(refs[4:], (1, 0))
        hidden = padding((keys, 1), 0, image_rows, text_rows, real, count)
        query_grad = jnp.zeros((rows, LANES), jnp.float32)
        key_grad = jnp.zeros((keys, LANES), jnp.float32)
        value_grad = jnp.zeros((keys, LANES), jnp.float32)
        for head in range(LANES // HD):
            mine = head_lanes((rows, LANES), head)
            own_query = jnp.where(mine, queries, jnp.zeros_like(queries))
            own_grad = jnp.where(mine, grads, jnp.zeros_like(grads))
            scores = product_back(key_all, own_query)
            scores = jnp.where(hidden, -1e30, scores * 0.125)
            expd = jnp.exp(scores - jnp.max(scores, axis=0, keepdims=True))
            probs = expd * (1.0 / jnp.sum(expd, axis=0, keepdims=True))
            prob_grad = product_back(value_all, own_grad)
            delta = jnp.sum(probs * prob_grad, axis=0, keepdims=True)
            score_grad = (probs * (prob_grad - delta)).astype(jnp.bfloat16)
            value_grad += product(probs.astype(jnp.bfloat16), own_grad)
            key_grad += product(score_grad, own_query)
            back = lax.dot_general(
                score_grad, key_all, (((0,), (0,)), ((), ())), preferred_element_type=jnp.float32
            )
            query_grad = jnp.where(mine, back, query_grad)
        query_grad = (query_grad * 0.125).astype(jnp.bfloat16)
        image_out[0] = query_grad[:image_rows]
        text_out[0] = query_grad[image_rows:]
        key_grad = (key_grad * 0.125).astype(jnp.bfloat16)
        value_grad = value_grad.astype(jnp.bfloat16)
        for away in range(count):
            to, place = (send_ref if away & 1 else keep_ref), away // 2
            at = slice(away * image_rows, (away + 1) * image_rows)
            to[place, 0, :image_rows], to[place, 1, :image_rows] = key_grad[at], value_grad[at]
            first = count * image_rows + away * text_rows
            at = slice(first, first + text_rows)
            to[place, 0, image_rows:], to[place, 1, image_rows:] = key_grad[at], value_grad[at]

    def row_spec(length, at):
        return pl.BlockSpec((1, length, LANES), lambda part: (at, 0, part))

    def block_spec(length):
        return pl.BlockSpec((2, 1, length, LANES), lambda part: (0, seq, 0, part))

    def owner_spec(length):
        return pl.BlockSpec((count // 2, 2, length, LANES), lambda part: (0, 0, 0, part))

    sizes = (image_rows, text_rows)
    return pl.pallas_call(
        kernel,
        grid=(width // LANES,),
        in_specs=[row_spec(length, seq) for length in sizes] * 2
        + [block_spec(image_rows)] * count
        + [block_spec(text_rows)] * count,
        out_specs=[row_spec(length, 0) for length in sizes]
        + [owner_spec(rows)] * 2,
        out_shape=[bf16(1, length, width) for length in sizes]
        + [bf16(count // 2, 2, rows, width)] * 2,
        compiler_params=pltpu.CompilerParams(
            dimension_semantics=("arbitrary",), vmem_limit_bytes=VMEM_LIMIT
        ),
        cost_estimate=SMALL_COST,
    )(image, text, *grads_in, *image_blocks, *text_blocks)


def on_device(
    image_tokens,
    text_tokens,
    text_owner,
    conditioning,
    slot_sequence,
    image_w_mod,
    image_b_mod,
    image_w_qkv,
    image_w_proj,
    image_w_up,
    image_w_down,
    text_w_mod,
    text_b_mod,
    text_w_qkv,
    text_w_proj,
    text_w_up,
    text_w_down,
    image_cotangent,
    text_cotangent,
):
    tok_rank = lax.axis_index("tok")
    rep_rank = lax.axis_index("rep")
    rep_count = lax.axis_size("rep")
    tok_count = lax.axis_size("tok")
    seqs, image_rows, width = image_tokens.shape
    text_real = text_cotangent.shape[1]
    text_rows = -(-text_real // 16) * 16
    slots = conditioning.shape[0]
    share = image_w_mod.shape[0]
    heads_width = image_w_qkv.shape[2]
    spot = jnp.stack([tok_rank, lax.rem(rep_rank, 2)]).astype(jnp.int32)

    turn = lambda weight: jnp.transpose(weight, (1, 0, 2))
    chips = Lane("tok", 2)
    proj_stack = jnp.stack([image_w_proj, text_w_proj])
    qkv_held = fetch(turn(image_w_qkv), 1, chips)
    qkv_own, text_own = flip(turn(image_w_qkv), "tok", 1), flip(turn(text_w_qkv), "tok", 1)
    image_qkv_parts, unused = share_out(turn(image_w_qkv), qkv_own, qkv_held)

    picker = (slot_sequence[:, None] == jnp.arange(slots, dtype=jnp.int32)[None, :]).astype(
        jnp.float32
    )
    cond_slots = jnp.dot(picker, conditioning, precision=exact_mode)
    activ_all = jax.nn.silu(cond_slots).astype(jnp.bfloat16)
    activ_group = lax.dynamic_slice_in_dim(activ_all, rep_rank * seqs, seqs, axis=0)
    activ_share = lax.dynamic_slice_in_dim(activ_group, tok_rank * share, share, axis=1)
    both_mod = tok_total(
        jnp.stack(
            [
                jnp.einsum("sd,dke->ske", activ_share, weight, preferred_element_type=jnp.float32)
                for weight in (image_w_mod, text_w_mod)
            ]
        ),
        *qkv_held.values(),
    )
    image_mod = both_mod[0] + image_b_mod.astype(jnp.float32)[None]
    text_mod = both_mod[1] + text_b_mod.astype(jnp.float32)[None]

    text_held = fetch(turn(text_w_qkv), 1, chips, (both_mod,))
    cores = Lane("tok", 1)
    up_own = cores.flip(after(image_w_up, both_mod), 1)
    down_own = cores.flip(after(image_w_down, both_mod), 1)
    proj_held = fetch(proj_stack, 0, chips, tuple(text_held.values()))

    owned = (text_owner == tok_rank).astype(jnp.float32)
    total_text = text_owner.shape[1]
    before = jnp.dot(
        owned,
        jnp.triu(jnp.ones((total_text, total_text), jnp.float32), 1),
        precision=exact_mode,
    )
    chosen = (
        (before[:, None, :] == jnp.arange(text_rows, dtype=jnp.float32)[None, :, None])
        & (owned[:, None, :] > 0.5)
    ).astype(jnp.bfloat16)
    text_input = jnp.einsum(
        "srt,std->srd", chosen, text_tokens, preferred_element_type=jnp.float32
    ).astype(jnp.bfloat16)
    text_cot = jnp.pad(text_cotangent, ((0, 0), (0, text_rows - text_real), (0, 0)))

    seq = Sequence()
    flat = lambda values: values.reshape(-1, values.shape[-1])
    by_seq = lambda values: values.reshape(values.shape[:-2] + (seqs, -1, values.shape[-1]))
    both = lambda pair: tuple(by_seq(part) for part in pair)
    heads = lambda partial: both(head_pair(partial))

    image_hid_one = flat(first_hidden(seq, image_mod, image_tokens))
    image_qkv = seq.mark(
        project(
            spot,
            after(seq.then(image_hid_one), *text_held.values(), up_own, down_own),
            image_qkv_parts,
        )
    )
    image_blocks = gather_blocks(after(by_seq(image_qkv[1:]), *proj_held.values()), chips)
    text_qkv_parts, text_swapped = share_out(
        turn(text_w_qkv), text_own, text_held, (image_qkv,)
    )
    text_hid_one = flat(first_hidden(seq, text_mod, after(text_input, *proj_held.values())))
    text_qkv = project(spot, seq.then(text_hid_one), text_qkv_parts)
    text_blocks = gather_blocks(by_seq(text_qkv[1:]), chips)
    proj_own = flip(after(proj_stack, image_qkv), "tok", 1)
    seq.mark(text_qkv, proj_own)
    proj_parts, unused = share_out(
        proj_stack, proj_own, proj_held, (text_qkv,), (image_qkv,)
    )
    up_held = fetch(image_w_up, 0, chips)
    down_held = fetch(image_w_down, 0, chips)
    image_query, text_query = by_seq(image_qkv[0]), by_seq(text_qkv[0])
    image_mix, text_mix = attend(
        image_query, seq.then(text_query), image_blocks, text_blocks, text_real
    )
    seq.mark(image_mix, *up_held.values())
    image_mixed, text_mixed = flat(image_mix), flat(text_mix)
    text_out = seq.mark(project_back(spot, seq.then(text_mixed), proj_parts, 1, width))
    text_branch = heads(text_out)
    image_up_parts, up_swapped = share_out(image_w_up, up_own, up_held)
    image_down_parts, down_swapped = share_out(image_w_down, down_own, down_held)
    image_out = project_back(spot, seq.then(image_mixed), proj_parts, 0, width)
    seq.mark(image_out, *down_held.values())
    if lax.axis_size("head") == 2:
        image_branch = both((image_out, flip(after(image_out, text_branch[1]), "head", 1)))
    else:
        image_branch = heads(image_out)

    text_features = exchange(
        middle_spread(seq, spot, text_mod, text_input, text_branch, text_cot, tok_count)
    )
    image_hid_two, image_db_two = middle_hidden(
        seq, image_mod, image_tokens, image_branch, image_cotangent
    )
    seq.mark(image_hid_two, *up_swapped, *down_swapped)
    text_keep, text_send = spread_up(seq, spot, text_features, text_w_up, text_w_down)
    text_pieces = core_sums(seq, text_keep, flip(text_send, "tok", 1))
    text_stays, text_came = chip_moves(seq, text_pieces, chips)
    image_part, image_back, image_up_keep, image_up_send, image_down_keep, image_down_send = (
        feed_forward(
            spot,
            seq.then(flat(image_hid_two)),
            flat(image_db_two),
            image_up_parts,
            image_down_parts,
            heads_width,
        )
    )
    seq.mark(image_back)
    shape = (2,) + text_keep.shape[2:]
    text_act = activate(seq, text_stays.reshape(shape), text_came.reshape(shape))
    text_lane = chips
    image_hid_grad = heads(after(image_back, text_act))
    image_down_send = after(image_down_send, text_act)
    image_up_send = after(image_up_send, text_act)
    chips = Lane("tok", 3)
    image_down_pieces = core_sums(seq, image_down_keep, flip(image_down_send, "tok", 1))
    image_up_pieces = core_sums(seq, image_up_keep, flip(image_up_send, "tok", 1))
    text_active = gather_blocks(text_act, text_lane, (image_up_pieces[0],))
    text_sums, text_up_grad, text_down_grad = spread_down(
        spot,
        [seq.then(text_features[0])] + text_features[1:],
        text_active,
        text_w_up,
        text_w_down,
    )
    seq.mark(text_sums[0])
    text_back_pieces = exchange(text_sums)
    behind = lambda pieces: {
        away: after(part, text_sums[0]) if away else part for away, part in pieces.items()
    }
    image_down_pair = chip_moves(seq, behind(image_down_pieces), chips)
    image_up_pair = chip_moves(seq, behind(image_up_pieces), chips)
    line = Line(seq)
    if line.on_line:
        for whole in (text_down_grad, text_up_grad):
            for place in range(2):
                line.add(flat(whole.reshape(2, -1, share, whole.shape[-1])[place]))
        text_totals = None
    else:
        text_totals = [lax.psum(part, "rep") for part in (text_down_grad, text_up_grad)]

    image_mid_grad, image_db_one, image_mid_sums = middle_grads(
        seq, image_mod, image_tokens, image_branch, image_cotangent, image_hid_grad
    )
    text_back, text_part = gather_features(seq, spot, text_back_pieces)
    text_hid_grad = heads(text_back)
    image_mixed_grad, image_proj_keep, image_proj_send = proj_grads(
        spot, seq.then(flat(image_db_one)), image_mixed, proj_parts, 0
    )
    seq.mark(image_mixed_grad)
    text_mid_grad, text_db_one, text_mid_sums = middle_grads(
        seq, text_mod, text_input, text_branch, text_cot, text_hid_grad
    )
    text_mixed_grad, text_proj_keep, text_proj_send = proj_grads(
        spot, seq.then(flat(text_db_one)), text_mixed, proj_parts, 1
    )
    seq.mark(text_mixed_grad)
    line.step()
    proj_pieces = [
        core_sums(seq, keep, flip(send, "tok", 1))
        for keep, send in ((image_proj_keep, image_proj_send), (text_proj_keep, text_proj_send))
    ]
    made_grads, moved_grads = [], []
    mix_grads = (by_seq(image_mixed_grad), by_seq(text_mixed_grad))
    for at in range(seqs):
        made = attend_grads(
            (image_query, text_query),
            (seq.then(mix_grads[0]), mix_grads[1]),
            image_blocks,
            text_blocks,
            text_real,
            at,
        )
        made_grads.append(made)
        seq.mark(made[0])
        if at == 0 or at == seqs - 1:
            for part in add_blocks(seq, *(image_up_pair if at else image_down_pair), 2):
                line.add(part)
        if at == 0 and seqs == 1:
            for part in add_blocks(seq, *image_up_pair, 2):
                line.add(part)
        line.step()
        moved_grads.append(flip(after(made[3], *seq.last), "tok", 1))
    block_move = chip_moves(
        seq, core_sums_joined(seq, [made[2] for made in made_grads], moved_grads), chips
    )
    line.step()
    tail = Line(seq)
    block_grads = add_split(seq, *block_move, 2 * seqs, image_rows)
    proj_pairs = [chip_moves(seq, pieces, chips) for pieces in proj_pieces]
    image_in_part, image_qkv_keep, image_qkv_send = qkv_grads(
        spot,
        seq.then(image_hid_one),
        [made[0] for made in made_grads],
        block_grads[0],
        image_qkv_parts,
    )
    seq.mark(image_in_part)
    line.step()
    text_in_part, text_qkv_keep, text_qkv_send = qkv_grads(
        spot,
        seq.then(text_hid_one),
        [made[1] for made in made_grads],
        block_grads[1],
        text_qkv_parts,
    )
    seq.mark(text_in_part)
    qkv_pairs = [
        chip_moves(seq, core_sums(seq, keep, flip(send, "tok", 1)), chips)
        for keep, send in ((image_qkv_keep, image_qkv_send), (text_qkv_keep, text_qkv_send))
    ]
    line.step()
    image_in_grad = heads(image_in_part)
    text_in_grad = heads(text_in_part)
    image_proj_share, text_proj_share = [add_blocks(seq, *pair, 1)[0] for pair in proj_pairs]
    line.step()
    image_grad, image_in_sums = input_grads(
        seq, image_mod, image_tokens, image_mid_grad, image_in_grad
    )
    text_grad, text_in_sums = input_grads(
        seq, text_mod, text_input, text_mid_grad, text_in_grad
    )
    text_second = heads(after(text_part, image_in_sums))
    image_second = heads(after(image_part, image_in_sums))
    image_qkv_shares = add_blocks(seq, *qkv_pairs[0], 3)
    line.step()
    text_qkv_shares = add_blocks(seq, *qkv_pairs[1], 3)
    line.step()
    for part in [image_proj_share, text_proj_share, *image_qkv_shares, *text_qkv_shares]:
        tail.add(part)
    text_result, text_out_sums = results(
        seq, text_mod, text_input, text_branch, text_second, text_cot, text_real
    )
    image_result, image_out_sums = results(
        seq, image_mod, image_tokens, image_branch, image_second, image_cotangent, image_rows
    )
    line.step()
    line_sums = line.finish()
    tail_sums = tail.finish()
    columns_of = lambda parts: jnp.concatenate(
        [
            column.astype(jnp.float32)
            for part in parts
            for column in part.reshape(-1, share, part.shape[-1])
        ],
        axis=1,
    )
    if text_totals is None:
        text_totals = [jnp.concatenate(line_sums[at : at + 2]) for at in (0, 2)]
        text_totals = [part.reshape(tok_count, share, -1) for part in text_totals]
        line_sums = line_sums[4:]
    text_down_sum, text_up_sum = [columns_of([part]) for part in text_totals]
    image_down_sum, image_up_sum = columns_of(line_sums[:2]), columns_of(line_sums[2:])
    image_proj_sum, text_proj_sum = tail_sums[:2]
    image_qkv_sum = jnp.stack(tail_sums[2:5], axis=1)
    text_qkv_sum = jnp.stack(tail_sums[5:], axis=1)

    early = jnp.stack(
        [
            jnp.concatenate([mid_sums[:, :3], out_sums[:, :1]], axis=1)
            for mid_sums, out_sums in (
                (image_mid_sums, image_out_sums),
                (text_mid_sums, text_out_sums),
            )
        ]
    )
    late = jnp.stack([image_in_sums[:, :2], text_in_sums[:, :2]])
    squares = jnp.concatenate(
        [jnp.sum(out_sums[:, 1:6], axis=(0, 2)) for out_sums in (image_out_sums, text_out_sums)]
    )
    square_row = jnp.pad(squares, (0, width - 10))[None]
    all_sums = jnp.concatenate(
        [early.reshape(-1, width), late.reshape(-1, width), square_row], axis=0
    )
    waits = []
    if line.on_line:
        waits = [tail.totals[1], tail.totals[3]]
    all_sums = rep_gather(tok_total(all_sums), waits)
    square_total = jnp.sum(all_sums[:, -1, :10], axis=0)
    early_table = jnp.moveaxis(
        all_sums[:, : 8 * seqs].reshape(rep_count, 2, seqs, 4, width), 0, 1
    ).reshape(2, slots, 4, width)
    late_table = jnp.moveaxis(
        all_sums[:, 8 * seqs : -1].reshape(rep_count, 2, seqs, 2, width), 0, 1
    ).reshape(2, slots, 2, width)
    mod_sum = jnp.concatenate([late_table, early_table], axis=2)

    activ_rows = lax.dynamic_slice_in_dim(activ_all, tok_rank * share, share, axis=1).astype(
        jnp.float32
    )
    image_g_mod = jnp.einsum("sd,ske->dke", activ_rows, mod_sum[0], precision=lax.Precision.HIGH)
    text_g_mod = jnp.einsum("sd,ske->dke", activ_rows, mod_sum[1], precision=lax.Precision.HIGH)
    image_g_bmod = jnp.sum(mod_sum[0], axis=0)
    text_g_bmod = jnp.sum(mod_sum[1], axis=0)
    activ_grad = jnp.einsum(
        "ske,dke->sd", mod_sum[0], image_w_mod.astype(jnp.float32), precision=exact_mode
    ) + jnp.einsum("ske,dke->sd", mod_sum[1], text_w_mod.astype(jnp.float32), precision=exact_mode)
    cond_rows = lax.dynamic_slice_in_dim(cond_slots, tok_rank * share, share, axis=1)
    unused_value, silu_back = jax.vjp(jax.nn.silu, cond_rows)
    slot_grad = silu_back(activ_grad)[0]
    cond_grad = jnp.dot(jnp.transpose(picker), slot_grad, precision=exact_mode)
    image_count = float(slots * image_rows * tok_count * width)
    text_count = float(slots * text_real * tok_count * width)
    counts = jnp.concatenate(
        [jnp.full((5,), image_count, jnp.float32), jnp.full((5,), text_count, jnp.float32)]
    )
    stream_rms = jnp.sqrt(square_total / counts)
    return (
        image_result,
        text_result[:, :text_real],
        image_grad,
        text_grad[:, :text_real],
        cond_grad,
        image_g_mod,
        image_g_bmod,
        image_qkv_sum,
        image_proj_sum,
        image_up_sum,
        image_down_sum,
        text_g_mod,
        text_g_bmod,
        text_qkv_sum,
        text_proj_sum,
        text_up_sum,
        text_down_sum,
        stream_rms,
    )


def solution(mesh):
    in_specs = (
        P("rep", "tok", None),
        P("rep", None, None),
        P("rep", None),
        P(),
        P(),
        P("tok", None, None),
        P(),
        P("tok", None, "head"),
        P("tok", "head"),
        P("tok", "head"),
        P("tok", "head"),
        P("tok", None, None),
        P(),
        P("tok", None, "head"),
        P("tok", "head"),
        P("tok", "head"),
        P("tok", "head"),
        P("rep", "tok", None),
        P("rep", "tok", None),
    )
    out_specs = (
        P("rep", "tok", None),
        P("rep", "tok", None),
        P("rep", "tok", None),
        P("rep", "tok", None),
        P(None, "tok"),
        P("tok", None, None),
        P(),
        P("tok", None, "head"),
        P("tok", "head"),
        P("tok", "head"),
        P("tok", "head"),
        P("tok", None, None),
        P(),
        P("tok", None, "head"),
        P("tok", "head"),
        P("tok", "head"),
        P("tok", "head"),
        P(),
    )
    return jax.shard_map(
        on_device, mesh=mesh, in_specs=in_specs, out_specs=out_specs, check_vma=False
    )
```

```python
import functools

import jax
import jax.numpy as jnp
from jax import lax
from jax.experimental import pallas as pl
from jax.experimental.pallas import tpu as pltpu
from jax.sharding import PartitionSpec as P

HD = 64
LANES = 128
VMEM_LIMIT = 60 * 1024 * 1024
SMALL_COST = pl.CostEstimate(flops=1024, bytes_accessed=1024, transcendentals=0)

exact_mode = lax.Precision.HIGHEST


def normed(values):
    centered = values - jnp.mean(values, axis=-1, keepdims=True)
    scale = lax.rsqrt(jnp.mean(centered * centered, axis=-1, keepdims=True) + 1e-06)
    return centered * scale, scale


def flip(values, axis, bit):
    return lax.ppermute(
        values, axis, [(place, place ^ bit) for place in range(lax.axis_size(axis))]
    )


def head_pair(partial):
    if lax.axis_size("head") != 2:
        return lax.psum(partial, "head"), jnp.zeros_like(partial)
    return partial, flip(partial, "head", 1)


def after(values, *needed):
    return lax.optimization_barrier((values, *needed))[0]


class Sequence:
    def __init__(self):
        self.last = None

    def then(self, values):
        return values if self.last is None else after(values, *self.last)

    def mark(self, output, *moves):
        self.last = (output, *moves)
        return output


class Lane:
    def __init__(self, axis, depth):
        self.axis, self.depth, self.over = axis, depth, []

    def flip(self, values, bit):
        if len(self.over) >= self.depth:
            values = after(values, self.over[-self.depth])
        moved = flip(values, self.axis, bit)
        self.over.append(moved)
        return moved


class Part:
    def __init__(self, away, half, array):
        self.away, self.half, self.array = away, half, array


def fetch(weight, axis, lane, needed=()):
    parity = lax.rem(lax.axis_index("rep"), 2)
    size = weight.shape[axis] // 2
    held = {0: lax.dynamic_slice_in_dim(weight, parity * size, size, axis=axis)}
    if needed:
        held[0] = after(held[0], *needed)
    bit = lax.axis_size("tok") // 2
    while bit > 1:
        for away, array in list(held.items()):
            held[away ^ bit] = lane.flip(array, bit)
        bit //= 2
    del held[0]
    return held


def share_out(weight, own, held, needed=(), first=()):
    parts = []
    for away, array in held.items():
        leaving = after(array, *first) if first else array
        parts += [Part(away, 0, array), Part(away, 1, flip(leaving, "rep", 1))]
    others = [
        Part(
            part.away ^ 1,
            part.half,
            flip(after(part.array, *needed) if needed else part.array, "tok", 1),
        )
        for part in parts
    ]
    swapped = [part.array for part in parts if part.half == 1]
    return [Part(0, None, weight)] + parts + [Part(1, None, own)] + others, swapped


def gather_blocks(values, lane, needed=()):
    pieces = {0: values}
    bit = lax.axis_size("tok") // 2
    while bit > 0:
        for away, part in list(pieces.items()):
            if bit > 1:
                pieces[away ^ bit] = lane.flip(part, bit)
            else:
                part = after(part, *needed) if away and needed else part
                pieces[away ^ bit] = flip(part, "tok", bit)
        bit //= 2
    return [pieces[away] for away in range(len(pieces))]


def add_blocks(seq, first, second, outputs, kind=jnp.bfloat16):
    width = first.shape[-1]
    flat = lambda values: values.reshape(outputs, -1, width)
    first, second = flat(seq.then(first)), flat(second)
    rows = first.shape[1]
    tile = rows // 2

    def kernel(first_ref, second_ref, *out_refs):
        for place, out_ref in enumerate(out_refs):
            out_ref[...] = (
                first_ref[place].astype(jnp.float32) + second_ref[place].astype(jnp.float32)
            ).astype(kind)

    in_spec = pl.BlockSpec((outputs, tile, width), lambda step: (0, step, 0))
    sums = pl.pallas_call(
        kernel,
        grid=(2,),
        in_specs=[in_spec, in_spec],
        out_specs=[pl.BlockSpec((tile, width), lambda step: (step, 0))] * outputs,
        out_shape=[jax.ShapeDtypeStruct((rows, width), kind)] * outputs,
        compiler_params=pltpu.CompilerParams(
            dimension_semantics=("arbitrary",), vmem_limit_bytes=VMEM_LIMIT
        ),
        cost_estimate=SMALL_COST,
    )(first, second)
    seq.mark(sums[0])
    return sums


def core_sums(seq, keep, moved):
    sums = add_blocks(seq, keep, moved, keep.shape[0])
    return {2 * place: part for place, part in enumerate(sums)}


def core_sums_joined(seq, keeps, moved):
    pieces, pair, rows, width = keeps[0].shape
    pairs = len(keeps)

    def kernel(*refs):
        for at in range(pairs):
            for place in range(pieces):
                refs[2 * pairs + place][at] = (
                    refs[at][place].astype(jnp.float32)
                    + refs[pairs + at][place].astype(jnp.float32)
                ).astype(jnp.bfloat16)

    spec = pl.BlockSpec((pieces, 1, rows, width), lambda step: (0, step, 0, 0))
    sums = pl.pallas_call(
        kernel,
        grid=(pair,),
        in_specs=[spec] * (2 * pairs),
        out_specs=[pl.BlockSpec((pairs, 1, rows, width), lambda step: (0, step, 0, 0))] * pieces,
        out_shape=[bf16(pairs, pair, rows, width)] * pieces,
        compiler_params=pltpu.CompilerParams(
            dimension_semantics=("arbitrary",), vmem_limit_bytes=VMEM_LIMIT
        ),
        cost_estimate=SMALL_COST,
    )(seq.then(keeps[0]), *keeps[1:], *moved)
    seq.mark(sums[0])
    return {2 * place: part.reshape(-1, width) for place, part in enumerate(sums)}


def add_split(seq, first, second, groups, top):
    width = first.shape[-1]
    first, second = seq.then(first).reshape(groups, -1, width), second.reshape(groups, -1, width)
    rows = first.shape[1]

    def kernel(first_ref, second_ref, top_ref, bottom_ref):
        total = (first_ref[0].astype(jnp.float32) + second_ref[0].astype(jnp.float32)).astype(
            jnp.bfloat16
        )
        top_ref[0], bottom_ref[0] = total[:top], total[top:]

    spec = lambda length: pl.BlockSpec((1, length, width), lambda step: (step, 0, 0))
    parts = pl.pallas_call(
        kernel,
        grid=(groups,),
        in_specs=[spec(rows), spec(rows)],
        out_specs=[spec(top), spec(rows - top)],
        out_shape=[bf16(groups, top, width), bf16(groups, rows - top, width)],
        compiler_params=pltpu.CompilerParams(
            dimension_semantics=("arbitrary",), vmem_limit_bytes=VMEM_LIMIT
        ),
        cost_estimate=SMALL_COST,
    )(first, second)
    seq.mark(parts[0])
    return parts


def chip_moves(seq, pieces, lane):
    bit = 2
    while 2 * bit < lax.axis_size("tok"):
        pieces = {
            away: add_blocks(seq, part, lane.flip(pieces[away | bit], bit), 1)[0]
            for away, part in pieces.items()
            if not away & bit
        }
        bit *= 2
    if bit >= lax.axis_size("tok"):
        return pieces[0], jnp.zeros_like(pieces[0])
    return pieces[0], lane.flip(pieces[bit], bit)


def exchange(pieces):
    return [pieces[0]] + [flip(part, "tok", 1 + place) for place, part in enumerate(pieces[1:])]


class Line:
    def __init__(self, seq):
        self.seq = seq
        self.on_line = lax.axis_size("rep") == 4
        rank = lax.axis_index("rep")
        self.inner = ((rank == 1) | (rank == 2)).astype(jnp.int32).reshape(1)
        self.chunks, self.totals, self.outward = [], {}, {}
        self.place = 0
        self.came, self.pair, self.over = None, None, None

    def outer(self, load, pairs):
        return lax.ppermute(load, "rep", pairs)

    def add(self, chunk):
        self.chunks.append(chunk)
        if self.on_line and len(self.chunks) == 1:
            self.came = self.outer(chunk, [(0, 1), (3, 2)])

    def step(self, final=False):
        if not self.on_line or not self.chunks or self.place > len(self.chunks):
            return
        k, seq = self.place, self.seq
        count = len(self.chunks)
        has_pair, has_total, has_next = k < count, 1 <= k <= count, k + 1 < count
        shape = self.chunks[0].shape
        ins, names = [], []
        if has_pair:
            ins += [self.chunks[k], self.came]
        if has_total:
            ins += [self.pair, self.over]
        if has_total and has_next:
            ins += [self.chunks[k + 1]]
        ins[0] = seq.then(ins[0])
        outs = int(has_pair) + int(has_total) * (2 if has_next else 1)
        tile = shape[0] // 2

        def kernel(inner_ref, *refs):
            ins_left, outs_left = list(refs[: len(ins)]), list(refs[len(ins) :])

            def plus(one, two):
                return (one[...].astype(jnp.float32) + two[...].astype(jnp.float32)).astype(
                    jnp.bfloat16
                )

            if has_pair:
                outs_left.pop(0)[...] = plus(ins_left.pop(0), ins_left.pop(0))
            if has_total:
                total = plus(ins_left.pop(0), ins_left.pop(0))
                outs_left.pop(0)[...] = total
                if has_next:
                    load_ref, next_ref = outs_left.pop(0), ins_left.pop(0)

                    @pl.when(inner_ref[0] == 1)
                    def send_total():
                        load_ref[...] = total

                    @pl.when(inner_ref[0] != 1)
                    def send_chunk():
                        load_ref[...] = next_ref[...]

        spec = pl.BlockSpec((tile, shape[1]), lambda step: (step, 0))
        made = list(
            pl.pallas_call(
                kernel,
                grid=(2,),
                in_specs=[pl.BlockSpec(memory_space=pltpu.SMEM)] + [spec] * len(ins),
                out_specs=[spec] * outs,
                out_shape=[bf16(*shape)] * outs,
                compiler_params=pltpu.CompilerParams(
                    dimension_semantics=("arbitrary",), vmem_limit_bytes=VMEM_LIMIT
                ),
                cost_estimate=SMALL_COST,
            )(self.inner, *ins)
        )
        seq.mark(made[0])
        if has_pair:
            self.pair = made.pop(0)
            self.over = lax.ppermute(self.pair, "rep", [(1, 2), (2, 1)])
        if has_total:
            self.totals[k - 1] = made.pop(0)
            if has_next:
                self.came = self.outer(made.pop(0), [(0, 1), (1, 0), (2, 3), (3, 2)])
                self.outward[k - 1] = self.came
            else:
                self.outward[k - 1] = self.outer(self.totals[k - 1], [(1, 0), (2, 3)])
        elif has_next:
            self.came = self.outer(self.chunks[k + 1], [(0, 1), (3, 2)])
        self.place += 1

    def finish(self):
        if not self.on_line:
            return [lax.psum(chunk, "rep").astype(jnp.float32) for chunk in self.chunks]
        while self.place <= len(self.chunks):
            self.step()
        return [
            jnp.where(self.inner[0] == 1, self.totals[k], self.outward[k]).astype(jnp.float32)
            for k in range(len(self.chunks))
        ]


def tok_total(values, *needed):
    bit = 1
    while bit < lax.axis_size("tok"):
        if bit == 2 and needed:
            values = after(values, *needed)
        values = values + flip(values, "tok", bit)
        bit *= 2
    return values


def rep_gather(values, needed):
    count = lax.axis_size("rep")
    rank = lax.axis_index("rep")
    pieces = values[None]
    bit = 1
    while bit < count:
        moved = flip(pieces, "rep", bit)
        if needed:
            moved = after(moved, needed.pop(0))
        pieces = jnp.concatenate([pieces, moved], axis=0)
        bit *= 2
    return jnp.stack(
        [
            lax.dynamic_index_in_dim(pieces, jnp.bitwise_xor(rank, place), 0, keepdims=False)
            for place in range(count)
        ]
    )


def product(left, right):
    return jnp.dot(left, right, preferred_element_type=jnp.float32)


def product_back(left, right):
    return lax.dot_general(
        left, right, (((1,), (1,)), ((), ())), preferred_element_type=jnp.float32
    )


def tile_spec(rank, rows, columns):
    if rank == 3:
        return pl.BlockSpec((1, rows, columns), lambda step: (step, 0, 0))
    return pl.BlockSpec((rows, columns), lambda step: (0, step))


def whole_spec(array):
    zeros = (0,) * array.ndim
    return pl.BlockSpec(array.shape, lambda step: zeros, pipeline_mode=pl.Buffered(1))


def tile_of(ref):
    return ref[0] if len(ref.shape) == 3 else ref[...]


def fill(scratch, spot, parts, refs):
    rank, parity = spot[0], spot[1]
    share = parts[0].array.shape[-2]
    for part, ref in zip(parts, refs, strict=True):
        rows = part.array.shape[-2]
        start = jnp.bitwise_xor(rank, part.away) * share
        if part.half is not None:
            start = start + jnp.bitwise_xor(parity, part.half) * rows
        scratch[pl.ds(pl.multiple_of(start, rows), rows), :] = tile_of(ref)


def fill_one(scratch, spot, parts, refs, which):
    rank, parity = spot[0], spot[1]
    share = parts[0].array.shape[-2]
    for part, ref in zip(parts, refs, strict=True):
        start = pl.multiple_of(jnp.bitwise_xor(rank, part.away) * share, share)

        def lay(start=start, ref=ref):
            scratch[pl.ds(start, share), :] = tile_of(ref)

        if part.half is None:
            lay()
        else:
            pl.when(jnp.bitwise_xor(parity, part.half) == which)(lay)


def one_specs(parts, which):
    return [
        pl.BlockSpec(
            (1,) + part.array.shape[1:],
            functools.partial(lambda at, step: (at, 0, 0), which if part.half is None else 0),
        )
        for part in parts
    ]


def put_grad(spot, left_ref, right, keep_ref, send_ref, rows, count):
    rank = spot[0]
    for away in range(count):
        at = pl.ds(pl.multiple_of(jnp.bitwise_xor(rank, away) * rows, rows), rows)
        block = product(left_ref[at, :], right).astype(jnp.bfloat16)
        to = send_ref if away & 1 else keep_ref
        to[away // 2, 0] = block


def grad_specs(count, rows, columns):
    return pl.BlockSpec((count // 2, 1, rows, columns), lambda step: (0, step, 0, 0))


def call(kernel, tiles, spot, arrays, specs, outs, out_specs, scratch):
    return pl.pallas_call(
        kernel,
        grid=(tiles,),
        in_specs=[pl.BlockSpec(memory_space=pltpu.SMEM)] + specs,
        out_specs=out_specs,
        out_shape=outs,
        scratch_shapes=scratch,
        compiler_params=pltpu.CompilerParams(
            dimension_semantics=("arbitrary",), vmem_limit_bytes=VMEM_LIMIT
        ),
        cost_estimate=SMALL_COST,
    )(spot, *arrays)


def bf16(*shape):
    return jax.ShapeDtypeStruct(shape, jnp.bfloat16)


def project(spot, rows_in, parts):
    arrays = [part.array for part in parts]
    tiles, share, columns = arrays[0].shape
    length, width = rows_in.shape

    def kernel(spot_ref, in_ref, *rest):
        refs, out_ref, scratch = rest[:-2], rest[-2], rest[-1]
        fill(scratch, spot_ref, parts, refs)
        out_ref[0] = product(in_ref[...], scratch[...]).astype(jnp.bfloat16)

    return call(
        kernel,
        tiles,
        spot,
        [rows_in] + arrays,
        [whole_spec(rows_in)] + [tile_spec(3, part.shape[1], columns) for part in arrays],
        bf16(tiles, length, columns),
        pl.BlockSpec((1, length, columns), lambda step: (step, 0, 0)),
        [pltpu.VMEM((width, columns), jnp.bfloat16)],
    )


def project_back(spot, rows_in, parts, which, width):
    arrays = [part.array for part in parts]
    columns = arrays[0].shape[-1]
    length = rows_in.shape[0]

    def kernel(spot_ref, in_ref, *rest):
        refs, out_ref, scratch = rest[:-2], rest[-2], rest[-1]
        fill_one(scratch, spot_ref, parts, refs, which)
        out_ref[...] = product_back(in_ref[...], scratch[...]).astype(jnp.bfloat16)

    return call(
        kernel,
        1,
        spot,
        [rows_in] + arrays,
        [whole_spec(rows_in)] + one_specs(parts, which),
        bf16(length, width),
        pl.BlockSpec((length, width), lambda step: (0, 0)),
        [pltpu.VMEM((width, columns), jnp.bfloat16)],
    )


def proj_grads(spot, grad_rows, mixed_rows, parts, which):
    arrays = [part.array for part in parts]
    share, columns = arrays[0].shape[-2:]
    length, width = grad_rows.shape
    count = width // share

    def kernel(spot_ref, grad_ref, mixed_ref, *rest):
        refs, (out_ref, keep_ref, send_ref, scratch, turned) = rest[:-5], rest[-5:]
        fill_one(scratch, spot_ref, parts, refs, which)
        turned[...] = jnp.transpose(grad_ref[...])
        out_ref[...] = product(grad_ref[...], scratch[...]).astype(jnp.bfloat16)
        put_grad(spot_ref, turned, mixed_ref[...], keep_ref, send_ref, share, count)

    half = bf16(count // 2, 1, share, columns)
    return call(
        kernel,
        1,
        spot,
        [grad_rows, mixed_rows] + arrays,
        [whole_spec(grad_rows), whole_spec(mixed_rows)] + one_specs(parts, which),
        (bf16(length, columns), half, half),
        (pl.BlockSpec((length, columns), lambda step: (0, 0)),)
        + (grad_specs(count, share, columns),) * 2,
        [pltpu.VMEM((width, columns), jnp.bfloat16), pltpu.VMEM((width, length), jnp.bfloat16)],
    )


def qkv_grads(spot, hidden, query_grads, block_grads, parts):
    arrays = [part.array for part in parts]
    tiles, share, columns = arrays[0].shape
    length, width = hidden.shape
    count = width // share

    seqs, rows = len(query_grads), query_grads[0].shape[1]

    def kernel(spot_ref, hid_ref, *rest):
        query_refs, block_refs, rest = rest[:seqs], rest[seqs : 2 * seqs], rest[2 * seqs :]
        refs, (out_ref, keep_ref, send_ref, scratch, total, turned, grad) = rest[:-7], rest[-7:]
        step = pl.program_id(0)
        fill(scratch, spot_ref, parts, refs)

        @pl.when(step == 0)
        def first():
            turned[...] = jnp.transpose(hid_ref[...])
            total[...] = jnp.zeros_like(total)
            for at, ref in enumerate(query_refs):
                grad[at * rows : (at + 1) * rows] = ref[0]

        @pl.when(step > 0)
        def later():
            for at, ref in enumerate(block_refs):
                grad[at * rows : (at + 1) * rows] = ref[0]

        total[...] += product_back(grad[...], scratch[...])
        put_grad(spot_ref, turned, grad[...], keep_ref, send_ref, share, count)

        @pl.when(step == tiles - 1)
        def finish():
            out_ref[...] = total[...].astype(jnp.bfloat16)

    half = bf16(count // 2, tiles, share, columns)
    return call(
        kernel,
        tiles,
        spot,
        [hidden, *query_grads] + [block_grads] * seqs + arrays,
        [whole_spec(hidden)]
        + [whole_spec(part) for part in query_grads]
        + [
            pl.BlockSpec(
                (1, rows, columns),
                functools.partial(lambda at, step: (2 * at + jnp.maximum(step - 1, 0), 0, 0), at),
            )
            for at in range(seqs)
        ]
        + [tile_spec(3, part.shape[1], columns) for part in arrays],
        (bf16(length, width), half, half),
        (pl.BlockSpec((length, width), lambda step: (0, 0)),)
        + (grad_specs(count, share, columns),) * 2,
        [
            pltpu.VMEM((width, columns), jnp.bfloat16),
            pltpu.VMEM((length, width), jnp.float32),
            pltpu.VMEM((width, length), jnp.bfloat16),
            pltpu.VMEM((length, columns), jnp.bfloat16),
        ],
    )


def gelu_parts(upward):
    squared = upward * upward
    bent = jnp.tanh(0.7978845608028654 * (upward + 0.044715 * (upward * squared)))
    activ = 0.5 * upward * (1.0 + bent)
    slope = 0.5 * (1.0 + bent) + 0.5 * upward * (1.0 - bent * bent) * (
        0.7978845608028654 * (1.0 + 3 * 0.044715 * squared)
    )
    return activ, slope


def feed_forward(spot, hidden, grad, up_parts, down_parts, columns):
    arrays = [part.array for part in up_parts + down_parts]
    share, units = arrays[0].shape
    tiles = units // columns
    length, width = hidden.shape
    count = width // share

    def kernel(spot_ref, hid_ref, grad_ref, *rest):
        refs, rest = rest[: len(arrays)], rest[len(arrays) :]
        out_ref, back_ref, up_keep, up_send, down_keep, down_send = rest[:6]
        up, down, out_sum, back_sum, hid_turned, grad_turned = rest[6:]
        step = pl.program_id(0)

        @pl.when(step == 0)
        def begin():
            hid_turned[...] = jnp.transpose(hid_ref[...])
            grad_turned[...] = jnp.transpose(grad_ref[...])
            out_sum[...] = jnp.zeros_like(out_sum)
            back_sum[...] = jnp.zeros_like(back_sum)

        fill(up, spot_ref, up_parts, refs[: len(up_parts)])
        fill(down, spot_ref, down_parts, refs[len(up_parts) :])
        activ, slope = gelu_parts(product(hid_ref[...], up[...]))
        activ = activ.astype(jnp.bfloat16)
        upward_grad = (product(grad_ref[...], down[...]) * slope).astype(jnp.bfloat16)
        out_sum[...] += product_back(activ, down[...])
        back_sum[...] += product_back(upward_grad, up[...])
        put_grad(spot_ref, grad_turned, activ, down_keep, down_send, share, count)
        put_grad(spot_ref, hid_turned, upward_grad, up_keep, up_send, share, count)

        @pl.when(step == tiles - 1)
        def finish():
            out_ref[...] = out_sum[...].astype(jnp.bfloat16)
            back_ref[...] = back_sum[...].astype(jnp.bfloat16)

    rows_spec = pl.BlockSpec((length, width), lambda step: (0, 0))
    wholes = [hidden, grad]
    return call(
        kernel,
        tiles,
        spot,
        wholes + arrays,
        [whole_spec(part) for part in wholes]
        + [tile_spec(2, part.shape[0], columns) for part in arrays],
        (bf16(length, width), bf16(length, width))
        + (bf16(count // 2, tiles, share, columns),) * 4,
        (rows_spec, rows_spec) + (grad_specs(count, share, columns),) * 4,
        [pltpu.VMEM((width, columns), jnp.bfloat16)] * 2
        + [pltpu.VMEM((length, width), jnp.float32)] * 2
        + [pltpu.VMEM((width, length), jnp.bfloat16)] * 2,
    )


def activate(seq, first, second):
    shape = first.shape
    tile = shape[1] // 2

    def kernel(first_ref, second_ref, out_ref):
        upward = first_ref[0].astype(jnp.float32) + second_ref[0].astype(jnp.float32)
        activ_grad = first_ref[1].astype(jnp.float32) + second_ref[1].astype(jnp.float32)
        activ, slope = gelu_parts(upward)
        out_ref[0] = activ.astype(jnp.bfloat16)
        out_ref[1] = (activ_grad * slope).astype(jnp.bfloat16)

    spec = pl.BlockSpec((2, tile, shape[2]), lambda step: (0, step, 0))
    return seq.mark(
        pl.pallas_call(
            kernel,
            grid=(2,),
            in_specs=[spec, spec],
            out_specs=spec,
            out_shape=bf16(*shape),
            compiler_params=pltpu.CompilerParams(
                dimension_semantics=("arbitrary",), vmem_limit_bytes=VMEM_LIMIT
            ),
            cost_estimate=SMALL_COST,
        )(seq.then(first), second)
    )


def middle_spread(seq, spot, modul, stream, branch, cot, count):
    seqs, length, width = stream.shape
    share = width // count

    def kernel(spot_ref, mod_ref, x_ref, one_ref, two_ref, cot_ref, *rest):
        outs, hid_all, grad_all = rest[:-2], rest[-2], rest[-1]
        middle = wide(x_ref) + mod_ref[0, 2:3] * (wide(one_ref) + wide(two_ref))
        norm, factor = normed(middle)
        hid_all[...] = (norm * (1.0 + mod_ref[0, 4:5]) + mod_ref[0, 3:4]).astype(jnp.bfloat16)
        grad_all[...] = (mod_ref[0, 5:6] * wide(cot_ref)).astype(jnp.bfloat16)
        for away, out in enumerate(outs):
            at = pl.multiple_of(jnp.bitwise_xor(spot_ref[0], away) * share, LANES)
            out[0, 0] = hid_all[:, pl.ds(at, share)]
            out[1, 0] = grad_all[:, pl.ds(at, share)]

    row_spec = pl.BlockSpec((1, length, width), lambda at: (at, 0, 0))
    made = pl.pallas_call(
        kernel,
        grid=(seqs,),
        in_specs=[
            pl.BlockSpec(memory_space=pltpu.SMEM),
            pl.BlockSpec((1,) + modul.shape[1:], lambda at: (at, 0, 0)),
        ]
        + [row_spec] * 4,
        out_specs=[pl.BlockSpec((2, 1, length, share), lambda at: (0, at, 0, 0))] * count,
        out_shape=[bf16(2, seqs, length, share)] * count,
        scratch_shapes=[pltpu.VMEM((length, width), jnp.bfloat16)] * 2,
        compiler_params=pltpu.CompilerParams(
            dimension_semantics=("arbitrary",), vmem_limit_bytes=VMEM_LIMIT
        ),
        cost_estimate=SMALL_COST,
    )(spot, modul, seq.then(stream), *branch, cot)
    seq.mark(made[0])
    return [part.reshape(2, -1, share) for part in made]


def lay_rows(spot, refs, scratch):
    rows = refs[0].shape[1]
    for away, ref in enumerate(refs):
        at = pl.multiple_of(jnp.bitwise_xor(spot[0], away) * rows, rows)
        scratch[:, pl.ds(at, rows), :] = ref[...]


def spread_up(seq, spot, features, up_shard, down_shard):
    count = len(features)
    rows, share = features[0].shape[1:]
    length = rows * count
    columns = up_shard.shape[1] // count

    def kernel(spot_ref, up_ref, down_ref, *rest):
        refs, (keep_ref, send_ref, rows_in) = rest[:count], rest[count:]

        @pl.when(pl.program_id(0) == 0)
        def begin():
            lay_rows(spot_ref, refs, rows_in)

        upward = product(rows_in[0], up_ref[...]).astype(jnp.bfloat16)
        activ_grad = product(rows_in[1], down_ref[...]).astype(jnp.bfloat16)
        odd = pl.program_id(0) % 2

        @pl.when(odd == 0)
        def keep():
            keep_ref[0, 0], keep_ref[0, 1] = upward, activ_grad

        @pl.when(odd != 0)
        def send():
            send_ref[0, 0], send_ref[0, 1] = upward, activ_grad

    shard_spec = pl.BlockSpec(
        (share, columns), lambda step, spot_ref: (0, jnp.bitwise_xor(spot_ref[0], step))
    )
    out_spec = pl.BlockSpec((1, 2, length, columns), lambda step, spot_ref: (step // 2, 0, 0, 0))
    out = bf16(count // 2, 2, length, columns)
    keep, send = pl.pallas_call(
        kernel,
        grid_spec=pltpu.PrefetchScalarGridSpec(
            num_scalar_prefetch=1,
            grid=(count,),
            in_specs=[shard_spec, shard_spec]
            + [pl.BlockSpec(part.shape, lambda step, spot_ref: (0, 0, 0)) for part in features],
            out_specs=[out_spec, out_spec],
            scratch_shapes=[pltpu.VMEM((2, length, share), jnp.bfloat16)],
        ),
        out_shape=[out, out],
        compiler_params=pltpu.CompilerParams(
            dimension_semantics=("arbitrary",), vmem_limit_bytes=VMEM_LIMIT
        ),
        cost_estimate=SMALL_COST,
    )(spot, up_shard, down_shard, seq.then(features[0]), *features[1:])
    seq.mark(keep)
    return keep, send


def spread_down(spot, features, blocks, up_shard, down_shard):
    count = len(blocks)
    length, columns = blocks[0].shape[1:]
    share, units = up_shard.shape
    rows = length // count

    def kernel(spot_ref, up_ref, down_ref, *rest):
        feature_refs, refs, rest = rest[:count], rest[count : 2 * count], rest[2 * count :]
        outs, (up_grad_ref, down_grad_ref, rows_in, sums) = rest[:count], rest[count:]
        lay_rows(spot_ref, feature_refs, rows_in)
        hid_turned, grad_turned = jnp.transpose(rows_in[0]), jnp.transpose(rows_in[1])
        out_sum = jnp.zeros((length, share), jnp.float32)
        back_sum = jnp.zeros((length, share), jnp.float32)
        for away, ref in enumerate(refs):
            place = jnp.bitwise_xor(spot_ref[0], away)
            at = pl.ds(pl.multiple_of(place * columns, columns), columns)
            activ, upward_grad = ref[0], ref[1]
            out_sum += product_back(activ, down_ref[:, at])
            back_sum += product_back(upward_grad, up_ref[:, at])
            up_grad_ref[place] = product(hid_turned, upward_grad).astype(jnp.bfloat16)
            down_grad_ref[place] = product(grad_turned, activ).astype(jnp.bfloat16)
        sums[0] = back_sum.astype(jnp.bfloat16)
        sums[1] = out_sum.astype(jnp.bfloat16)
        for away, out in enumerate(outs):
            at = pl.multiple_of(jnp.bitwise_xor(spot_ref[0], away) * rows, rows)
            out[...] = sums[:, pl.ds(at, rows), :]

    zeros = lambda step: (0, 0, 0)
    arrays = [up_shard, down_shard] + list(features) + list(blocks)
    *sums, up_grad, down_grad = call(
        kernel,
        1,
        spot,
        arrays,
        [whole_spec(part) for part in arrays],
        (bf16(2, rows, share),) * count + (bf16(count, share, columns),) * 2,
        (pl.BlockSpec((2, rows, share), zeros),) * count
        + (pl.BlockSpec((count, share, columns), zeros),) * 2,
        [pltpu.VMEM((2, length, share), jnp.bfloat16)] * 2,
    )
    return sums, up_grad, down_grad


def gather_features(seq, spot, pieces):
    count = len(pieces)
    rows, share = pieces[0].shape[1:]

    def kernel(spot_ref, *rest):
        refs, outs = rest[:count], rest[count:]
        for away, ref in enumerate(refs):
            at = pl.multiple_of(jnp.bitwise_xor(spot_ref[0], away) * share, LANES)
            for place, out in enumerate(outs):
                out[:, pl.ds(at, share)] = ref[place]

    out_spec = pl.BlockSpec((rows, share * count), lambda step: (0, 0))
    arrays = [seq.then(pieces[0])] + list(pieces[1:])
    made = call(
        kernel,
        1,
        spot,
        arrays,
        [whole_spec(part) for part in arrays],
        (bf16(rows, share * count),) * 2,
        (out_spec, out_spec),
        [],
    )
    seq.mark(made[0])
    return made


def row_kernel(seq, kernel, modul, rows_in, outs):
    seqs, length, width = rows_in[0].shape
    row_spec = pl.BlockSpec((1, length, width), lambda at: (at, 0, 0))
    sum_spec = pl.BlockSpec((1, 8, width), lambda at: (at, 0, 0))
    made = pl.pallas_call(
        kernel,
        grid=(seqs,),
        in_specs=[pl.BlockSpec((1,) + modul.shape[1:], lambda at: (at, 0, 0))]
        + [row_spec] * len(rows_in),
        out_specs=[sum_spec if kind is None else row_spec for kind in outs],
        out_shape=[
            jax.ShapeDtypeStruct((seqs, 8, width), jnp.float32)
            if kind is None
            else jax.ShapeDtypeStruct((seqs, length, width), kind)
            for kind in outs
        ],
        compiler_params=pltpu.CompilerParams(
            dimension_semantics=("arbitrary",), vmem_limit_bytes=VMEM_LIMIT
        ),
        cost_estimate=SMALL_COST,
    )(modul, seq.then(rows_in[0]), *rows_in[1:])
    seq.mark(made[0])
    return made


def wide(ref):
    return ref[0].astype(jnp.float32)


def put_sums(ref, rows):
    ref[0] = jnp.zeros_like(ref[0])
    for place, row in enumerate(rows):
        ref[0, place : place + 1] = jnp.sum(row, axis=0, keepdims=True)


def back_through(values, grad, scale_part):
    norm, factor = normed(values)
    inner = grad * (1.0 + scale_part)
    own = jnp.mean(inner, axis=-1, keepdims=True)
    along = jnp.mean(inner * norm, axis=-1, keepdims=True)
    return (inner - own - norm * along) * factor, norm


def first_hidden(seq, modul, stream):
    def kernel(mod_ref, x_ref, out_ref):
        norm, factor = normed(wide(x_ref))
        out_ref[0] = (norm * (1.0 + mod_ref[0, 1:2]) + mod_ref[0, 0:1]).astype(jnp.bfloat16)

    return row_kernel(seq, kernel, modul, [stream], [jnp.bfloat16])[0]


def middle_hidden(seq, modul, stream, branch, cot):
    def kernel(mod_ref, x_ref, one_ref, two_ref, cot_ref, hid_ref, grad_ref):
        middle = wide(x_ref) + mod_ref[0, 2:3] * (wide(one_ref) + wide(two_ref))
        norm, factor = normed(middle)
        hid_ref[0] = (norm * (1.0 + mod_ref[0, 4:5]) + mod_ref[0, 3:4]).astype(jnp.bfloat16)
        grad_ref[0] = (mod_ref[0, 5:6] * wide(cot_ref)).astype(jnp.bfloat16)

    return row_kernel(seq, kernel, modul, [stream, *branch, cot], [jnp.bfloat16, jnp.bfloat16])


def middle_grads(seq, modul, stream, branch, cot, hidden_grad):
    def kernel(mod_ref, x_ref, one_ref, two_ref, cot_ref, hid_ref, other_ref, mid_out, out, sums):
        branch_sum = wide(one_ref) + wide(two_ref)
        middle = wide(x_ref) + mod_ref[0, 2:3] * branch_sum
        grad = wide(hid_ref) + wide(other_ref)
        through, norm = back_through(middle, grad, mod_ref[0, 4:5])
        mid_grad = wide(cot_ref) + through
        mid_out[0] = mid_grad
        out[0] = (mod_ref[0, 2:3] * mid_grad).astype(jnp.bfloat16)
        put_sums(sums, [mid_grad * branch_sum, grad, grad * norm])

    return row_kernel(
        seq,
        kernel,
        modul,
        [stream, *branch, cot, *hidden_grad],
        [jnp.float32, jnp.bfloat16, None],
    )


def input_grads(seq, modul, stream, mid_grad, hidden_grad):
    def kernel(mod_ref, x_ref, mid_ref, hid_ref, other_ref, out, sums):
        grad = wide(hid_ref) + wide(other_ref)
        through, norm = back_through(wide(x_ref), grad, mod_ref[0, 1:2])
        out[0] = (mid_ref[0] + through).astype(jnp.bfloat16)
        put_sums(sums, [grad, grad * norm])

    return row_kernel(
        seq, kernel, modul, [stream, mid_grad, *hidden_grad], [jnp.bfloat16, None]
    )


def results(seq, modul, stream, branch, second, cot, real):
    def kernel(mod_ref, x_ref, one_ref, two_ref, three_ref, four_ref, cot_ref, out, sums):
        start = wide(x_ref)
        gated_one = mod_ref[0, 2:3] * (wide(one_ref) + wide(two_ref))
        middle = start + gated_one
        branch_two = wide(three_ref) + wide(four_ref)
        gated_two = mod_ref[0, 5:6] * branch_two
        result = middle + gated_two
        out[0] = result.astype(jnp.bfloat16)
        shown = lax.broadcasted_iota(jnp.int32, start.shape, 0) < real
        put_sums(
            sums,
            [wide(cot_ref) * branch_two]
            + [
                jnp.where(shown, member * member, 0.0)
                for member in (start, gated_one, middle, gated_two, result)
            ],
        )

    return row_kernel(
        seq, kernel, modul, [stream, *branch, *second, cot], [jnp.bfloat16, None]
    )


def head_lanes(shape, head):
    lane = lax.broadcasted_iota(jnp.int32, shape, len(shape) - 1)
    return (lane >= head * HD) & (lane < (head + 1) * HD)


def padding(shape, axis, image_rows, text_rows, real, count):
    place = lax.broadcasted_iota(jnp.int32, shape, axis) - image_rows * count
    hidden = (place >= real) & (place < text_rows)
    for other in range(1, count):
        hidden = hidden | (
            (place >= other * text_rows + real) & (place < (other + 1) * text_rows)
        )
    return hidden


def attention_specs(image, text):
    row = [
        pl.BlockSpec((1, rows, LANES), lambda seq, part: (seq, 0, part))
        for rows in (image.shape[1], text.shape[1])
    ]
    block = [
        pl.BlockSpec((2, 1, rows, LANES), lambda seq, part: (0, seq, 0, part))
        for rows in (image.shape[1], text.shape[1])
    ]
    return row, block


def joint(refs, index):
    return jnp.concatenate([ref[index] for ref in refs], axis=0)


def attend(image, text, image_blocks, text_blocks, real):
    seqs, image_rows, width = image.shape
    text_rows = text.shape[1]
    rows = image_rows + text_rows
    count = len(image_blocks)
    keys = rows * count

    def kernel(*rest):
        refs, (image_out, text_out) = rest[:-2], rest[-2:]
        queries = joint(refs[:2], 0)
        key_all = joint(refs[2:], (0, 0))
        value_all = joint(refs[2:], (1, 0))
        hidden = padding((1, keys), 1, image_rows, text_rows, real, count)
        result = jnp.zeros((rows, LANES), jnp.float32)
        for head in range(LANES // HD):
            mine = head_lanes((rows, LANES), head)
            scores = product_back(jnp.where(mine, queries, jnp.zeros_like(queries)), key_all)
            scores = jnp.where(hidden, -1e30, scores * 0.125)
            expd = jnp.exp(scores - jnp.max(scores, axis=1, keepdims=True))
            share = 1.0 / jnp.sum(expd, axis=1, keepdims=True)
            mixed = product((expd * share).astype(jnp.bfloat16), value_all)
            result = jnp.where(mine, mixed, result)
        image_out[0] = result[:image_rows].astype(jnp.bfloat16)
        text_out[0] = result[image_rows:].astype(jnp.bfloat16)

    row, block = attention_specs(image, text)
    return pl.pallas_call(
        kernel,
        grid=(seqs, width // LANES),
        in_specs=row + [block[0]] * count + [block[1]] * count,
        out_specs=row,
        out_shape=[bf16(*image.shape), bf16(*text.shape)],
        compiler_params=pltpu.CompilerParams(
            dimension_semantics=("arbitrary", "arbitrary"), vmem_limit_bytes=VMEM_LIMIT
        ),
        cost_estimate=SMALL_COST,
    )(image, text, *image_blocks, *text_blocks)


def attend_grads(queries_in, grads_in, image_blocks, text_blocks, real, seq):
    image, text = queries_in
    image_rows, width = image.shape[1:]
    text_rows = text.shape[1]
    rows = image_rows + text_rows
    count = len(image_blocks)
    keys = rows * count

    def kernel(*rest):
        refs, (image_out, text_out, keep_ref, send_ref) = rest[:-4], rest[-4:]
        queries = joint(refs[:2], 0)
        grads = joint(refs[2:4], 0)
        key_all = joint(refs[4:], (0, 0))
        value_all = joint(refs[4:], (1, 0))
        hidden = padding((keys, 1), 0, image_rows, text_rows, real, count)
        query_grad = jnp.zeros((rows, LANES), jnp.float32)
        key_grad = jnp.zeros((keys, LANES), jnp.float32)
        value_grad = jnp.zeros((keys, LANES), jnp.float32)
        for head in range(LANES // HD):
            mine = head_lanes((rows, LANES), head)
            own_query = jnp.where(mine, queries, jnp.zeros_like(queries))
            own_grad = jnp.where(mine, grads, jnp.zeros_like(grads))
            scores = product_back(key_all, own_query)
            scores = jnp.where(hidden, -1e30, scores * 0.125)
            expd = jnp.exp(scores - jnp.max(scores, axis=0, keepdims=True))
            probs = expd * (1.0 / jnp.sum(expd, axis=0, keepdims=True))
            prob_grad = product_back(value_all, own_grad)
            delta = jnp.sum(probs * prob_grad, axis=0, keepdims=True)
            score_grad = (probs * (prob_grad - delta)).astype(jnp.bfloat16)
            value_grad += product(probs.astype(jnp.bfloat16), own_grad)
            key_grad += product(score_grad, own_query)
            back = lax.dot_general(
                score_grad, key_all, (((0,), (0,)), ((), ())), preferred_element_type=jnp.float32
            )
            query_grad = jnp.where(mine, back, query_grad)
        query_grad = (query_grad * 0.125).astype(jnp.bfloat16)
        image_out[0] = query_grad[:image_rows]
        text_out[0] = query_grad[image_rows:]
        key_grad = (key_grad * 0.125).astype(jnp.bfloat16)
        value_grad = value_grad.astype(jnp.bfloat16)
        for away in range(count):
            to, place = (send_ref if away & 1 else keep_ref), away // 2
            at = slice(away * image_rows, (away + 1) * image_rows)
            to[place, 0, :image_rows], to[place, 1, :image_rows] = key_grad[at], value_grad[at]
            first = count * image_rows + away * text_rows
            at = slice(first, first + text_rows)
            to[place, 0, image_rows:], to[place, 1, image_rows:] = key_grad[at], value_grad[at]

    def row_spec(length, at):
        return pl.BlockSpec((1, length, LANES), lambda part: (at, 0, part))

    def block_spec(length):
        return pl.BlockSpec((2, 1, length, LANES), lambda part: (0, seq, 0, part))

    def owner_spec(length):
        return pl.BlockSpec((count // 2, 2, length, LANES), lambda part: (0, 0, 0, part))

    sizes = (image_rows, text_rows)
    return pl.pallas_call(
        kernel,
        grid=(width // LANES,),
        in_specs=[row_spec(length, seq) for length in sizes] * 2
        + [block_spec(image_rows)] * count
        + [block_spec(text_rows)] * count,
        out_specs=[row_spec(length, 0) for length in sizes]
        + [owner_spec(rows)] * 2,
        out_shape=[bf16(1, length, width) for length in sizes]
        + [bf16(count // 2, 2, rows, width)] * 2,
        compiler_params=pltpu.CompilerParams(
            dimension_semantics=("arbitrary",), vmem_limit_bytes=VMEM_LIMIT
        ),
        cost_estimate=SMALL_COST,
    )(image, text, *grads_in, *image_blocks, *text_blocks)


def on_device(
    image_tokens,
    text_tokens,
    text_owner,
    conditioning,
    slot_sequence,
    image_w_mod,
    image_b_mod,
    image_w_qkv,
    image_w_proj,
    image_w_up,
    image_w_down,
    text_w_mod,
    text_b_mod,
    text_w_qkv,
    text_w_proj,
    text_w_up,
    text_w_down,
    image_cotangent,
    text_cotangent,
):
    tok_rank = lax.axis_index("tok")
    rep_rank = lax.axis_index("rep")
    rep_count = lax.axis_size("rep")
    tok_count = lax.axis_size("tok")
    seqs, image_rows, width = image_tokens.shape
    text_real = text_cotangent.shape[1]
    text_rows = -(-text_real // 16) * 16
    slots = conditioning.shape[0]
    share = image_w_mod.shape[0]
    heads_width = image_w_qkv.shape[2]
    spot = jnp.stack([tok_rank, lax.rem(rep_rank, 2)]).astype(jnp.int32)

    turn = lambda weight: jnp.transpose(weight, (1, 0, 2))
    chips = Lane("tok", 2)
    proj_stack = jnp.stack([image_w_proj, text_w_proj])
    qkv_held = fetch(turn(image_w_qkv), 1, chips)
    qkv_own, text_own = flip(turn(image_w_qkv), "tok", 1), flip(turn(text_w_qkv), "tok", 1)
    image_qkv_parts, unused = share_out(turn(image_w_qkv), qkv_own, qkv_held)

    picker = (slot_sequence[:, None] == jnp.arange(slots, dtype=jnp.int32)[None, :]).astype(
        jnp.float32
    )
    cond_slots = jnp.dot(picker, conditioning, precision=exact_mode)
    activ_all = jax.nn.silu(cond_slots).astype(jnp.bfloat16)
    activ_group = lax.dynamic_slice_in_dim(activ_all, rep_rank * seqs, seqs, axis=0)
    activ_share = lax.dynamic_slice_in_dim(activ_group, tok_rank * share, share, axis=1)
    both_mod = tok_total(
        jnp.stack(
            [
                jnp.einsum("sd,dke->ske", activ_share, weight, preferred_element_type=jnp.float32)
                for weight in (image_w_mod, text_w_mod)
            ]
        ),
        *qkv_held.values(),
    )
    image_mod = both_mod[0] + image_b_mod.astype(jnp.float32)[None]
    text_mod = both_mod[1] + text_b_mod.astype(jnp.float32)[None]

    text_held = fetch(turn(text_w_qkv), 1, chips, (both_mod,))
    cores = Lane("tok", 1)
    up_own = cores.flip(after(image_w_up, both_mod), 1)
    down_own = cores.flip(after(image_w_down, both_mod), 1)
    proj_held = fetch(proj_stack, 0, chips, tuple(text_held.values()))

    owned = (text_owner == tok_rank).astype(jnp.float32)
    total_text = text_owner.shape[1]
    before = jnp.dot(
        owned,
        jnp.triu(jnp.ones((total_text, total_text), jnp.float32), 1),
        precision=exact_mode,
    )
    chosen = (
        (before[:, None, :] == jnp.arange(text_rows, dtype=jnp.float32)[None, :, None])
        & (owned[:, None, :] > 0.5)
    ).astype(jnp.bfloat16)
    text_input = jnp.einsum(
        "srt,std->srd", chosen, text_tokens, preferred_element_type=jnp.float32
    ).astype(jnp.bfloat16)
    text_cot = jnp.pad(text_cotangent, ((0, 0), (0, text_rows - text_real), (0, 0)))

    seq = Sequence()
    flat = lambda values: values.reshape(-1, values.shape[-1])
    by_seq = lambda values: values.reshape(values.shape[:-2] + (seqs, -1, values.shape[-1]))
    both = lambda pair: tuple(by_seq(part) for part in pair)
    heads = lambda partial: both(head_pair(partial))

    image_hid_one = flat(first_hidden(seq, image_mod, image_tokens))
    image_qkv = seq.mark(
        project(
            spot,
            after(seq.then(image_hid_one), *text_held.values(), up_own, down_own),
            image_qkv_parts,
        )
    )
    text_qkv_parts, text_swapped = share_out(
        turn(text_w_qkv), text_own, text_held, (image_qkv,)
    )
    text_hid_one = flat(first_hidden(seq, text_mod, after(text_input, *proj_held.values())))
    text_qkv = project(spot, seq.then(text_hid_one), text_qkv_parts)
    image_blocks = gather_blocks(
        after(by_seq(image_qkv[1:]), *proj_held.values()), chips, (text_qkv,)
    )
    text_blocks = gather_blocks(by_seq(text_qkv[1:]), chips)
    proj_own = flip(after(proj_stack, image_qkv), "tok", 1)
    seq.mark(text_qkv, proj_own)
    proj_parts, unused = share_out(
        proj_stack, proj_own, proj_held, (text_qkv,), (image_qkv,)
    )
    up_held = fetch(image_w_up, 0, chips)
    down_held = fetch(image_w_down, 0, chips)
    image_query, text_query = by_seq(image_qkv[0]), by_seq(text_qkv[0])
    image_mix, text_mix = attend(
        image_query, seq.then(text_query), image_blocks, text_blocks, text_real
    )
    seq.mark(image_mix, *up_held.values())
    image_mixed, text_mixed = flat(image_mix), flat(text_mix)
    text_out = seq.mark(project_back(spot, seq.then(text_mixed), proj_parts, 1, width))
    text_branch = heads(text_out)
    image_up_parts, up_swapped = share_out(image_w_up, up_own, up_held)
    image_down_parts, down_swapped = share_out(image_w_down, down_own, down_held)
    image_out = project_back(spot, seq.then(image_mixed), proj_parts, 0, width)
    seq.mark(image_out, *down_held.values())
    if lax.axis_size("head") == 2:
        image_branch = both((image_out, flip(after(image_out, text_branch[1]), "head", 1)))
    else:
        image_branch = heads(image_out)

    text_features = exchange(
        middle_spread(seq, spot, text_mod, text_input, text_branch, text_cot, tok_count)
    )
    image_hid_two, image_db_two = middle_hidden(
        seq, image_mod, image_tokens, image_branch, image_cotangent
    )
    seq.mark(image_hid_two, *up_swapped, *down_swapped)
    text_keep, text_send = spread_up(seq, spot, text_features, text_w_up, text_w_down)
    text_pieces = core_sums(seq, text_keep, flip(text_send, "tok", 1))
    text_stays, text_came = chip_moves(seq, text_pieces, chips)
    image_part, image_back, image_up_keep, image_up_send, image_down_keep, image_down_send = (
        feed_forward(
            spot,
            seq.then(flat(image_hid_two)),
            flat(image_db_two),
            image_up_parts,
            image_down_parts,
            heads_width,
        )
    )
    seq.mark(image_back)
    shape = (2,) + text_keep.shape[2:]
    text_act = activate(seq, text_stays.reshape(shape), text_came.reshape(shape))
    text_lane = chips
    image_hid_grad = heads(after(image_back, text_act))
    image_down_send = after(image_down_send, text_act)
    image_up_send = after(image_up_send, text_act)
    chips = Lane("tok", 3)
    image_down_pieces = core_sums(seq, image_down_keep, flip(image_down_send, "tok", 1))
    image_up_pieces = core_sums(seq, image_up_keep, flip(image_up_send, "tok", 1))
    text_active = gather_blocks(text_act, text_lane, (image_up_pieces[0],))
    text_sums, text_up_grad, text_down_grad = spread_down(
        spot,
        [seq.then(text_features[0])] + text_features[1:],
        text_active,
        text_w_up,
        text_w_down,
    )
    seq.mark(text_sums[0])
    text_back_pieces = exchange(text_sums)
    behind = lambda pieces: {
        away: after(part, text_sums[0]) if away else part for away, part in pieces.items()
    }
    image_down_pair = chip_moves(seq, behind(image_down_pieces), chips)
    image_up_pair = chip_moves(seq, behind(image_up_pieces), chips)
    line = Line(seq)
    if line.on_line:
        for whole in (text_down_grad, text_up_grad):
            for place in range(2):
                line.add(flat(whole.reshape(2, -1, share, whole.shape[-1])[place]))
        text_totals = None
    else:
        text_totals = [lax.psum(part, "rep") for part in (text_down_grad, text_up_grad)]

    image_mid_grad, image_db_one, image_mid_sums = middle_grads(
        seq, image_mod, image_tokens, image_branch, image_cotangent, image_hid_grad
    )
    text_back, text_part = gather_features(seq, spot, text_back_pieces)
    text_hid_grad = heads(text_back)
    image_mixed_grad, image_proj_keep, image_proj_send = proj_grads(
        spot, seq.then(flat(image_db_one)), image_mixed, proj_parts, 0
    )
    seq.mark(image_mixed_grad)
    text_mid_grad, text_db_one, text_mid_sums = middle_grads(
        seq, text_mod, text_input, text_branch, text_cot, text_hid_grad
    )
    text_mixed_grad, text_proj_keep, text_proj_send = proj_grads(
        spot, seq.then(flat(text_db_one)), text_mixed, proj_parts, 1
    )
    seq.mark(text_mixed_grad)
    line.step()
    proj_pieces = [
        core_sums(seq, keep, flip(send, "tok", 1))
        for keep, send in ((image_proj_keep, image_proj_send), (text_proj_keep, text_proj_send))
    ]
    made_grads, moved_grads = [], []
    mix_grads = (by_seq(image_mixed_grad), by_seq(text_mixed_grad))
    for at in range(seqs):
        made = attend_grads(
            (image_query, text_query),
            (seq.then(mix_grads[0]), mix_grads[1]),
            image_blocks,
            text_blocks,
            text_real,
            at,
        )
        made_grads.append(made)
        seq.mark(made[0])
        if at == 0 or at == seqs - 1:
            for part in add_blocks(seq, *(image_up_pair if at else image_down_pair), 2):
                line.add(part)
        if at == 0 and seqs == 1:
            for part in add_blocks(seq, *image_up_pair, 2):
                line.add(part)
        line.step()
        moved_grads.append(flip(after(made[3], *seq.last), "tok", 1))
    block_move = chip_moves(
        seq, core_sums_joined(seq, [made[2] for made in made_grads], moved_grads), chips
    )
    line.step()
    tail, text_tail = Line(seq), Line(seq)
    block_grads = add_split(seq, *block_move, 2 * seqs, image_rows)
    proj_pairs = [chip_moves(seq, pieces, chips) for pieces in proj_pieces]
    image_in_part, image_qkv_keep, image_qkv_send = qkv_grads(
        spot,
        seq.then(image_hid_one),
        [made[0] for made in made_grads],
        block_grads[0],
        image_qkv_parts,
    )
    seq.mark(image_in_part)
    line.step()
    text_in_part, text_qkv_keep, text_qkv_send = qkv_grads(
        spot,
        seq.then(text_hid_one),
        [made[1] for made in made_grads],
        block_grads[1],
        text_qkv_parts,
    )
    seq.mark(text_in_part)
    qkv_pairs = [
        chip_moves(seq, core_sums(seq, keep, flip(send, "tok", 1)), chips)
        for keep, send in ((image_qkv_keep, image_qkv_send), (text_qkv_keep, text_qkv_send))
    ]
    line.step()
    image_in_grad = heads(image_in_part)
    text_in_grad = heads(text_in_part)
    image_proj_share, text_proj_share = [add_blocks(seq, *pair, 1)[0] for pair in proj_pairs]
    line.step()
    image_grad, image_in_sums = input_grads(
        seq, image_mod, image_tokens, image_mid_grad, image_in_grad
    )
    text_grad, text_in_sums = input_grads(
        seq, text_mod, text_input, text_mid_grad, text_in_grad
    )
    text_second = heads(after(text_part, image_in_sums))
    image_second = heads(after(image_part, image_in_sums))
    image_qkv_shares = add_blocks(seq, *qkv_pairs[0], 3)
    line.step()
    text_qkv_shares = add_blocks(seq, *qkv_pairs[1], 3)
    line.step()
    for part in (image_proj_share, *image_qkv_shares):
        tail.add(part)
    for part in (text_proj_share, *text_qkv_shares):
        text_tail.add(part)
    text_result, text_out_sums = results(
        seq, text_mod, text_input, text_branch, text_second, text_cot, text_real
    )
    image_result, image_out_sums = results(
        seq, image_mod, image_tokens, image_branch, image_second, image_cotangent, image_rows
    )
    line.step()
    line_sums = line.finish()
    for at in range(len(tail.chunks) + 1):
        tail.step()
        text_tail.step()
    tail_sums = tail.finish()
    text_tail_sums = text_tail.finish()
    columns_of = lambda parts: jnp.concatenate(
        [
            column.astype(jnp.float32)
            for part in parts
            for column in part.reshape(-1, share, part.shape[-1])
        ],
        axis=1,
    )
    if text_totals is None:
        text_totals = [jnp.concatenate(line_sums[at : at + 2]) for at in (0, 2)]
        text_totals = [part.reshape(tok_count, share, -1) for part in text_totals]
        line_sums = line_sums[4:]
    text_down_sum, text_up_sum = [columns_of([part]) for part in text_totals]
    image_down_sum, image_up_sum = columns_of(line_sums[:2]), columns_of(line_sums[2:])
    image_proj_sum, text_proj_sum = tail_sums[0], text_tail_sums[0]
    image_qkv_sum = jnp.stack(tail_sums[1:], axis=1)
    text_qkv_sum = jnp.stack(text_tail_sums[1:], axis=1)

    early = jnp.stack(
        [
            jnp.concatenate([mid_sums[:, :3], out_sums[:, :1]], axis=1)
            for mid_sums, out_sums in (
                (image_mid_sums, image_out_sums),
                (text_mid_sums, text_out_sums),
            )
        ]
    )
    late = jnp.stack([image_in_sums[:, :2], text_in_sums[:, :2]])
    squares = jnp.concatenate(
        [jnp.sum(out_sums[:, 1:6], axis=(0, 2)) for out_sums in (image_out_sums, text_out_sums)]
    )
    square_row = jnp.pad(squares, (0, width - 10))[None]
    all_sums = jnp.concatenate(
        [early.reshape(-1, width), late.reshape(-1, width), square_row], axis=0
    )
    waits = []
    if line.on_line:
        waits = [tail.totals[0], tail.totals[2]]
    all_sums = rep_gather(tok_total(all_sums), waits)
    square_total = jnp.sum(all_sums[:, -1, :10], axis=0)
    early_table = jnp.moveaxis(
        all_sums[:, : 8 * seqs].reshape(rep_count, 2, seqs, 4, width), 0, 1
    ).reshape(2, slots, 4, width)
    late_table = jnp.moveaxis(
        all_sums[:, 8 * seqs : -1].reshape(rep_count, 2, seqs, 2, width), 0, 1
    ).reshape(2, slots, 2, width)
    mod_sum = jnp.concatenate([late_table, early_table], axis=2)

    activ_rows = lax.dynamic_slice_in_dim(activ_all, tok_rank * share, share, axis=1).astype(
        jnp.float32
    )
    image_g_mod = jnp.einsum("sd,ske->dke", activ_rows, mod_sum[0], precision=lax.Precision.HIGH)
    text_g_mod = jnp.einsum("sd,ske->dke", activ_rows, mod_sum[1], precision=lax.Precision.HIGH)
    image_g_bmod = jnp.sum(mod_sum[0], axis=0)
    text_g_bmod = jnp.sum(mod_sum[1], axis=0)
    activ_grad = jnp.einsum(
        "ske,dke->sd", mod_sum[0], image_w_mod.astype(jnp.float32), precision=exact_mode
    ) + jnp.einsum("ske,dke->sd", mod_sum[1], text_w_mod.astype(jnp.float32), precision=exact_mode)
    cond_rows = lax.dynamic_slice_in_dim(cond_slots, tok_rank * share, share, axis=1)
    unused_value, silu_back = jax.vjp(jax.nn.silu, cond_rows)
    slot_grad = silu_back(activ_grad)[0]
    cond_grad = jnp.dot(jnp.transpose(picker), slot_grad, precision=exact_mode)
    image_count = float(slots * image_rows * tok_count * width)
    text_count = float(slots * text_real * tok_count * width)
    counts = jnp.concatenate(
        [jnp.full((5,), image_count, jnp.float32), jnp.full((5,), text_count, jnp.float32)]
    )
    stream_rms = jnp.sqrt(square_total / counts)
    return (
        image_result,
        text_result[:, :text_real],
        image_grad,
        text_grad[:, :text_real],
        cond_grad,
        image_g_mod,
        image_g_bmod,
        image_qkv_sum,
        image_proj_sum,
        image_up_sum,
        image_down_sum,
        text_g_mod,
        text_g_bmod,
        text_qkv_sum,
        text_proj_sum,
        text_up_sum,
        text_down_sum,
        stream_rms,
    )


def solution(mesh):
    in_specs = (
        P("rep", "tok", None),
        P("rep", None, None),
        P("rep", None),
        P(),
        P(),
        P("tok", None, None),
        P(),
        P("tok", None, "head"),
        P("tok", "head"),
        P("tok", "head"),
        P("tok", "head"),
        P("tok", None, None),
        P(),
        P("tok", None, "head"),
        P("tok", "head"),
        P("tok", "head"),
        P("tok", "head"),
        P("rep", "tok", None),
        P("rep", "tok", None),
    )
    out_specs = (
        P("rep", "tok", None),
        P("rep", "tok", None),
        P("rep", "tok", None),
        P("rep", "tok", None),
        P(None, "tok"),
        P("tok", None, None),
        P(),
        P("tok", None, "head"),
        P("tok", "head"),
        P("tok", "head"),
        P("tok", "head"),
        P("tok", None, None),
        P(),
        P("tok", None, "head"),
        P("tok", "head"),
        P("tok", "head"),
        P("tok", "head"),
        P(),
    )
    return jax.shard_map(
        on_device, mesh=mesh, in_specs=in_specs, out_specs=out_specs, check_vma=False
    )
```

```python
import functools

import jax
import jax.numpy as jnp
from jax import lax
from jax.experimental import pallas as pl
from jax.experimental.pallas import tpu as pltpu
from jax.sharding import PartitionSpec as P

HD = 64
LANES = 128
VMEM_LIMIT = 60 * 1024 * 1024
SMALL_COST = pl.CostEstimate(flops=1024, bytes_accessed=1024, transcendentals=0)

exact_mode = lax.Precision.HIGHEST


def normed(values):
    centered = values - jnp.mean(values, axis=-1, keepdims=True)
    scale = lax.rsqrt(jnp.mean(centered * centered, axis=-1, keepdims=True) + 1e-06)
    return centered * scale, scale


def flip(values, axis, bit):
    return lax.ppermute(
        values, axis, [(place, place ^ bit) for place in range(lax.axis_size(axis))]
    )


def head_pair(partial):
    if lax.axis_size("head") != 2:
        return lax.psum(partial, "head"), jnp.zeros_like(partial)
    return partial, flip(partial, "head", 1)


def after(values, *needed):
    return lax.optimization_barrier((values, *needed))[0]


class Sequence:
    def __init__(self):
        self.last = None

    def then(self, values):
        return values if self.last is None else after(values, *self.last)

    def mark(self, output, *moves):
        self.last = (output, *moves)
        return output


class Lane:
    def __init__(self, axis, depth):
        self.axis, self.depth, self.over = axis, depth, []

    def flip(self, values, bit):
        if len(self.over) >= self.depth:
            values = after(values, self.over[-self.depth])
        moved = flip(values, self.axis, bit)
        self.over.append(moved)
        return moved


class Part:
    def __init__(self, away, half, array):
        self.away, self.half, self.array = away, half, array


def fetch(weight, axis, lane, needed=()):
    parity = lax.rem(lax.axis_index("rep"), 2)
    size = weight.shape[axis] // 2
    held = {0: lax.dynamic_slice_in_dim(weight, parity * size, size, axis=axis)}
    if needed:
        held[0] = after(held[0], *needed)
    bit = lax.axis_size("tok") // 2
    while bit > 1:
        for away, array in list(held.items()):
            held[away ^ bit] = lane.flip(array, bit)
        bit //= 2
    del held[0]
    return held


def share_out(weight, own, held, needed=(), first=()):
    parts = []
    for away, array in held.items():
        leaving = after(array, *first) if first else array
        parts += [Part(away, 0, array), Part(away, 1, flip(leaving, "rep", 1))]
    others = [
        Part(
            part.away ^ 1,
            part.half,
            flip(after(part.array, *needed) if needed else part.array, "tok", 1),
        )
        for part in parts
    ]
    swapped = [part.array for part in parts if part.half == 1]
    return [Part(0, None, weight)] + parts + [Part(1, None, own)] + others, swapped


def gather_blocks(values, lane, needed=()):
    pieces = {0: values}
    bit = lax.axis_size("tok") // 2
    while bit > 0:
        for away, part in list(pieces.items()):
            if bit > 1:
                pieces[away ^ bit] = lane.flip(part, bit)
            else:
                part = after(part, *needed) if away and needed else part
                pieces[away ^ bit] = flip(part, "tok", bit)
        bit //= 2
    return [pieces[away] for away in range(len(pieces))]


def add_blocks(seq, first, second, outputs, kind=jnp.bfloat16):
    width = first.shape[-1]
    flat = lambda values: values.reshape(outputs, -1, width)
    first, second = flat(seq.then(first)), flat(second)
    rows = first.shape[1]
    tile = rows // 2

    def kernel(first_ref, second_ref, *out_refs):
        for place, out_ref in enumerate(out_refs):
            out_ref[...] = (
                first_ref[place].astype(jnp.float32) + second_ref[place].astype(jnp.float32)
            ).astype(kind)

    in_spec = pl.BlockSpec((outputs, tile, width), lambda step: (0, step, 0))
    sums = pl.pallas_call(
        kernel,
        grid=(2,),
        in_specs=[in_spec, in_spec],
        out_specs=[pl.BlockSpec((tile, width), lambda step: (step, 0))] * outputs,
        out_shape=[jax.ShapeDtypeStruct((rows, width), kind)] * outputs,
        compiler_params=pltpu.CompilerParams(
            dimension_semantics=("arbitrary",), vmem_limit_bytes=VMEM_LIMIT
        ),
        cost_estimate=SMALL_COST,
    )(first, second)
    seq.mark(sums[0])
    return sums


def core_sums(seq, keep, moved):
    sums = add_blocks(seq, keep, moved, keep.shape[0])
    return {2 * place: part for place, part in enumerate(sums)}


def core_sums_joined(seq, keeps, moved):
    pieces, pair, rows, width = keeps[0].shape
    pairs = len(keeps)

    def kernel(*refs):
        for at in range(pairs):
            for place in range(pieces):
                refs[2 * pairs + place][at] = (
                    refs[at][place].astype(jnp.float32)
                    + refs[pairs + at][place].astype(jnp.float32)
                ).astype(jnp.bfloat16)

    spec = pl.BlockSpec((pieces, 1, rows, width), lambda step: (0, step, 0, 0))
    sums = pl.pallas_call(
        kernel,
        grid=(pair,),
        in_specs=[spec] * (2 * pairs),
        out_specs=[pl.BlockSpec((pairs, 1, rows, width), lambda step: (0, step, 0, 0))] * pieces,
        out_shape=[bf16(pairs, pair, rows, width)] * pieces,
        compiler_params=pltpu.CompilerParams(
            dimension_semantics=("arbitrary",), vmem_limit_bytes=VMEM_LIMIT
        ),
        cost_estimate=SMALL_COST,
    )(seq.then(keeps[0]), *keeps[1:], *moved)
    seq.mark(sums[0])
    return {2 * place: part.reshape(-1, width) for place, part in enumerate(sums)}


def add_split(seq, first, second, groups, top):
    width = first.shape[-1]
    first, second = seq.then(first).reshape(groups, -1, width), second.reshape(groups, -1, width)
    rows = first.shape[1]

    def kernel(first_ref, second_ref, top_ref, bottom_ref):
        total = (first_ref[0].astype(jnp.float32) + second_ref[0].astype(jnp.float32)).astype(
            jnp.bfloat16
        )
        top_ref[0], bottom_ref[0] = total[:top], total[top:]

    spec = lambda length: pl.BlockSpec((1, length, width), lambda step: (step, 0, 0))
    parts = pl.pallas_call(
        kernel,
        grid=(groups,),
        in_specs=[spec(rows), spec(rows)],
        out_specs=[spec(top), spec(rows - top)],
        out_shape=[bf16(groups, top, width), bf16(groups, rows - top, width)],
        compiler_params=pltpu.CompilerParams(
            dimension_semantics=("arbitrary",), vmem_limit_bytes=VMEM_LIMIT
        ),
        cost_estimate=SMALL_COST,
    )(first, second)
    seq.mark(parts[0])
    return parts


def chip_moves(seq, pieces, lane):
    bit = 2
    while 2 * bit < lax.axis_size("tok"):
        pieces = {
            away: add_blocks(seq, part, lane.flip(pieces[away | bit], bit), 1)[0]
            for away, part in pieces.items()
            if not away & bit
        }
        bit *= 2
    if bit >= lax.axis_size("tok"):
        return pieces[0], jnp.zeros_like(pieces[0])
    return pieces[0], lane.flip(pieces[bit], bit)


def exchange(pieces):
    return [pieces[0]] + [flip(part, "tok", 1 + place) for place, part in enumerate(pieces[1:])]


class Line:
    def __init__(self, seq):
        self.seq = seq
        self.on_line = lax.axis_size("rep") == 4
        rank = lax.axis_index("rep")
        self.inner = ((rank == 1) | (rank == 2)).astype(jnp.int32).reshape(1)
        self.chunks, self.totals, self.outward = [], {}, {}
        self.place = 0
        self.came, self.pair, self.over = None, None, None

    def outer(self, load, pairs):
        return lax.ppermute(load, "rep", pairs)

    def add(self, chunk):
        self.chunks.append(chunk)
        if self.on_line and len(self.chunks) == 1:
            self.came = self.outer(chunk, [(0, 1), (3, 2)])

    def step(self, final=False):
        if not self.on_line or not self.chunks or self.place > len(self.chunks):
            return
        k, seq = self.place, self.seq
        count = len(self.chunks)
        has_pair, has_total, has_next = k < count, 1 <= k <= count, k + 1 < count
        shape = self.chunks[0].shape
        ins, names = [], []
        if has_pair:
            ins += [self.chunks[k], self.came]
        if has_total:
            ins += [self.pair, self.over]
        if has_total and has_next:
            ins += [self.chunks[k + 1]]
        ins[0] = seq.then(ins[0])
        outs = int(has_pair) + int(has_total) * (2 if has_next else 1)
        tile = shape[0] // 2

        def kernel(inner_ref, *refs):
            ins_left, outs_left = list(refs[: len(ins)]), list(refs[len(ins) :])

            def plus(one, two):
                return (one[...].astype(jnp.float32) + two[...].astype(jnp.float32)).astype(
                    jnp.bfloat16
                )

            if has_pair:
                outs_left.pop(0)[...] = plus(ins_left.pop(0), ins_left.pop(0))
            if has_total:
                total = plus(ins_left.pop(0), ins_left.pop(0))
                outs_left.pop(0)[...] = total
                if has_next:
                    load_ref, next_ref = outs_left.pop(0), ins_left.pop(0)

                    @pl.when(inner_ref[0] == 1)
                    def send_total():
                        load_ref[...] = total

                    @pl.when(inner_ref[0] != 1)
                    def send_chunk():
                        load_ref[...] = next_ref[...]

        spec = pl.BlockSpec((tile, shape[1]), lambda step: (step, 0))
        made = list(
            pl.pallas_call(
                kernel,
                grid=(2,),
                in_specs=[pl.BlockSpec(memory_space=pltpu.SMEM)] + [spec] * len(ins),
                out_specs=[spec] * outs,
                out_shape=[bf16(*shape)] * outs,
                compiler_params=pltpu.CompilerParams(
                    dimension_semantics=("arbitrary",), vmem_limit_bytes=VMEM_LIMIT
                ),
                cost_estimate=SMALL_COST,
            )(self.inner, *ins)
        )
        seq.mark(made[0])
        if has_pair:
            self.pair = made.pop(0)
            self.over = lax.ppermute(self.pair, "rep", [(1, 2), (2, 1)])
        if has_total:
            self.totals[k - 1] = made.pop(0)
            if has_next:
                self.came = self.outer(made.pop(0), [(0, 1), (1, 0), (2, 3), (3, 2)])
                self.outward[k - 1] = self.came
            else:
                self.outward[k - 1] = self.outer(self.totals[k - 1], [(1, 0), (2, 3)])
        elif has_next:
            self.came = self.outer(self.chunks[k + 1], [(0, 1), (3, 2)])
        self.place += 1

    def finish(self):
        if not self.on_line:
            return [lax.psum(chunk, "rep").astype(jnp.float32) for chunk in self.chunks]
        while self.place <= len(self.chunks):
            self.step()
        return [
            jnp.where(self.inner[0] == 1, self.totals[k], self.outward[k]).astype(jnp.float32)
            for k in range(len(self.chunks))
        ]


def tok_total(values, *needed):
    bit = 1
    while bit < lax.axis_size("tok"):
        if bit == 2 and needed:
            values = after(values, *needed)
        values = values + flip(values, "tok", bit)
        bit *= 2
    return values


def rep_gather(values, needed):
    count = lax.axis_size("rep")
    rank = lax.axis_index("rep")
    pieces = values[None]
    bit = 1
    while bit < count:
        moved = flip(pieces, "rep", bit)
        if needed:
            moved = after(moved, needed.pop(0))
        pieces = jnp.concatenate([pieces, moved], axis=0)
        bit *= 2
    return jnp.stack(
        [
            lax.dynamic_index_in_dim(pieces, jnp.bitwise_xor(rank, place), 0, keepdims=False)
            for place in range(count)
        ]
    )


def product(left, right):
    return jnp.dot(left, right, preferred_element_type=jnp.float32)


def product_back(left, right):
    return lax.dot_general(
        left, right, (((1,), (1,)), ((), ())), preferred_element_type=jnp.float32
    )


def tile_spec(rank, rows, columns):
    if rank == 3:
        return pl.BlockSpec((1, rows, columns), lambda step: (step, 0, 0))
    return pl.BlockSpec((rows, columns), lambda step: (0, step))


def whole_spec(array):
    zeros = (0,) * array.ndim
    return pl.BlockSpec(array.shape, lambda step: zeros, pipeline_mode=pl.Buffered(1))


def tile_of(ref):
    return ref[0] if len(ref.shape) == 3 else ref[...]


def fill(scratch, spot, parts, refs):
    rank, parity = spot[0], spot[1]
    share = parts[0].array.shape[-2]
    for part, ref in zip(parts, refs, strict=True):
        rows = part.array.shape[-2]
        start = jnp.bitwise_xor(rank, part.away) * share
        if part.half is not None:
            start = start + jnp.bitwise_xor(parity, part.half) * rows
        scratch[pl.ds(pl.multiple_of(start, rows), rows), :] = tile_of(ref)


def fill_one(scratch, spot, parts, refs, which):
    rank, parity = spot[0], spot[1]
    share = parts[0].array.shape[-2]
    for part, ref in zip(parts, refs, strict=True):
        start = pl.multiple_of(jnp.bitwise_xor(rank, part.away) * share, share)

        def lay(start=start, ref=ref):
            scratch[pl.ds(start, share), :] = tile_of(ref)

        if part.half is None:
            lay()
        else:
            pl.when(jnp.bitwise_xor(parity, part.half) == which)(lay)


def one_specs(parts, which):
    return [
        pl.BlockSpec(
            (1,) + part.array.shape[1:],
            functools.partial(lambda at, step: (at, 0, 0), which if part.half is None else 0),
        )
        for part in parts
    ]


def put_grad(spot, left_ref, right, keep_ref, send_ref, rows, count):
    rank = spot[0]
    for away in range(count):
        at = pl.ds(pl.multiple_of(jnp.bitwise_xor(rank, away) * rows, rows), rows)
        block = product(left_ref[at, :], right).astype(jnp.bfloat16)
        to = send_ref if away & 1 else keep_ref
        to[away // 2, 0] = block


def grad_specs(count, rows, columns):
    return pl.BlockSpec((count // 2, 1, rows, columns), lambda step: (0, step, 0, 0))


def call(kernel, tiles, spot, arrays, specs, outs, out_specs, scratch):
    return pl.pallas_call(
        kernel,
        grid=(tiles,),
        in_specs=[pl.BlockSpec(memory_space=pltpu.SMEM)] + specs,
        out_specs=out_specs,
        out_shape=outs,
        scratch_shapes=scratch,
        compiler_params=pltpu.CompilerParams(
            dimension_semantics=("arbitrary",), vmem_limit_bytes=VMEM_LIMIT
        ),
        cost_estimate=SMALL_COST,
    )(spot, *arrays)


def bf16(*shape):
    return jax.ShapeDtypeStruct(shape, jnp.bfloat16)


def project(spot, rows_in, parts):
    arrays = [part.array for part in parts]
    tiles, share, columns = arrays[0].shape
    length, width = rows_in.shape

    def kernel(spot_ref, in_ref, *rest):
        refs, out_ref, scratch = rest[:-2], rest[-2], rest[-1]
        fill(scratch, spot_ref, parts, refs)
        out_ref[0] = product(in_ref[...], scratch[...]).astype(jnp.bfloat16)

    return call(
        kernel,
        tiles,
        spot,
        [rows_in] + arrays,
        [whole_spec(rows_in)] + [tile_spec(3, part.shape[1], columns) for part in arrays],
        bf16(tiles, length, columns),
        pl.BlockSpec((1, length, columns), lambda step: (step, 0, 0)),
        [pltpu.VMEM((width, columns), jnp.bfloat16)],
    )


def project_back(spot, rows_in, parts, which, width):
    arrays = [part.array for part in parts]
    columns = arrays[0].shape[-1]
    length = rows_in.shape[0]

    def kernel(spot_ref, in_ref, *rest):
        refs, out_ref, scratch = rest[:-2], rest[-2], rest[-1]
        fill_one(scratch, spot_ref, parts, refs, which)
        out_ref[...] = product_back(in_ref[...], scratch[...]).astype(jnp.bfloat16)

    return call(
        kernel,
        1,
        spot,
        [rows_in] + arrays,
        [whole_spec(rows_in)] + one_specs(parts, which),
        bf16(length, width),
        pl.BlockSpec((length, width), lambda step: (0, 0)),
        [pltpu.VMEM((width, columns), jnp.bfloat16)],
    )


def proj_grads(spot, grad_rows, mixed_rows, parts, which):
    arrays = [part.array for part in parts]
    share, columns = arrays[0].shape[-2:]
    length, width = grad_rows.shape
    count = width // share

    def kernel(spot_ref, grad_ref, mixed_ref, *rest):
        refs, (out_ref, keep_ref, send_ref, scratch, turned) = rest[:-5], rest[-5:]
        fill_one(scratch, spot_ref, parts, refs, which)
        turned[...] = jnp.transpose(grad_ref[...])
        out_ref[...] = product(grad_ref[...], scratch[...]).astype(jnp.bfloat16)
        put_grad(spot_ref, turned, mixed_ref[...], keep_ref, send_ref, share, count)

    half = bf16(count // 2, 1, share, columns)
    return call(
        kernel,
        1,
        spot,
        [grad_rows, mixed_rows] + arrays,
        [whole_spec(grad_rows), whole_spec(mixed_rows)] + one_specs(parts, which),
        (bf16(length, columns), half, half),
        (pl.BlockSpec((length, columns), lambda step: (0, 0)),)
        + (grad_specs(count, share, columns),) * 2,
        [pltpu.VMEM((width, columns), jnp.bfloat16), pltpu.VMEM((width, length), jnp.bfloat16)],
    )


def qkv_grads(spot, hidden, query_grads, block_grads, parts):
    arrays = [part.array for part in parts]
    tiles, share, columns = arrays[0].shape
    length, width = hidden.shape
    count = width // share

    seqs, rows = len(query_grads), query_grads[0].shape[1]

    def kernel(spot_ref, hid_ref, *rest):
        query_refs, block_refs, rest = rest[:seqs], rest[seqs : 2 * seqs], rest[2 * seqs :]
        refs, (out_ref, keep_ref, send_ref, scratch, total, turned, grad) = rest[:-7], rest[-7:]
        step = pl.program_id(0)
        fill(scratch, spot_ref, parts, refs)

        @pl.when(step == 0)
        def first():
            turned[...] = jnp.transpose(hid_ref[...])
            total[...] = jnp.zeros_like(total)
            for at, ref in enumerate(query_refs):
                grad[at * rows : (at + 1) * rows] = ref[0]

        @pl.when(step > 0)
        def later():
            for at, ref in enumerate(block_refs):
                grad[at * rows : (at + 1) * rows] = ref[0]

        total[...] += product_back(grad[...], scratch[...])
        put_grad(spot_ref, turned, grad[...], keep_ref, send_ref, share, count)

        @pl.when(step == tiles - 1)
        def finish():
            out_ref[...] = total[...].astype(jnp.bfloat16)

    half = bf16(count // 2, tiles, share, columns)
    return call(
        kernel,
        tiles,
        spot,
        [hidden, *query_grads] + [block_grads] * seqs + arrays,
        [whole_spec(hidden)]
        + [whole_spec(part) for part in query_grads]
        + [
            pl.BlockSpec(
                (1, rows, columns),
                functools.partial(lambda at, step: (2 * at + jnp.maximum(step - 1, 0), 0, 0), at),
            )
            for at in range(seqs)
        ]
        + [tile_spec(3, part.shape[1], columns) for part in arrays],
        (bf16(length, width), half, half),
        (pl.BlockSpec((length, width), lambda step: (0, 0)),)
        + (grad_specs(count, share, columns),) * 2,
        [
            pltpu.VMEM((width, columns), jnp.bfloat16),
            pltpu.VMEM((length, width), jnp.float32),
            pltpu.VMEM((width, length), jnp.bfloat16),
            pltpu.VMEM((length, columns), jnp.bfloat16),
        ],
    )


def gelu_parts(upward):
    squared = upward * upward
    bent = jnp.tanh(0.7978845608028654 * (upward + 0.044715 * (upward * squared)))
    activ = 0.5 * upward * (1.0 + bent)
    slope = 0.5 * (1.0 + bent) + 0.5 * upward * (1.0 - bent * bent) * (
        0.7978845608028654 * (1.0 + 3 * 0.044715 * squared)
    )
    return activ, slope


def feed_forward(spot, hidden, grad, up_parts, down_parts, columns):
    arrays = [part.array for part in up_parts + down_parts]
    share, units = arrays[0].shape
    tiles = units // columns
    length, width = hidden.shape
    count = width // share

    def kernel(spot_ref, hid_ref, grad_ref, *rest):
        refs, rest = rest[: len(arrays)], rest[len(arrays) :]
        out_ref, back_ref, up_keep, up_send, down_keep, down_send = rest[:6]
        up, down, out_sum, back_sum, hid_turned, grad_turned = rest[6:]
        step = pl.program_id(0)

        @pl.when(step == 0)
        def begin():
            hid_turned[...] = jnp.transpose(hid_ref[...])
            grad_turned[...] = jnp.transpose(grad_ref[...])
            out_sum[...] = jnp.zeros_like(out_sum)
            back_sum[...] = jnp.zeros_like(back_sum)

        fill(up, spot_ref, up_parts, refs[: len(up_parts)])
        fill(down, spot_ref, down_parts, refs[len(up_parts) :])
        activ, slope = gelu_parts(product(hid_ref[...], up[...]))
        activ = activ.astype(jnp.bfloat16)
        upward_grad = (product(grad_ref[...], down[...]) * slope).astype(jnp.bfloat16)
        out_sum[...] += product_back(activ, down[...])
        back_sum[...] += product_back(upward_grad, up[...])
        put_grad(spot_ref, grad_turned, activ, down_keep, down_send, share, count)
        put_grad(spot_ref, hid_turned, upward_grad, up_keep, up_send, share, count)

        @pl.when(step == tiles - 1)
        def finish():
            out_ref[...] = out_sum[...].astype(jnp.bfloat16)
            back_ref[...] = back_sum[...].astype(jnp.bfloat16)

    rows_spec = pl.BlockSpec((length, width), lambda step: (0, 0))
    wholes = [hidden, grad]
    return call(
        kernel,
        tiles,
        spot,
        wholes + arrays,
        [whole_spec(part) for part in wholes]
        + [tile_spec(2, part.shape[0], columns) for part in arrays],
        (bf16(length, width), bf16(length, width))
        + (bf16(count // 2, tiles, share, columns),) * 4,
        (rows_spec, rows_spec) + (grad_specs(count, share, columns),) * 4,
        [pltpu.VMEM((width, columns), jnp.bfloat16)] * 2
        + [pltpu.VMEM((length, width), jnp.float32)] * 2
        + [pltpu.VMEM((width, length), jnp.bfloat16)] * 2,
    )


def activate(seq, first, second):
    shape = first.shape
    tile = shape[1] // 2

    def kernel(first_ref, second_ref, out_ref):
        upward = first_ref[0].astype(jnp.float32) + second_ref[0].astype(jnp.float32)
        activ_grad = first_ref[1].astype(jnp.float32) + second_ref[1].astype(jnp.float32)
        activ, slope = gelu_parts(upward)
        out_ref[0] = activ.astype(jnp.bfloat16)
        out_ref[1] = (activ_grad * slope).astype(jnp.bfloat16)

    spec = pl.BlockSpec((2, tile, shape[2]), lambda step: (0, step, 0))
    return seq.mark(
        pl.pallas_call(
            kernel,
            grid=(2,),
            in_specs=[spec, spec],
            out_specs=spec,
            out_shape=bf16(*shape),
            compiler_params=pltpu.CompilerParams(
                dimension_semantics=("arbitrary",), vmem_limit_bytes=VMEM_LIMIT
            ),
            cost_estimate=SMALL_COST,
        )(seq.then(first), second)
    )


def middle_spread(seq, spot, modul, stream, branch, cot, count):
    seqs, length, width = stream.shape
    share = width // count

    def kernel(spot_ref, mod_ref, x_ref, one_ref, two_ref, cot_ref, *rest):
        outs, hid_all, grad_all = rest[:-2], rest[-2], rest[-1]
        middle = wide(x_ref) + mod_ref[0, 2:3] * (wide(one_ref) + wide(two_ref))
        norm, factor = normed(middle)
        hid_all[...] = (norm * (1.0 + mod_ref[0, 4:5]) + mod_ref[0, 3:4]).astype(jnp.bfloat16)
        grad_all[...] = (mod_ref[0, 5:6] * wide(cot_ref)).astype(jnp.bfloat16)
        for away, out in enumerate(outs):
            at = pl.multiple_of(jnp.bitwise_xor(spot_ref[0], away) * share, LANES)
            out[0, 0] = hid_all[:, pl.ds(at, share)]
            out[1, 0] = grad_all[:, pl.ds(at, share)]

    row_spec = pl.BlockSpec((1, length, width), lambda at: (at, 0, 0))
    made = pl.pallas_call(
        kernel,
        grid=(seqs,),
        in_specs=[
            pl.BlockSpec(memory_space=pltpu.SMEM),
            pl.BlockSpec((1,) + modul.shape[1:], lambda at: (at, 0, 0)),
        ]
        + [row_spec] * 4,
        out_specs=[pl.BlockSpec((2, 1, length, share), lambda at: (0, at, 0, 0))] * count,
        out_shape=[bf16(2, seqs, length, share)] * count,
        scratch_shapes=[pltpu.VMEM((length, width), jnp.bfloat16)] * 2,
        compiler_params=pltpu.CompilerParams(
            dimension_semantics=("arbitrary",), vmem_limit_bytes=VMEM_LIMIT
        ),
        cost_estimate=SMALL_COST,
    )(spot, modul, seq.then(stream), *branch, cot)
    seq.mark(made[0])
    return [part.reshape(2, -1, share) for part in made]


def lay_rows(spot, refs, scratch):
    rows = refs[0].shape[1]
    for away, ref in enumerate(refs):
        at = pl.multiple_of(jnp.bitwise_xor(spot[0], away) * rows, rows)
        scratch[:, pl.ds(at, rows), :] = ref[...]


def spread_up(seq, spot, features, up_shard, down_shard):
    count = len(features)
    rows, share = features[0].shape[1:]
    length = rows * count
    columns = up_shard.shape[1] // count

    def kernel(spot_ref, up_ref, down_ref, *rest):
        refs, (keep_ref, send_ref, rows_in) = rest[:count], rest[count:]

        @pl.when(pl.program_id(0) == 0)
        def begin():
            lay_rows(spot_ref, refs, rows_in)

        upward = product(rows_in[0], up_ref[...]).astype(jnp.bfloat16)
        activ_grad = product(rows_in[1], down_ref[...]).astype(jnp.bfloat16)
        odd = pl.program_id(0) % 2

        @pl.when(odd == 0)
        def keep():
            keep_ref[0, 0], keep_ref[0, 1] = upward, activ_grad

        @pl.when(odd != 0)
        def send():
            send_ref[0, 0], send_ref[0, 1] = upward, activ_grad

    shard_spec = pl.BlockSpec(
        (share, columns), lambda step, spot_ref: (0, jnp.bitwise_xor(spot_ref[0], step))
    )
    out_spec = pl.BlockSpec((1, 2, length, columns), lambda step, spot_ref: (step // 2, 0, 0, 0))
    out = bf16(count // 2, 2, length, columns)
    keep, send = pl.pallas_call(
        kernel,
        grid_spec=pltpu.PrefetchScalarGridSpec(
            num_scalar_prefetch=1,
            grid=(count,),
            in_specs=[shard_spec, shard_spec]
            + [pl.BlockSpec(part.shape, lambda step, spot_ref: (0, 0, 0)) for part in features],
            out_specs=[out_spec, out_spec],
            scratch_shapes=[pltpu.VMEM((2, length, share), jnp.bfloat16)],
        ),
        out_shape=[out, out],
        compiler_params=pltpu.CompilerParams(
            dimension_semantics=("arbitrary",), vmem_limit_bytes=VMEM_LIMIT
        ),
        cost_estimate=SMALL_COST,
    )(spot, up_shard, down_shard, seq.then(features[0]), *features[1:])
    seq.mark(keep)
    return keep, send


def spread_down(spot, features, blocks, up_shard, down_shard):
    count = len(blocks)
    length, columns = blocks[0].shape[1:]
    share, units = up_shard.shape
    rows, half = length // count, count // 2

    def kernel(spot_ref, up_ref, down_ref, *rest):
        feature_refs, refs, rest = rest[:count], rest[count : 2 * count], rest[2 * count :]
        outs, (up_low, up_high, down_low, down_high, rows_in, sums) = rest[:count], rest[count:]
        lay_rows(spot_ref, feature_refs, rows_in)
        hid_turned, grad_turned = jnp.transpose(rows_in[0]), jnp.transpose(rows_in[1])
        out_sum = jnp.zeros((length, share), jnp.float32)
        back_sum = jnp.zeros((length, share), jnp.float32)
        for away, ref in enumerate(refs):
            place = jnp.bitwise_xor(spot_ref[0], away)
            at = pl.ds(pl.multiple_of(place * columns, columns), columns)
            activ, upward_grad = ref[0], ref[1]
            out_sum += product_back(activ, down_ref[:, at])
            back_sum += product_back(upward_grad, up_ref[:, at])
            up_block = product(hid_turned, upward_grad).astype(jnp.bfloat16)
            down_block = product(grad_turned, activ).astype(jnp.bfloat16)

            def put_low(place=place, up_block=up_block, down_block=down_block):
                up_low[place], down_low[place] = up_block, down_block

            def put_high(place=place, up_block=up_block, down_block=down_block):
                up_high[place - half], down_high[place - half] = up_block, down_block

            pl.when(place < half)(put_low)
            pl.when(place >= half)(put_high)
        sums[0] = back_sum.astype(jnp.bfloat16)
        sums[1] = out_sum.astype(jnp.bfloat16)
        for away, out in enumerate(outs):
            at = pl.multiple_of(jnp.bitwise_xor(spot_ref[0], away) * rows, rows)
            out[...] = sums[:, pl.ds(at, rows), :]

    zeros = lambda step: (0, 0, 0)
    arrays = [up_shard, down_shard] + list(features) + list(blocks)
    *sums, up_low, up_high, down_low, down_high = call(
        kernel,
        1,
        spot,
        arrays,
        [whole_spec(part) for part in arrays],
        (bf16(2, rows, share),) * count + (bf16(half, share, columns),) * 4,
        (pl.BlockSpec((2, rows, share), zeros),) * count
        + (pl.BlockSpec((half, share, columns), zeros),) * 4,
        [pltpu.VMEM((2, length, share), jnp.bfloat16)] * 2,
    )
    return sums, (up_low, up_high), (down_low, down_high)


def gather_features(seq, spot, pieces):
    count = len(pieces)
    rows, share = pieces[0].shape[1:]

    def kernel(spot_ref, *rest):
        refs, outs = rest[:count], rest[count:]
        for away, ref in enumerate(refs):
            at = pl.multiple_of(jnp.bitwise_xor(spot_ref[0], away) * share, LANES)
            for place, out in enumerate(outs):
                out[:, pl.ds(at, share)] = ref[place]

    out_spec = pl.BlockSpec((rows, share * count), lambda step: (0, 0))
    arrays = [seq.then(pieces[0])] + list(pieces[1:])
    made = call(
        kernel,
        1,
        spot,
        arrays,
        [whole_spec(part) for part in arrays],
        (bf16(rows, share * count),) * 2,
        (out_spec, out_spec),
        [],
    )
    seq.mark(made[0])
    return made


def row_kernel(seq, kernel, modul, rows_in, outs):
    seqs, length, width = rows_in[0].shape
    row_spec = pl.BlockSpec((1, length, width), lambda at: (at, 0, 0))
    sum_spec = pl.BlockSpec((1, 8, width), lambda at: (at, 0, 0))
    made = pl.pallas_call(
        kernel,
        grid=(seqs,),
        in_specs=[pl.BlockSpec((1,) + modul.shape[1:], lambda at: (at, 0, 0))]
        + [row_spec] * len(rows_in),
        out_specs=[sum_spec if kind is None else row_spec for kind in outs],
        out_shape=[
            jax.ShapeDtypeStruct((seqs, 8, width), jnp.float32)
            if kind is None
            else jax.ShapeDtypeStruct((seqs, length, width), kind)
            for kind in outs
        ],
        compiler_params=pltpu.CompilerParams(
            dimension_semantics=("arbitrary",), vmem_limit_bytes=VMEM_LIMIT
        ),
        cost_estimate=SMALL_COST,
    )(modul, seq.then(rows_in[0]), *rows_in[1:])
    seq.mark(made[0])
    return made


def wide(ref):
    return ref[0].astype(jnp.float32)


def put_sums(ref, rows):
    ref[0] = jnp.zeros_like(ref[0])
    for place, row in enumerate(rows):
        ref[0, place : place + 1] = jnp.sum(row, axis=0, keepdims=True)


def back_through(values, grad, scale_part):
    norm, factor = normed(values)
    inner = grad * (1.0 + scale_part)
    own = jnp.mean(inner, axis=-1, keepdims=True)
    along = jnp.mean(inner * norm, axis=-1, keepdims=True)
    return (inner - own - norm * along) * factor, norm


def first_hidden(seq, modul, stream):
    def kernel(mod_ref, x_ref, out_ref):
        norm, factor = normed(wide(x_ref))
        out_ref[0] = (norm * (1.0 + mod_ref[0, 1:2]) + mod_ref[0, 0:1]).astype(jnp.bfloat16)

    return row_kernel(seq, kernel, modul, [stream], [jnp.bfloat16])[0]


def middle_hidden(seq, modul, stream, branch, cot):
    def kernel(mod_ref, x_ref, one_ref, two_ref, cot_ref, hid_ref, grad_ref):
        middle = wide(x_ref) + mod_ref[0, 2:3] * (wide(one_ref) + wide(two_ref))
        norm, factor = normed(middle)
        hid_ref[0] = (norm * (1.0 + mod_ref[0, 4:5]) + mod_ref[0, 3:4]).astype(jnp.bfloat16)
        grad_ref[0] = (mod_ref[0, 5:6] * wide(cot_ref)).astype(jnp.bfloat16)

    return row_kernel(seq, kernel, modul, [stream, *branch, cot], [jnp.bfloat16, jnp.bfloat16])


def middle_grads(seq, modul, stream, branch, cot, hidden_grad):
    def kernel(mod_ref, x_ref, one_ref, two_ref, cot_ref, hid_ref, other_ref, mid_out, out, sums):
        branch_sum = wide(one_ref) + wide(two_ref)
        middle = wide(x_ref) + mod_ref[0, 2:3] * branch_sum
        grad = wide(hid_ref) + wide(other_ref)
        through, norm = back_through(middle, grad, mod_ref[0, 4:5])
        mid_grad = wide(cot_ref) + through
        mid_out[0] = mid_grad
        out[0] = (mod_ref[0, 2:3] * mid_grad).astype(jnp.bfloat16)
        put_sums(sums, [mid_grad * branch_sum, grad, grad * norm])

    return row_kernel(
        seq,
        kernel,
        modul,
        [stream, *branch, cot, *hidden_grad],
        [jnp.float32, jnp.bfloat16, None],
    )


def input_grads(seq, modul, stream, mid_grad, hidden_grad):
    def kernel(mod_ref, x_ref, mid_ref, hid_ref, other_ref, out, sums):
        grad = wide(hid_ref) + wide(other_ref)
        through, norm = back_through(wide(x_ref), grad, mod_ref[0, 1:2])
        out[0] = (mid_ref[0] + through).astype(jnp.bfloat16)
        put_sums(sums, [grad, grad * norm])

    return row_kernel(
        seq, kernel, modul, [stream, mid_grad, *hidden_grad], [jnp.bfloat16, None]
    )


def results(seq, modul, stream, branch, second, cot, real):
    def kernel(mod_ref, x_ref, one_ref, two_ref, three_ref, four_ref, cot_ref, out, sums):
        start = wide(x_ref)
        gated_one = mod_ref[0, 2:3] * (wide(one_ref) + wide(two_ref))
        middle = start + gated_one
        branch_two = wide(three_ref) + wide(four_ref)
        gated_two = mod_ref[0, 5:6] * branch_two
        result = middle + gated_two
        out[0] = result.astype(jnp.bfloat16)
        shown = lax.broadcasted_iota(jnp.int32, start.shape, 0) < real
        put_sums(
            sums,
            [wide(cot_ref) * branch_two]
            + [
                jnp.where(shown, member * member, 0.0)
                for member in (start, gated_one, middle, gated_two, result)
            ],
        )

    return row_kernel(
        seq, kernel, modul, [stream, *branch, *second, cot], [jnp.bfloat16, None]
    )


def head_lanes(shape, head):
    lane = lax.broadcasted_iota(jnp.int32, shape, len(shape) - 1)
    return (lane >= head * HD) & (lane < (head + 1) * HD)


def padding(shape, axis, image_rows, text_rows, real, count):
    place = lax.broadcasted_iota(jnp.int32, shape, axis) - image_rows * count
    hidden = (place >= real) & (place < text_rows)
    for other in range(1, count):
        hidden = hidden | (
            (place >= other * text_rows + real) & (place < (other + 1) * text_rows)
        )
    return hidden


def attention_specs(image, text):
    row = [
        pl.BlockSpec((1, rows, LANES), lambda seq, part: (seq, 0, part))
        for rows in (image.shape[1], text.shape[1])
    ]
    block = [
        pl.BlockSpec((2, 1, rows, LANES), lambda seq, part: (0, seq, 0, part))
        for rows in (image.shape[1], text.shape[1])
    ]
    return row, block


def joint(refs, index):
    return jnp.concatenate([ref[index] for ref in refs], axis=0)


def attend(image, text, image_blocks, text_blocks, real):
    seqs, image_rows, width = image.shape
    text_rows = text.shape[1]
    rows = image_rows + text_rows
    count = len(image_blocks)
    keys = rows * count

    def kernel(*rest):
        refs, (image_out, text_out) = rest[:-2], rest[-2:]
        queries = joint(refs[:2], 0)
        key_all = joint(refs[2:], (0, 0))
        value_all = joint(refs[2:], (1, 0))
        hidden = padding((1, keys), 1, image_rows, text_rows, real, count)
        result = jnp.zeros((rows, LANES), jnp.float32)
        for head in range(LANES // HD):
            mine = head_lanes((rows, LANES), head)
            scores = product_back(jnp.where(mine, queries, jnp.zeros_like(queries)), key_all)
            scores = jnp.where(hidden, -1e30, scores * 0.125)
            expd = jnp.exp(scores - jnp.max(scores, axis=1, keepdims=True))
            share = 1.0 / jnp.sum(expd, axis=1, keepdims=True)
            mixed = product((expd * share).astype(jnp.bfloat16), value_all)
            result = jnp.where(mine, mixed, result)
        image_out[0] = result[:image_rows].astype(jnp.bfloat16)
        text_out[0] = result[image_rows:].astype(jnp.bfloat16)

    row, block = attention_specs(image, text)
    return pl.pallas_call(
        kernel,
        grid=(seqs, width // LANES),
        in_specs=row + [block[0]] * count + [block[1]] * count,
        out_specs=row,
        out_shape=[bf16(*image.shape), bf16(*text.shape)],
        compiler_params=pltpu.CompilerParams(
            dimension_semantics=("arbitrary", "arbitrary"), vmem_limit_bytes=VMEM_LIMIT
        ),
        cost_estimate=SMALL_COST,
    )(image, text, *image_blocks, *text_blocks)


def attend_grads(queries_in, grads_in, image_blocks, text_blocks, real, seq):
    image, text = queries_in
    image_rows, width = image.shape[1:]
    text_rows = text.shape[1]
    rows = image_rows + text_rows
    count = len(image_blocks)
    keys = rows * count

    def kernel(*rest):
        refs, (image_out, text_out, keep_ref, send_ref) = rest[:-4], rest[-4:]
        queries = joint(refs[:2], 0)
        grads = joint(refs[2:4], 0)
        key_all = joint(refs[4:], (0, 0))
        value_all = joint(refs[4:], (1, 0))
        hidden = padding((keys, 1), 0, image_rows, text_rows, real, count)
        query_grad = jnp.zeros((rows, LANES), jnp.float32)
        key_grad = jnp.zeros((keys, LANES), jnp.float32)
        value_grad = jnp.zeros((keys, LANES), jnp.float32)
        for head in range(LANES // HD):
            mine = head_lanes((rows, LANES), head)
            own_query = jnp.where(mine, queries, jnp.zeros_like(queries))
            own_grad = jnp.where(mine, grads, jnp.zeros_like(grads))
            scores = product_back(key_all, own_query)
            scores = jnp.where(hidden, -1e30, scores * 0.125)
            expd = jnp.exp(scores - jnp.max(scores, axis=0, keepdims=True))
            probs = expd * (1.0 / jnp.sum(expd, axis=0, keepdims=True))
            prob_grad = product_back(value_all, own_grad)
            delta = jnp.sum(probs * prob_grad, axis=0, keepdims=True)
            score_grad = (probs * (prob_grad - delta)).astype(jnp.bfloat16)
            value_grad += product(probs.astype(jnp.bfloat16), own_grad)
            key_grad += product(score_grad, own_query)
            back = lax.dot_general(
                score_grad, key_all, (((0,), (0,)), ((), ())), preferred_element_type=jnp.float32
            )
            query_grad = jnp.where(mine, back, query_grad)
        query_grad = (query_grad * 0.125).astype(jnp.bfloat16)
        image_out[0] = query_grad[:image_rows]
        text_out[0] = query_grad[image_rows:]
        key_grad = (key_grad * 0.125).astype(jnp.bfloat16)
        value_grad = value_grad.astype(jnp.bfloat16)
        for away in range(count):
            to, place = (send_ref if away & 1 else keep_ref), away // 2
            at = slice(away * image_rows, (away + 1) * image_rows)
            to[place, 0, :image_rows], to[place, 1, :image_rows] = key_grad[at], value_grad[at]
            first = count * image_rows + away * text_rows
            at = slice(first, first + text_rows)
            to[place, 0, image_rows:], to[place, 1, image_rows:] = key_grad[at], value_grad[at]

    def row_spec(length, at):
        return pl.BlockSpec((1, length, LANES), lambda part: (at, 0, part))

    def block_spec(length):
        return pl.BlockSpec((2, 1, length, LANES), lambda part: (0, seq, 0, part))

    def owner_spec(length):
        return pl.BlockSpec((count // 2, 2, length, LANES), lambda part: (0, 0, 0, part))

    sizes = (image_rows, text_rows)
    return pl.pallas_call(
        kernel,
        grid=(width // LANES,),
        in_specs=[row_spec(length, seq) for length in sizes] * 2
        + [block_spec(image_rows)] * count
        + [block_spec(text_rows)] * count,
        out_specs=[row_spec(length, 0) for length in sizes]
        + [owner_spec(rows)] * 2,
        out_shape=[bf16(1, length, width) for length in sizes]
        + [bf16(count // 2, 2, rows, width)] * 2,
        compiler_params=pltpu.CompilerParams(
            dimension_semantics=("arbitrary",), vmem_limit_bytes=VMEM_LIMIT
        ),
        cost_estimate=SMALL_COST,
    )(image, text, *grads_in, *image_blocks, *text_blocks)


def on_device(
    image_tokens,
    text_tokens,
    text_owner,
    conditioning,
    slot_sequence,
    image_w_mod,
    image_b_mod,
    image_w_qkv,
    image_w_proj,
    image_w_up,
    image_w_down,
    text_w_mod,
    text_b_mod,
    text_w_qkv,
    text_w_proj,
    text_w_up,
    text_w_down,
    image_cotangent,
    text_cotangent,
):
    tok_rank = lax.axis_index("tok")
    rep_rank = lax.axis_index("rep")
    rep_count = lax.axis_size("rep")
    tok_count = lax.axis_size("tok")
    seqs, image_rows, width = image_tokens.shape
    text_real = text_cotangent.shape[1]
    text_rows = -(-text_real // 16) * 16
    slots = conditioning.shape[0]
    share = image_w_mod.shape[0]
    heads_width = image_w_qkv.shape[2]
    spot = jnp.stack([tok_rank, lax.rem(rep_rank, 2)]).astype(jnp.int32)

    turn = lambda weight: jnp.transpose(weight, (1, 0, 2))
    chips = Lane("tok", 2)
    proj_stack = jnp.stack([image_w_proj, text_w_proj])
    qkv_held = fetch(turn(image_w_qkv), 1, chips)
    qkv_own, text_own = flip(turn(image_w_qkv), "tok", 1), flip(turn(text_w_qkv), "tok", 1)
    image_qkv_parts, unused = share_out(turn(image_w_qkv), qkv_own, qkv_held)

    picker = (slot_sequence[:, None] == jnp.arange(slots, dtype=jnp.int32)[None, :]).astype(
        jnp.float32
    )
    cond_slots = jnp.dot(picker, conditioning, precision=exact_mode)
    activ_all = jax.nn.silu(cond_slots).astype(jnp.bfloat16)
    activ_group = lax.dynamic_slice_in_dim(activ_all, rep_rank * seqs, seqs, axis=0)
    activ_share = lax.dynamic_slice_in_dim(activ_group, tok_rank * share, share, axis=1)
    both_mod = tok_total(
        jnp.stack(
            [
                jnp.einsum("sd,dke->ske", activ_share, weight, preferred_element_type=jnp.float32)
                for weight in (image_w_mod, text_w_mod)
            ]
        ),
        *qkv_held.values(),
    )
    image_mod = both_mod[0] + image_b_mod.astype(jnp.float32)[None]
    text_mod = both_mod[1] + text_b_mod.astype(jnp.float32)[None]

    text_held = fetch(turn(text_w_qkv), 1, chips, (both_mod,))
    cores = Lane("tok", 1)
    up_own = cores.flip(after(image_w_up, both_mod), 1)
    down_own = cores.flip(after(image_w_down, both_mod), 1)
    proj_held = fetch(proj_stack, 0, chips, tuple(text_held.values()))

    owned = (text_owner == tok_rank).astype(jnp.float32)
    total_text = text_owner.shape[1]
    before = jnp.dot(
        owned,
        jnp.triu(jnp.ones((total_text, total_text), jnp.float32), 1),
        precision=exact_mode,
    )
    chosen = (
        (before[:, None, :] == jnp.arange(text_rows, dtype=jnp.float32)[None, :, None])
        & (owned[:, None, :] > 0.5)
    ).astype(jnp.bfloat16)
    text_input = jnp.einsum(
        "srt,std->srd", chosen, text_tokens, preferred_element_type=jnp.float32
    ).astype(jnp.bfloat16)
    text_cot = jnp.pad(text_cotangent, ((0, 0), (0, text_rows - text_real), (0, 0)))

    seq = Sequence()
    flat = lambda values: values.reshape(-1, values.shape[-1])
    by_seq = lambda values: values.reshape(values.shape[:-2] + (seqs, -1, values.shape[-1]))
    both = lambda pair: tuple(by_seq(part) for part in pair)
    heads = lambda partial: both(head_pair(partial))

    image_hid_one = flat(first_hidden(seq, image_mod, image_tokens))
    image_qkv = seq.mark(
        project(
            spot,
            after(seq.then(image_hid_one), *text_held.values(), up_own, down_own),
            image_qkv_parts,
        )
    )
    text_qkv_parts, text_swapped = share_out(
        turn(text_w_qkv), text_own, text_held, (image_qkv,)
    )
    text_hid_one = flat(first_hidden(seq, text_mod, after(text_input, *proj_held.values())))
    text_qkv = project(spot, seq.then(text_hid_one), text_qkv_parts)
    image_blocks = gather_blocks(
        after(by_seq(image_qkv[1:]), *proj_held.values()), chips, (text_qkv,)
    )
    text_blocks = gather_blocks(by_seq(text_qkv[1:]), chips)
    proj_own = flip(after(proj_stack, image_qkv), "tok", 1)
    seq.mark(text_qkv, proj_own)
    proj_parts, unused = share_out(
        proj_stack, proj_own, proj_held, (text_qkv,), (image_qkv,)
    )
    up_held = fetch(image_w_up, 0, chips)
    down_held = fetch(image_w_down, 0, chips)
    image_query, text_query = by_seq(image_qkv[0]), by_seq(text_qkv[0])
    image_mix, text_mix = attend(
        image_query, seq.then(text_query), image_blocks, text_blocks, text_real
    )
    seq.mark(image_mix, *up_held.values())
    image_mixed, text_mixed = flat(image_mix), flat(text_mix)
    text_out = seq.mark(project_back(spot, seq.then(text_mixed), proj_parts, 1, width))
    text_branch = heads(text_out)
    image_up_parts, up_swapped = share_out(image_w_up, up_own, up_held)
    image_down_parts, down_swapped = share_out(image_w_down, down_own, down_held)
    image_out = project_back(spot, seq.then(image_mixed), proj_parts, 0, width)
    seq.mark(image_out, *down_held.values())
    if lax.axis_size("head") == 2:
        image_branch = both((image_out, flip(after(image_out, text_branch[1]), "head", 1)))
    else:
        image_branch = heads(image_out)

    text_features = exchange(
        middle_spread(seq, spot, text_mod, text_input, text_branch, text_cot, tok_count)
    )
    image_hid_two, image_db_two = middle_hidden(
        seq, image_mod, image_tokens, image_branch, image_cotangent
    )
    seq.mark(image_hid_two, *up_swapped, *down_swapped)
    text_keep, text_send = spread_up(seq, spot, text_features, text_w_up, text_w_down)
    text_pieces = core_sums(seq, text_keep, flip(text_send, "tok", 1))
    text_stays, text_came = chip_moves(seq, text_pieces, chips)
    image_part, image_back, image_up_keep, image_up_send, image_down_keep, image_down_send = (
        feed_forward(
            spot,
            seq.then(flat(image_hid_two)),
            flat(image_db_two),
            image_up_parts,
            image_down_parts,
            heads_width,
        )
    )
    seq.mark(image_back)
    shape = (2,) + text_keep.shape[2:]
    text_act = activate(seq, text_stays.reshape(shape), text_came.reshape(shape))
    text_lane = chips
    image_hid_grad = heads(after(image_back, text_act))
    image_down_send = after(image_down_send, text_act)
    image_up_send = after(image_up_send, text_act)
    chips = Lane("tok", 3)
    image_down_pieces = core_sums(seq, image_down_keep, flip(image_down_send, "tok", 1))
    image_up_pieces = core_sums(seq, image_up_keep, flip(image_up_send, "tok", 1))
    text_active = gather_blocks(text_act, text_lane, (image_up_pieces[0],))
    text_sums, text_up_grad, text_down_grad = spread_down(
        spot,
        [seq.then(text_features[0])] + text_features[1:],
        text_active,
        text_w_up,
        text_w_down,
    )
    seq.mark(text_sums[0])
    text_back_pieces = exchange(text_sums)
    behind = lambda pieces: {
        away: after(part, text_sums[0]) if away else part for away, part in pieces.items()
    }
    image_down_pair = chip_moves(seq, behind(image_down_pieces), chips)
    image_up_pair = chip_moves(seq, behind(image_up_pieces), chips)
    line = Line(seq)
    if line.on_line:
        for whole in (text_down_grad, text_up_grad):
            for part in whole:
                line.add(flat(part))
        text_totals = None
    else:
        text_totals = [
            lax.psum(jnp.concatenate(parts), "rep") for parts in (text_down_grad, text_up_grad)
        ]

    image_mid_grad, image_db_one, image_mid_sums = middle_grads(
        seq, image_mod, image_tokens, image_branch, image_cotangent, image_hid_grad
    )
    text_back, text_part = gather_features(seq, spot, text_back_pieces)
    text_hid_grad = heads(text_back)
    image_mixed_grad, image_proj_keep, image_proj_send = proj_grads(
        spot, seq.then(flat(image_db_one)), image_mixed, proj_parts, 0
    )
    seq.mark(image_mixed_grad)
    text_mid_grad, text_db_one, text_mid_sums = middle_grads(
        seq, text_mod, text_input, text_branch, text_cot, text_hid_grad
    )
    text_mixed_grad, text_proj_keep, text_proj_send = proj_grads(
        spot, seq.then(flat(text_db_one)), text_mixed, proj_parts, 1
    )
    seq.mark(text_mixed_grad)
    line.step()
    proj_pieces = [
        core_sums(seq, keep, flip(send, "tok", 1))
        for keep, send in ((image_proj_keep, image_proj_send), (text_proj_keep, text_proj_send))
    ]
    made_grads, moved_grads = [], []
    mix_grads = (by_seq(image_mixed_grad), by_seq(text_mixed_grad))
    for at in range(seqs):
        made = attend_grads(
            (image_query, text_query),
            (seq.then(mix_grads[0]), mix_grads[1]),
            image_blocks,
            text_blocks,
            text_real,
            at,
        )
        made_grads.append(made)
        seq.mark(made[0])
        if at == 0 or at == seqs - 1:
            for part in add_blocks(seq, *(image_up_pair if at else image_down_pair), 2):
                line.add(part)
        if at == 0 and seqs == 1:
            for part in add_blocks(seq, *image_up_pair, 2):
                line.add(part)
        line.step()
        moved_grads.append(flip(after(made[3], *seq.last), "tok", 1))
    block_move = chip_moves(
        seq, core_sums_joined(seq, [made[2] for made in made_grads], moved_grads), chips
    )
    line.step()
    tail, text_tail = Line(seq), Line(seq)
    block_grads = add_split(seq, *block_move, 2 * seqs, image_rows)
    proj_pairs = [chip_moves(seq, pieces, chips) for pieces in proj_pieces]
    image_in_part, image_qkv_keep, image_qkv_send = qkv_grads(
        spot,
        seq.then(image_hid_one),
        [made[0] for made in made_grads],
        block_grads[0],
        image_qkv_parts,
    )
    seq.mark(image_in_part)
    line.step()
    text_in_part, text_qkv_keep, text_qkv_send = qkv_grads(
        spot,
        seq.then(text_hid_one),
        [made[1] for made in made_grads],
        block_grads[1],
        text_qkv_parts,
    )
    seq.mark(text_in_part)
    qkv_pairs = [
        chip_moves(seq, core_sums(seq, keep, flip(send, "tok", 1)), chips)
        for keep, send in ((image_qkv_keep, image_qkv_send), (text_qkv_keep, text_qkv_send))
    ]
    line.step()
    image_in_grad = heads(image_in_part)
    text_in_grad = heads(text_in_part)
    image_proj_share, text_proj_share = [add_blocks(seq, *pair, 1)[0] for pair in proj_pairs]
    line.step()
    image_grad, image_in_sums = input_grads(
        seq, image_mod, image_tokens, image_mid_grad, image_in_grad
    )
    text_grad, text_in_sums = input_grads(
        seq, text_mod, text_input, text_mid_grad, text_in_grad
    )
    text_second = heads(after(text_part, image_in_sums))
    image_second = heads(after(image_part, image_in_sums))
    image_qkv_shares = add_blocks(seq, *qkv_pairs[0], 3)
    line.step()
    text_qkv_shares = add_blocks(seq, *qkv_pairs[1], 3)
    line.step()
    for part in (image_proj_share, *image_qkv_shares):
        tail.add(part)
    for part in (text_proj_share, *text_qkv_shares):
        text_tail.add(part)
    text_result, text_out_sums = results(
        seq, text_mod, text_input, text_branch, text_second, text_cot, text_real
    )
    image_result, image_out_sums = results(
        seq, image_mod, image_tokens, image_branch, image_second, image_cotangent, image_rows
    )
    line.step()
    line_sums = line.finish()
    for at in range(len(tail.chunks) + 1):
        tail.step()
        text_tail.step()
    tail_sums = tail.finish()
    text_tail_sums = text_tail.finish()
    columns_of = lambda parts: jnp.concatenate(
        [
            column.astype(jnp.float32)
            for part in parts
            for column in part.reshape(-1, share, part.shape[-1])
        ],
        axis=1,
    )
    if text_totals is None:
        text_totals = [jnp.concatenate(line_sums[at : at + 2]) for at in (0, 2)]
        text_totals = [part.reshape(tok_count, share, -1) for part in text_totals]
        line_sums = line_sums[4:]
    text_down_sum, text_up_sum = [columns_of([part]) for part in text_totals]
    image_down_sum, image_up_sum = columns_of(line_sums[:2]), columns_of(line_sums[2:])
    image_proj_sum, text_proj_sum = tail_sums[0], text_tail_sums[0]
    image_qkv_sum = jnp.stack(tail_sums[1:], axis=1)
    text_qkv_sum = jnp.stack(text_tail_sums[1:], axis=1)

    early = jnp.stack(
        [
            jnp.concatenate([mid_sums[:, :3], out_sums[:, :1]], axis=1)
            for mid_sums, out_sums in (
                (image_mid_sums, image_out_sums),
                (text_mid_sums, text_out_sums),
            )
        ]
    )
    late = jnp.stack([image_in_sums[:, :2], text_in_sums[:, :2]])
    squares = jnp.concatenate(
        [jnp.sum(out_sums[:, 1:6], axis=(0, 2)) for out_sums in (image_out_sums, text_out_sums)]
    )
    square_row = jnp.pad(squares, (0, width - 10))[None]
    all_sums = jnp.concatenate(
        [early.reshape(-1, width), late.reshape(-1, width), square_row], axis=0
    )
    waits = []
    if line.on_line:
        waits = [tail.totals[0], tail.totals[2]]
    all_sums = rep_gather(tok_total(all_sums), waits)
    square_total = jnp.sum(all_sums[:, -1, :10], axis=0)
    early_table = jnp.moveaxis(
        all_sums[:, : 8 * seqs].reshape(rep_count, 2, seqs, 4, width), 0, 1
    ).reshape(2, slots, 4, width)
    late_table = jnp.moveaxis(
        all_sums[:, 8 * seqs : -1].reshape(rep_count, 2, seqs, 2, width), 0, 1
    ).reshape(2, slots, 2, width)
    mod_sum = jnp.concatenate([late_table, early_table], axis=2)

    activ_rows = lax.dynamic_slice_in_dim(activ_all, tok_rank * share, share, axis=1).astype(
        jnp.float32
    )
    image_g_mod = jnp.einsum("sd,ske->dke", activ_rows, mod_sum[0], precision=lax.Precision.HIGH)
    text_g_mod = jnp.einsum("sd,ske->dke", activ_rows, mod_sum[1], precision=lax.Precision.HIGH)
    image_g_bmod = jnp.sum(mod_sum[0], axis=0)
    text_g_bmod = jnp.sum(mod_sum[1], axis=0)
    activ_grad = jnp.einsum(
        "ske,dke->sd", mod_sum[0], image_w_mod.astype(jnp.float32), precision=exact_mode
    ) + jnp.einsum("ske,dke->sd", mod_sum[1], text_w_mod.astype(jnp.float32), precision=exact_mode)
    cond_rows = lax.dynamic_slice_in_dim(cond_slots, tok_rank * share, share, axis=1)
    unused_value, silu_back = jax.vjp(jax.nn.silu, cond_rows)
    slot_grad = silu_back(activ_grad)[0]
    cond_grad = jnp.dot(jnp.transpose(picker), slot_grad, precision=exact_mode)
    image_count = float(slots * image_rows * tok_count * width)
    text_count = float(slots * text_real * tok_count * width)
    counts = jnp.concatenate(
        [jnp.full((5,), image_count, jnp.float32), jnp.full((5,), text_count, jnp.float32)]
    )
    stream_rms = jnp.sqrt(square_total / counts)
    return (
        image_result,
        text_result[:, :text_real],
        image_grad,
        text_grad[:, :text_real],
        cond_grad,
        image_g_mod,
        image_g_bmod,
        image_qkv_sum,
        image_proj_sum,
        image_up_sum,
        image_down_sum,
        text_g_mod,
        text_g_bmod,
        text_qkv_sum,
        text_proj_sum,
        text_up_sum,
        text_down_sum,
        stream_rms,
    )


def solution(mesh):
    in_specs = (
        P("rep", "tok", None),
        P("rep", None, None),
        P("rep", None),
        P(),
        P(),
        P("tok", None, None),
        P(),
        P("tok", None, "head"),
        P("tok", "head"),
        P("tok", "head"),
        P("tok", "head"),
        P("tok", None, None),
        P(),
        P("tok", None, "head"),
        P("tok", "head"),
        P("tok", "head"),
        P("tok", "head"),
        P("rep", "tok", None),
        P("rep", "tok", None),
    )
    out_specs = (
        P("rep", "tok", None),
        P("rep", "tok", None),
        P("rep", "tok", None),
        P("rep", "tok", None),
        P(None, "tok"),
        P("tok", None, None),
        P(),
        P("tok", None, "head"),
        P("tok", "head"),
        P("tok", "head"),
        P("tok", "head"),
        P("tok", None, None),
        P(),
        P("tok", None, "head"),
        P("tok", "head"),
        P("tok", "head"),
        P("tok", "head"),
        P(),
    )
    return jax.shard_map(
        on_device, mesh=mesh, in_specs=in_specs, out_specs=out_specs, check_vma=False
    )
```
